32 devices in a mesh: groups: 2 (over y), blk: 4 (over z), col: 2 (over x), rep: 2 (over core).
Axes of the slice: x: 2, y: 2, z: 4, core: 2. Of those that a mesh axis runs over, the one named last changes fastest.
Arguments:
- blocks: bfloat16 [4, 2, 6, 128, 128], P('blk', 'col'), may hold values from -0.21875 to 0.21875
- block_index: int32 [4, 2, 6], P('blk', 'col'), may hold values from 0 to 7, as said below
- live: int32 [4, 2], P('blk', 'col'), may hold values from 3 to 6, as said below
- cost: float32 [1024, 512], P(('blk', 'col'), ('groups', 'rep')), parts along dimension 1
- rhs: float32 [1024, 512], P(('blk', 'col'), ('groups', 'rep')), parts along dimension 1
- upper: float32 [1024, 512], P(('blk', 'col'), ('groups', 'rep')), parts along dimension 1, may hold values from 0.5 to 1.5
- x_init: float32 [1024, 512], P(('blk', 'col'), ('groups', 'rep')), parts along dimension 1, may hold values from 0 to 1
- y_init: float32 [1024, 512], P(('blk', 'col'), ('groups', 'rep')), parts along dimension 1, may hold values from 0 to 1
- bounded: int32 [512], P(('groups', 'rep')), parts along dimension 0, may hold values from 0 to 1
Outputs:
- x_final: float32 [1024, 512], P(('blk', 'col'), ('groups', 'rep')), parts along dimension 1
- y_final: float32 [1024, 512], P(('blk', 'col'), ('groups', 'rep')), parts along dimension 1
The draws below stay inside these ranges and needn't reach their ends.
There are 2 independent parts, one for each index of `groups`. The reference program is written for one: setup_inputs(seed, part) draws one part's arguments, and reference() takes and returns one part's arrays. A program takes and returns all parts, laid end to end along the dimension named above; an argument that names none is the same for every part. Nothing has to cross between parts.
Inputs may be any that keep to these rules, and one draw needn't show every extreme that they name: `block_index`: within one device the positions are distinct; a position p stands for block row p // 4 and block column p % 4 of the device's tile. `live`: some device uses all its slots.
All inputs are finite; a program needn't handle non-finite values.
Results may differ from the reference program's by a relative error of at most 0.0025.
Values may be sent and summed in bfloat16 or wider, within the bound.
No kernel may reach another device: no remote copies, remote signals or barrier semaphores. Data moves between devices by JAX's collectives and lax.ppermute only.
A program may use at most 64 MiB of HBM per device.

```python
import jax
import jax.numpy as jnp
from jax import lax

TILE = 128
ITERS = 2
NBLK = 6
SCENARIOS = 256
ROWS = 1024
COLS = 1024
N_BLK = 4
N_COL = 2


def scaled_field(key, length, width, column_spread):
    key_rows, key_cols, key_base = jax.random.split(key, 3)
    trend = 3.0 ** (jnp.arange(length, dtype=jnp.float32)[:, None] / length)
    row_scale = 10.0 ** jax.random.uniform(key_rows, (length, 1), jnp.float32) * trend / 5.0
    col_scale = 10.0 ** (column_spread * jax.random.uniform(key_cols, (1, width), jnp.float32))
    base = jax.random.normal(key_base, (length, width), jnp.float32)
    return (row_scale * col_scale * base).astype(jnp.float32)


def draw_cost(key, part):
    key = jax.random.fold_in(key, 11)
    return scaled_field(key, COLS, SCENARIOS, 1.0)


def draw_rhs(key, part):
    key = jax.random.fold_in(key, 23)
    return scaled_field(key, ROWS, SCENARIOS, 0.5)


def draw_block_index(key, part):
    key = jax.random.fold_in(key, 37)
    keys = jax.random.split(key, N_BLK * N_COL)
    picked = jax.vmap(lambda single: jax.random.permutation(single, N_BLK * N_COL)[:NBLK])(keys)
    return picked.reshape(N_BLK, N_COL, NBLK).astype(jnp.int32)


def draw_live(key, part):
    key = jax.random.fold_in(key, 53)
    key_counts, key_pick = jax.random.split(key)
    counts = jax.random.randint(key_counts, (N_BLK * N_COL,), NBLK // 2, NBLK + 1)
    chosen = jax.random.randint(key_pick, (), 0, N_BLK * N_COL)
    counts = jnp.where(jnp.arange(N_BLK * N_COL) == chosen, NBLK, counts)
    return counts.reshape(N_BLK, N_COL).astype(jnp.int32)


def set_ends(values, stream_key, least, high):
    place = [jax.random.randint(jax.random.fold_in(stream_key, axis), (), 0, length) for axis, length in enumerate(values.shape)]
    longest = values.shape.index(max(values.shape))
    next_to = place[:longest] + [(place[longest] + 1) % values.shape[longest]] + place[longest + 1:]
    return values.at[tuple(place)].set(least).at[tuple(next_to)].set(high)


def levels(own_key, extent, cuts, smallest, high):
    factor_of, own = 1.0, jax.random.fold_in(own_key, 6)
    for axis_at, blocks in cuts:
        draws = jnp.exp(jax.random.uniform(jax.random.fold_in(own, axis_at), (blocks,), jnp.float32, smallest / len(cuts), high / len(cuts)))
        factor_of = factor_of * jnp.repeat(draws, extent[axis_at] // blocks).reshape([-1 if axis == axis_at else 1 for axis in range(len(extent))])
    return factor_of


def scatter_about(stream_key, extent, scale, reach, cuts=(), held_as=jnp.bfloat16):
    result = jax.random.normal(stream_key, extent, jnp.float32) * scale
    if len(cuts) > 0:
        result = levels(stream_key, extent, cuts, -0.22, 0.18) * result
    return jnp.clip(result, min=-reach, max=reach).astype(held_as)


def setup_inputs(seed: int = 0, part: int = 0) -> dict:
    splits = jax.random.split(jax.random.key(seed), 10)
    own_keys = jax.random.split(jax.random.fold_in(splits[9], part), 10)
    return {
        "blocks": scatter_about(splits[0], (N_BLK, N_COL, NBLK, TILE, TILE), (TILE * NBLK) ** -0.5, 0.21875, ((0, 4), (1, 2))),
        "block_index": draw_block_index(jax.random.fold_in(splits[9], 71), part),
        "live": draw_live(jax.random.fold_in(splits[9], 71), part),
        "cost": draw_cost(jax.random.fold_in(jax.random.fold_in(splits[9], part), 71), part),
        "rhs": draw_rhs(jax.random.fold_in(jax.random.fold_in(splits[9], part), 71), part),
        "upper": jnp.clip(0.5 + 1.0 * jax.random.uniform(own_keys[5], (COLS, SCENARIOS), jnp.float32) ** levels(own_keys[5], (COLS, SCENARIOS), ((0, 8), (1, 2)), -0.2, 0.2), 0.5, 1.5),
        "x_init": jnp.clip(1.0 * jax.random.uniform(own_keys[6], (COLS, SCENARIOS), jnp.float32) ** levels(own_keys[6], (COLS, SCENARIOS), ((0, 8), (1, 2)), -0.2, 0.2), 0.0, 1.0),
        "y_init": jnp.clip(1.0 * jax.random.uniform(own_keys[7], (ROWS, SCENARIOS), jnp.float32) ** levels(own_keys[7], (ROWS, SCENARIOS), ((0, 8), (1, 2)), -0.2, 0.2), 0.0, 1.0),
        "bounded": set_ends(jax.random.randint(own_keys[8], (SCENARIOS,), 0, 2), jax.random.fold_in(own_keys[8], 1), 0, 1).astype(jnp.int32),
    }


ETA = 0.4
EPS = 1e-06

def project_box(value, upper, bounded):
    capped = jnp.where(bounded[None, :] > 0, jnp.minimum(value, upper), value)
    return jnp.maximum(capped, 0.0)

def apply_forward(blocks, block_index, live, columns):
    scn_count = columns.shape[1]
    panels = columns.reshape(N_BLK, N_COL, TILE, scn_count)

    def one_device(device, total):
        row_owner = device // N_COL
        col_owner = device % N_COL
        block_mats = blocks[row_owner, col_owner].astype(jnp.float32)
        slots = block_index[row_owner, col_owner]
        row_block = slots // N_BLK
        col_block = slots % N_BLK
        keep_mask = (jnp.arange(NBLK) < live[row_owner, col_owner]).astype(jnp.float32)
        pieces = panels[:, col_owner][col_block].astype(jnp.float32)
        products = jnp.einsum('bkt,bts->bks', block_mats, pieces) * keep_mask[:, None, None]
        onehot = (row_block[None, :] == jnp.arange(N_COL)[:, None]).astype(jnp.float32)
        rows = jnp.einsum('cb,bks->cks', onehot, products, precision=lax.Precision.HIGHEST)
        rows = lax.optimization_barrier(rows.astype(jnp.bfloat16)).astype(jnp.float32)
        return total.at[row_owner].add(rows)
    total = lax.fori_loop(0, N_BLK * N_COL, one_device, jnp.zeros((N_BLK, N_COL, TILE, scn_count), jnp.float32))
    return total.reshape(ROWS, scn_count)

def apply_backward(blocks, block_index, live, duals):
    scn_count = duals.shape[1]
    panels = duals.reshape(N_BLK, N_COL, TILE, scn_count)

    def one_device(device, total):
        row_owner = device // N_COL
        col_owner = device % N_COL
        block_mats = blocks[row_owner, col_owner].astype(jnp.float32)
        slots = block_index[row_owner, col_owner]
        row_block = slots // N_BLK
        col_block = slots % N_BLK
        keep_mask = (jnp.arange(NBLK) < live[row_owner, col_owner]).astype(jnp.float32)
        pieces = panels[row_owner][row_block].astype(jnp.float32)
        products = jnp.einsum('bkt,bks->bts', block_mats, pieces) * keep_mask[:, None, None]
        onehot = (col_block[None, :] == jnp.arange(N_BLK)[:, None]).astype(jnp.float32)
        cols = jnp.einsum('cb,bts->cts', onehot, products, precision=lax.Precision.HIGHEST)
        cols = lax.optimization_barrier(cols.astype(jnp.bfloat16)).astype(jnp.float32)
        return total.at[:, col_owner].add(cols)
    total = lax.fori_loop(0, N_BLK * N_COL, one_device, jnp.zeros((N_BLK, N_COL, TILE, scn_count), jnp.float32))
    return total.reshape(COLS, scn_count)

def reference(blocks, block_index, live, cost, rhs, upper, x_init, y_init, bounded):
    weight = jnp.sqrt(lax.optimization_barrier(jnp.sum(cost * cost, axis=0)) + EPS) / jnp.sqrt(lax.optimization_barrier(jnp.sum(rhs * rhs, axis=0)) + EPS)
    tau = (ETA / weight)[None, :]
    sigma = (ETA * weight)[None, :]
    primal = x_init
    dual = y_init
    for step in range(ITERS):
        kty = apply_backward(blocks, block_index, live, dual.astype(jnp.bfloat16))
        x_new = project_box(primal - tau * (cost - kty), upper, bounded)
        xbar = (2.0 * x_new - primal).astype(jnp.bfloat16)
        kx = apply_forward(blocks, block_index, live, xbar)
        dual = jnp.maximum(dual + sigma * (rhs - kx), 0.0)
        primal = x_new
    return (primal, dual)
```

```python
import functools

import jax
import jax.numpy as jnp
from jax import lax
from jax.experimental import pallas as pl
from jax.experimental.pallas import tpu as pltpu
from jax.sharding import PartitionSpec as P

ITERS = 2


ETA = 0.4
EPS = 1e-06
MAX_PEERS = 16
SPLIT_ROWS = 16

VMEM = pl.BlockSpec(memory_space=pltpu.VMEM)
SMEM = pl.BlockSpec(memory_space=pltpu.SMEM)
F32 = jnp.float32
BF16 = jnp.bfloat16


def call(body, outs, ins_specs, args, scratch=(), flops=0):
    nbytes = sum(a.size * a.dtype.itemsize for a in list(args) + list(outs))
    return pl.pallas_call(
        body,
        out_shape=list(outs),
        in_specs=ins_specs,
        out_specs=[VMEM] * len(outs),
        scratch_shapes=list(scratch),
        compiler_params=pltpu.CompilerParams(vmem_limit_bytes=32 * 1024 * 1024),
        cost_estimate=pl.CostEstimate(flops=flops, bytes_accessed=nbytes, transcendentals=0),
    )(*args)


def split_sums(values):
    high = values.astype(BF16)
    rest = values - high.astype(F32)
    middle = rest.astype(BF16)
    low = (rest - middle.astype(F32)).astype(BF16)
    return [high, middle, low]


def pack_sums(cost_sum, rhs_sum):
    rows = [r.astype(F32) for r in split_sums(cost_sum) + split_sums(rhs_sum)]
    rows.append(jnp.zeros((SPLIT_ROWS - len(rows), cost_sum.shape[1]), F32))
    return jnp.concatenate(rows, axis=0).astype(BF16)


def unpack_sums(packed):
    rows = packed.astype(F32)
    return rows[0:1] + rows[1:2] + rows[2:3], rows[3:4] + rows[4:5] + rows[5:6]


def prep_body(cost, rhs, y, out):
    tile = y.shape[0]
    out[0:tile, :] = y[...].astype(BF16)
    c, r = cost[...], rhs[...]
    out[tile:, :] = pack_sums(jnp.sum(c * c, axis=0, keepdims=True), jnp.sum(r * r, axis=0, keepdims=True))


def dense_body(n_blk, n_col, index, live, blocks, *outs):
    tile = blocks.shape[-1]
    me_c = lax.axis_index("col")
    for out in outs:
        out[...] = jnp.zeros(out.shape, BF16)

    def one(k, carry):
        position = index[0, 0, k]
        rel = (position // n_blk) ^ me_c
        col = position % n_blk
        for s, out in enumerate(outs):

            @pl.when(rel == s)
            def _():
                out[:, pl.ds(pl.multiple_of(col * tile, tile), tile)] = blocks[0, 0, k]

        return carry

    lax.fori_loop(0, live[0, 0], one, 0)


def transposed_dot(mat, vec):
    return lax.dot_general(mat, vec, (((0,), (0,)), ((), ())), preferred_element_type=F32)


def first_terms_body(n_blk, n_col, *refs):
    payloads, mats = refs[:n_col], refs[n_col : 2 * n_col]
    outs, scratch = refs[2 * n_col : 2 * n_col + n_blk], refs[-1]
    tile = mats[0].shape[0]
    me_b = lax.axis_index("blk")
    total = transposed_dot(mats[0][...], payloads[0][0:tile, :])
    cost_sum, rhs_sum = unpack_sums(payloads[0][tile:, :])
    for s in range(1, n_col):
        total += transposed_dot(mats[s][...], payloads[s][0:tile, :])
        c, r = unpack_sums(payloads[s][tile:, :])
        cost_sum += c
        rhs_sum += r
    scratch[...] = total
    packed = pack_sums(cost_sum, rhs_sum)
    for t, out in enumerate(outs):
        rows = pl.ds(pl.multiple_of((me_b ^ t) * tile, tile), tile)
        out[0:tile, :] = scratch[rows, :].astype(BF16)
        out[tile:, :] = packed


def project(primal, grad, tau, upper, bounded):
    value = primal - tau * grad
    capped = jnp.where(bounded > 0, jnp.minimum(value, upper), value)
    return jnp.maximum(capped, 0.0)


def first_primal_body(n_blk, *refs):
    terms = refs[:n_blk]
    cost, primal, upper, bounded = refs[n_blk : n_blk + 4]
    x_out, xbar_out, scales_out = refs[n_blk + 4 :]
    tile = cost.shape[0]
    kty = terms[0][0:tile, :].astype(F32)
    cost_sum, rhs_sum = unpack_sums(terms[0][tile:, :])
    for term in terms[1:]:
        kty += term[0:tile, :].astype(F32)
        c, r = unpack_sums(term[tile:, :])
        cost_sum += c
        rhs_sum += r
    weight = jnp.sqrt(cost_sum + EPS) / jnp.sqrt(rhs_sum + EPS)
    tau = ETA / weight
    sigma = ETA * weight
    scales_out[...] = jnp.concatenate([tau, sigma, jnp.zeros((6, tau.shape[1]), F32)], axis=0)
    x = primal[...]
    x_new = project(x, cost[...] - kty, tau, upper[...], bounded[...])
    x_out[...] = x_new
    xbar_out[...] = (2.0 * x_new - x).astype(BF16)


def primal_body(n, last, *refs):
    terms = refs[:n]
    cost, primal, upper, bounded, scales = refs[n : n + 5]
    x_out, xbar_out = refs[n + 5 :]
    kty = terms[0][...].astype(F32)
    for term in terms[1:]:
        kty += term[...].astype(F32)
    x = primal[...]
    x_new = project(x, cost[...] - kty, scales[0:1, :], upper[...], bounded[...])
    x_out[...] = x_new
    xbar_out[...] = (2.0 * x_new - x).astype(BF16)


def dual_body(n_blk, n_col, last, *refs):
    n = n_blk * n_col
    bars, slabs = refs[:n], refs[n : n + n_col]
    dual, rhs, scales = refs[n + n_col : n + n_col + 3]
    y_out = refs[n + n_col + 3]
    tile = dual.shape[0]
    me_b = lax.axis_index("blk")
    field = refs[-2]
    scratch = refs[-1]
    kx = jnp.zeros(dual.shape, F32)
    for s in range(n_col):
        for t in range(n_blk):
            rows = pl.ds(pl.multiple_of((me_b ^ t) * tile, tile), tile)
            field[s, rows, :] = bars[t * n_col + s][...]
        kx += jnp.dot(slabs[s][...], field[s], preferred_element_type=F32)
    y_new = jnp.maximum(dual[...] + scales[1:2, :] * (rhs[...] - kx), 0.0)
    y_out[...] = y_new
    if not last:
        outs = refs[n + n_col + 4 : n + n_col + 4 + n]
        y_half = y_new.astype(BF16)
        for s in range(n_col):
            scratch[...] = transposed_dot(slabs[s][...], y_half)
            for t in range(n_blk):
                rows = pl.ds(pl.multiple_of((me_b ^ t) * tile, tile), tile)
                outs[t * n_col + s][...] = scratch[rows, :].astype(BF16)


def direct_plan(blocks, block_index, live, cost, rhs, upper, x_init, y_init, bounded):
    n_blk = lax.axis_size("blk")
    n_col = lax.axis_size("col")
    n = n_blk * n_col
    tile = blocks.shape[-1]
    scn = cost.shape[1]
    like = jax.ShapeDtypeStruct
    field_f32 = like((tile, scn), F32)
    field_half = like((tile, scn), BF16)
    payload = like((tile + SPLIT_ROWS, scn), BF16)
    limits = bounded[None, :]

    def over_col(value, s):
        return lax.ppermute(value, "col", [(c, c ^ s) for c in range(n_col)])

    def over_blk(value, t):
        return lax.ppermute(value, "blk", [(b, b ^ t) for b in range(n_blk)])

    def over_both(value, t, s):
        pairs = [(b * n_col + c, (b ^ t) * n_col + (c ^ s)) for b in range(n_blk) for c in range(n_col)]
        return lax.ppermute(value, ("blk", "col"), pairs)

    shifts = [(t, s) for t in range(n_blk) for s in range(n_col)]

    def spread(values):
        return [v if (t, s) == (0, 0) else over_both(v, t, s) for v, (t, s) in zip(values, shifts)]

    (own,) = call(prep_body, [payload], [VMEM] * 3, [cost, rhs, y_init])
    payloads = [own] + [over_col(own, s) for s in range(1, n_col)]
    mats = call(
        functools.partial(dense_body, n_blk, n_col),
        [like((tile, n_blk * tile), BF16)] * n_col,
        [SMEM, SMEM, VMEM],
        [block_index, live, blocks],
    )
    slabs = [mats[0]] + [over_col(mats[s], s) for s in range(1, n_col)]
    terms = call(
        functools.partial(first_terms_body, n_blk, n_col),
        [payload] * n_blk,
        [VMEM] * (2 * n_col),
        payloads + list(mats),
        scratch=[pltpu.VMEM((n_blk * tile, scn), F32)],
        flops=2 * n * tile * tile * scn,
    )
    terms = [terms[0]] + [over_blk(terms[t], t) for t in range(1, n_blk)]
    primal, xbar, scales = call(
        functools.partial(first_primal_body, n_blk),
        [field_f32, field_half, like((8, scn), F32)],
        [VMEM] * (n_blk + 4),
        terms + [cost, x_init, upper, limits],
    )
    dual = y_init
    for step in range(ITERS):
        last = step == ITERS - 1
        bars = spread([xbar] * n)
        outs = call(
            functools.partial(dual_body, n_blk, n_col, last),
            [field_f32] + ([] if last else [field_half] * n),
            [VMEM] * (n + n_col + 3),
            bars + slabs + [dual, rhs, scales],
            scratch=[pltpu.VMEM((n_col, n_blk * tile, scn), BF16), pltpu.VMEM((n_blk * tile, scn), F32)],
            flops=4 * n * tile * tile * scn,
        )
        dual = outs[0]
        if not last:
            terms = spread(outs[1:])
            primal, xbar = call(
                functools.partial(primal_body, n, last),
                [field_f32, field_half],
                [VMEM] * (n + 5),
                terms + [cost, primal, upper, limits, scales],
            )
    return (primal, dual)


def project_box(value, upper, bounded):
    capped = jnp.where(bounded[None, :] > 0, jnp.minimum(value, upper), value)
    return jnp.maximum(capped, 0.0)


def collectives_plan(blocks, block_index, live, cost, rhs, upper, x_init, y_init, bounded):
    block_mats = blocks[0, 0]
    slots = block_index[0, 0]
    n_blk = lax.axis_size("blk")
    n_col = lax.axis_size("col")
    tile_size = block_mats.shape[1]
    scn_count = cost.shape[1]
    row_block = slots // n_blk
    col_block = slots % n_blk
    keep_mask = (jnp.arange(slots.shape[0]) < live[0, 0]).astype(jnp.float32)[:, None, None]
    totals = lax.psum((jnp.sum(cost * cost, axis=0), jnp.sum(rhs * rhs, axis=0)), ("blk", "col"))
    weight = jnp.sqrt(totals[0] + EPS) / jnp.sqrt(totals[1] + EPS)
    tau = (ETA / weight)[None, :]
    sigma = (ETA * weight)[None, :]
    primal = x_init
    dual = y_init
    for step in range(ITERS):
        gathered = lax.all_gather(dual.astype(jnp.bfloat16), "col", axis=0, tiled=True)
        pieces = gathered.reshape(n_col, tile_size, scn_count)[row_block]
        products = (
            jnp.einsum("bkt,bks->bts", block_mats, pieces, preferred_element_type=jnp.float32)
            * keep_mask
        )
        cols = jnp.zeros((n_blk, tile_size, scn_count), jnp.float32).at[col_block].add(products)
        kty = lax.psum_scatter(
            cols.reshape(n_blk * tile_size, scn_count).astype(jnp.bfloat16),
            "blk",
            scatter_dimension=0,
            tiled=True,
        ).astype(jnp.float32)
        x_new = project_box(primal - tau * (cost - kty), upper, bounded)
        xbar = (2.0 * x_new - primal).astype(jnp.bfloat16)
        whole = lax.all_gather(xbar, "blk", axis=0, tiled=True)
        primal = x_new
        row_pieces = whole.reshape(n_blk, tile_size, scn_count)[col_block]
        row_products = (
            jnp.einsum("bkt,bts->bks", block_mats, row_pieces, preferred_element_type=jnp.float32)
            * keep_mask
        )
        rows = jnp.zeros((n_col, tile_size, scn_count), jnp.float32).at[row_block].add(row_products)
        terms = rows.reshape(n_col * tile_size, scn_count)
        kx = lax.psum_scatter(
            terms.astype(jnp.bfloat16), "col", scatter_dimension=0, tiled=True
        ).astype(jnp.float32)
        dual = jnp.maximum(dual + sigma * (rhs - kx), 0.0)
    return (primal, dual)


def shards(*args):
    n_blk, n_col = lax.axis_size("blk"), lax.axis_size("col")
    powers = n_blk & (n_blk - 1) == 0 and n_col & (n_col - 1) == 0
    plan = direct_plan if powers and n_blk * n_col <= MAX_PEERS else collectives_plan
    return plan(*args)


def solution(mesh):
    in_specs = (
        P("blk", "col", None, None, None),
        P("blk", "col", None),
        P("blk", "col"),
        P(("blk", "col"), ("groups", "rep")),
        P(("blk", "col"), ("groups", "rep")),
        P(("blk", "col"), ("groups", "rep")),
        P(("blk", "col"), ("groups", "rep")),
        P(("blk", "col"), ("groups", "rep")),
        P(("groups", "rep")),
    )
    out_specs = (P(("blk", "col"), ("groups", "rep")), P(("blk", "col"), ("groups", "rep")))
    return jax.shard_map(shards, mesh=mesh, in_specs=in_specs, out_specs=out_specs, check_vma=False)
```

```python
import functools

import jax
import jax.numpy as jnp
from jax import lax
from jax.experimental import pallas as pl
from jax.experimental.pallas import tpu as pltpu
from jax.sharding import PartitionSpec as P

ITERS = 2


ETA = 0.4
EPS = 1e-06
MAX_PEERS = 16
SPLIT_ROWS = 16

VMEM = pl.BlockSpec(memory_space=pltpu.VMEM)
SMEM = pl.BlockSpec(memory_space=pltpu.SMEM)
F32 = jnp.float32
BF16 = jnp.bfloat16


def call(body, outs, ins_specs, args, scratch=(), flops=0):
    nbytes = sum(a.size * a.dtype.itemsize for a in list(args) + list(outs))
    return pl.pallas_call(
        body,
        out_shape=list(outs),
        in_specs=ins_specs,
        out_specs=[VMEM] * len(outs),
        scratch_shapes=list(scratch),
        compiler_params=pltpu.CompilerParams(vmem_limit_bytes=32 * 1024 * 1024),
        cost_estimate=pl.CostEstimate(flops=flops, bytes_accessed=nbytes, transcendentals=0),
    )(*args)


def split_sums(values):
    high = values.astype(BF16)
    rest = values - high.astype(F32)
    middle = rest.astype(BF16)
    low = (rest - middle.astype(F32)).astype(BF16)
    return [high, middle, low]


def pack_sums(cost_sum, rhs_sum):
    rows = [r.astype(F32) for r in split_sums(cost_sum) + split_sums(rhs_sum)]
    rows.append(jnp.zeros((SPLIT_ROWS - len(rows), cost_sum.shape[1]), F32))
    return jnp.concatenate(rows, axis=0).astype(BF16)


def unpack_sums(packed):
    rows = packed.astype(F32)
    return rows[0:1] + rows[1:2] + rows[2:3], rows[3:4] + rows[4:5] + rows[5:6]


def prep_body(cost_hbm, rhs_hbm, y_hbm, out, cost, rhs, y, sems):
    copies = [
        pltpu.make_async_copy(source, target, sems.at[k])
        for k, (source, target) in enumerate(((y_hbm, y), (cost_hbm, cost), (rhs_hbm, rhs)))
    ]
    for copy in copies:
        copy.start()
    for copy in copies:
        copy.wait()
    tile = y.shape[0]
    out[0:tile, :] = y[...].astype(BF16)
    c, r = cost[...], rhs[...]
    out[tile:, :] = pack_sums(jnp.sum(c * c, axis=0, keepdims=True), jnp.sum(r * r, axis=0, keepdims=True))


def dense_body(n_blk, n_col, index, live, blocks, bounded, *outs):
    tile = blocks.shape[-1]
    me_c = lax.axis_index("col")
    *mats, limits = outs
    limits[...] = jnp.broadcast_to(bounded[...], limits.shape).astype(F32)
    for mat in mats:
        mat[...] = jnp.zeros(mat.shape, BF16)

    def one(k, carry):
        position = index[0, 0, k]
        rel = (position // n_blk) ^ me_c
        col = position % n_blk
        for s, mat in enumerate(mats):

            @pl.when(rel == s)
            def _():
                mat[:, pl.ds(pl.multiple_of(col * tile, tile), tile)] = blocks[0, 0, k]

        return carry

    lax.fori_loop(0, live[0, 0], one, 0)


def transposed_dot(mat, vec):
    return lax.dot_general(mat, vec, (((0,), (0,)), ((), ())), preferred_element_type=F32)


def first_terms_body(n_blk, n_col, *refs):
    payloads, mats = refs[:n_col], refs[n_col : 2 * n_col]
    out = refs[-1]
    tile = mats[0].shape[0]
    total = transposed_dot(mats[0][...], payloads[0][0:tile, :])
    cost_sum, rhs_sum = unpack_sums(payloads[0][tile:, :])
    for s in range(1, n_col):
        total += transposed_dot(mats[s][...], payloads[s][0:tile, :])
        c, r = unpack_sums(payloads[s][tile:, :])
        cost_sum += c
        rhs_sum += r
    packed = pack_sums(cost_sum, rhs_sum)
    for p in range(n_blk):
        out[p, 0:tile, :] = total[p * tile : (p + 1) * tile, :].astype(BF16)
        out[p, tile:, :] = packed


def project(primal, grad, tau, upper, limited):
    value = primal - tau * grad
    capped = jnp.where(limited > 0, jnp.minimum(value, upper), value)
    return jnp.maximum(capped, 0.0)


def write_bar(x_new, x, xbar_out):
    xbar = (2.0 * x_new - x).astype(BF16)
    for d in range(xbar_out.shape[0]):
        xbar_out[d] = xbar


def first_primal_body(terms, cost, primal, upper, limits, x_out, xbar_out, scales_out):
    tile = cost.shape[0]
    kty = terms[0, 0:tile, :].astype(F32)
    cost_sum, rhs_sum = unpack_sums(terms[0, tile:, :])
    for p in range(1, terms.shape[0]):
        kty += terms[p, 0:tile, :].astype(F32)
        c, r = unpack_sums(terms[p, tile:, :])
        cost_sum += c
        rhs_sum += r
    weight = jnp.sqrt(cost_sum + EPS) / jnp.sqrt(rhs_sum + EPS)
    tau = ETA / weight
    sigma = ETA * weight
    scales_out[...] = jnp.concatenate([tau, sigma, jnp.zeros((6, tau.shape[1]), F32)], axis=0)
    x = primal[...]
    x_new = project(x, cost[...] - kty, tau, upper[...], limits[0:1, :])
    x_out[...] = x_new
    write_bar(x_new, x, xbar_out)


def primal_body(terms, cost, primal, upper, limits, scales, x_out, xbar_out):
    kty = terms[0].astype(F32)
    for d in range(1, terms.shape[0]):
        kty += terms[d].astype(F32)
    x = primal[...]
    x_new = project(x, cost[...] - kty, scales[0:1, :], upper[...], limits[0:1, :])
    x_out[...] = x_new
    write_bar(x_new, x, xbar_out)


def dual_body(n_blk, n_col, last, bars, *refs):
    slabs = refs[:n_col]
    dual, rhs, scales, y_out = refs[n_col : n_col + 4]
    tile = dual.shape[0]
    me_c = lax.axis_index("col")
    field = refs[-1]
    kx = jnp.zeros(dual.shape, F32)
    for s in range(n_col):
        for p in range(n_blk):
            field[s, p * tile : (p + 1) * tile, :] = bars[p * n_col + (me_c ^ s)]
        kx += jnp.dot(slabs[s][...], field[s], preferred_element_type=F32)
    y_new = jnp.maximum(dual[...] + scales[1:2, :] * (rhs[...] - kx), 0.0)
    y_out[...] = y_new
    if not last:
        out = refs[n_col + 4]
        y_half = y_new.astype(BF16)
        for s in range(n_col):
            total = transposed_dot(slabs[s][...], y_half)
            for p in range(n_blk):
                out[p * n_col + (me_c ^ s)] = total[p * tile : (p + 1) * tile, :].astype(BF16)


def direct_plan(blocks, block_index, live, cost, rhs, upper, x_init, y_init, bounded):
    n_blk = lax.axis_size("blk")
    n_col = lax.axis_size("col")
    n = n_blk * n_col
    tile = blocks.shape[-1]
    scn = cost.shape[1]
    like = jax.ShapeDtypeStruct
    field_f32 = like((tile, scn), F32)
    spread = like((n, tile, scn), BF16)
    rows = like((8, scn), F32)
    payload = like((tile + SPLIT_ROWS, scn), BF16)

    def over_col(value, s):
        return lax.ppermute(value, "col", [(c, c ^ s) for c in range(n_col)])

    def exchange(value, axes):
        return lax.all_to_all(value, axes, 0, 0, tiled=True)

    (own,) = call(
        prep_body,
        [payload],
        [pl.BlockSpec(memory_space=pltpu.HBM)] * 3,
        [cost, rhs, y_init],
        scratch=[pltpu.VMEM((tile, scn), F32)] * 3 + [pltpu.SemaphoreType.DMA((3,))],
    )
    payloads = [own] + [over_col(own, s) for s in range(1, n_col)]
    *mats, limits = call(
        functools.partial(dense_body, n_blk, n_col),
        [like((tile, n_blk * tile), BF16)] * n_col + [rows],
        [SMEM, SMEM, VMEM, VMEM],
        [block_index, live, blocks, bounded[None, :]],
    )
    slabs = [mats[0]] + [over_col(mats[s], s) for s in range(1, n_col)]
    (terms,) = call(
        functools.partial(first_terms_body, n_blk, n_col),
        [like((n_blk, *payload.shape), BF16)],
        [VMEM] * (2 * n_col),
        payloads + list(mats),
        flops=2 * n * tile * tile * scn,
    )
    primal, bars, scales = call(
        first_primal_body,
        [field_f32, spread, rows],
        [VMEM] * 5,
        [exchange(terms, "blk"), cost, x_init, upper, limits],
    )
    dual = y_init
    for step in range(ITERS):
        last = step == ITERS - 1
        outs = call(
            functools.partial(dual_body, n_blk, n_col, last),
            [field_f32] + ([] if last else [spread]),
            [VMEM] * (n_col + 4),
            [exchange(bars, ("blk", "col"))] + slabs + [dual, rhs, scales],
            scratch=[pltpu.VMEM((n_col, n_blk * tile, scn), BF16)],
            flops=4 * n * tile * tile * scn,
        )
        dual = outs[0]
        if not last:
            primal, bars = call(
                primal_body,
                [field_f32, spread],
                [VMEM] * 6,
                [exchange(outs[1], ("blk", "col")), cost, primal, upper, limits, scales],
            )
    return (primal, dual)


def project_box(value, upper, bounded):
    capped = jnp.where(bounded[None, :] > 0, jnp.minimum(value, upper), value)
    return jnp.maximum(capped, 0.0)


def collectives_plan(blocks, block_index, live, cost, rhs, upper, x_init, y_init, bounded):
    block_mats = blocks[0, 0]
    slots = block_index[0, 0]
    n_blk = lax.axis_size("blk")
    n_col = lax.axis_size("col")
    tile_size = block_mats.shape[1]
    scn_count = cost.shape[1]
    row_block = slots // n_blk
    col_block = slots % n_blk
    keep_mask = (jnp.arange(slots.shape[0]) < live[0, 0]).astype(jnp.float32)[:, None, None]
    totals = lax.psum((jnp.sum(cost * cost, axis=0), jnp.sum(rhs * rhs, axis=0)), ("blk", "col"))
    weight = jnp.sqrt(totals[0] + EPS) / jnp.sqrt(totals[1] + EPS)
    tau = (ETA / weight)[None, :]
    sigma = (ETA * weight)[None, :]
    primal = x_init
    dual = y_init
    for step in range(ITERS):
        gathered = lax.all_gather(dual.astype(jnp.bfloat16), "col", axis=0, tiled=True)
        pieces = gathered.reshape(n_col, tile_size, scn_count)[row_block]
        products = (
            jnp.einsum("bkt,bks->bts", block_mats, pieces, preferred_element_type=jnp.float32)
            * keep_mask
        )
        cols = jnp.zeros((n_blk, tile_size, scn_count), jnp.float32).at[col_block].add(products)
        kty = lax.psum_scatter(
            cols.reshape(n_blk * tile_size, scn_count).astype(jnp.bfloat16),
            "blk",
            scatter_dimension=0,
            tiled=True,
        ).astype(jnp.float32)
        x_new = project_box(primal - tau * (cost - kty), upper, bounded)
        xbar = (2.0 * x_new - primal).astype(jnp.bfloat16)
        whole = lax.all_gather(xbar, "blk", axis=0, tiled=True)
        primal = x_new
        row_pieces = whole.reshape(n_blk, tile_size, scn_count)[col_block]
        row_products = (
            jnp.einsum("bkt,bts->bks", block_mats, row_pieces, preferred_element_type=jnp.float32)
            * keep_mask
        )
        rows = jnp.zeros((n_col, tile_size, scn_count), jnp.float32).at[row_block].add(row_products)
        terms = rows.reshape(n_col * tile_size, scn_count)
        kx = lax.psum_scatter(
            terms.astype(jnp.bfloat16), "col", scatter_dimension=0, tiled=True
        ).astype(jnp.float32)
        dual = jnp.maximum(dual + sigma * (rhs - kx), 0.0)
    return (primal, dual)


def shards(*args):
    n_blk, n_col = lax.axis_size("blk"), lax.axis_size("col")
    powers = n_blk & (n_blk - 1) == 0 and n_col & (n_col - 1) == 0
    plan = direct_plan if powers and n_blk * n_col <= MAX_PEERS else collectives_plan
    return plan(*args)


def solution(mesh):
    in_specs = (
        P("blk", "col", None, None, None),
        P("blk", "col", None),
        P("blk", "col"),
        P(("blk", "col"), ("groups", "rep")),
        P(("blk", "col"), ("groups", "rep")),
        P(("blk", "col"), ("groups", "rep")),
        P(("blk", "col"), ("groups", "rep")),
        P(("blk", "col"), ("groups", "rep")),
        P(("groups", "rep")),
    )
    out_specs = (P(("blk", "col"), ("groups", "rep")), P(("blk", "col"), ("groups", "rep")))
    return jax.shard_map(shards, mesh=mesh, in_specs=in_specs, out_specs=out_specs, check_vma=False)
```

```python
import functools

import jax
import jax.numpy as jnp
from jax import lax
from jax.experimental import pallas as pl
from jax.experimental.pallas import tpu as pltpu
from jax.sharding import PartitionSpec as P

ITERS = 2


ETA = 0.4
EPS = 1e-06
MAX_MATRIX = 8 * 1024 * 1024
PARTS = 3
FIELDS = 5
SLOT_LANE = 2 * PARTS

MIB = 1024 * 1024
VMEM = pl.BlockSpec(memory_space=pltpu.VMEM)
SMEM = pl.BlockSpec(memory_space=pltpu.SMEM)
ANY = pl.BlockSpec(memory_space=pl.ANY)
F32 = jnp.float32
BF16 = jnp.bfloat16


def call(body, outs, in_specs, args, scratch=(), flops=0, limit=32):
    nbytes = sum(a.size * a.dtype.itemsize for a in list(args) + list(outs))
    return pl.pallas_call(
        body,
        out_shape=list(outs),
        in_specs=in_specs,
        out_specs=[VMEM] * len(outs),
        scratch_shapes=list(scratch),
        compiler_params=pltpu.CompilerParams(vmem_limit_bytes=limit * MIB),
        cost_estimate=pl.CostEstimate(flops=flops, bytes_accessed=nbytes, transcendentals=0),
    )(*args)


def split_parts(values):
    high = values.astype(BF16).astype(F32)
    rest = values - high
    middle = rest.astype(BF16).astype(F32)
    low = (rest - middle).astype(BF16).astype(F32)
    return [high, middle, low]


def project(primal, grad, tau, upper, limited):
    value = primal - tau * grad
    capped = jnp.where(limited > 0, jnp.minimum(value, upper), value)
    return jnp.maximum(capped, 0.0)


def share_body(blocks, out):
    tile = blocks.shape[-1]
    half = out.shape[0] // tile
    first = lax.axis_index("rep") * half
    for k in range(half):
        out[k * tile : (k + 1) * tile, :] = blocks[0, 0, first + k]


def prep_body(index, live, cost_in, rhs_in, upper_in, x_in, y_in, bounded, out, *scratch):
    *fields, sems = scratch
    copies = [
        pltpu.make_async_copy(source, target, sems.at[k])
        for k, (source, target) in enumerate(zip((cost_in, rhs_in, upper_in, x_in, y_in), fields))
    ]
    for copy in copies:
        copy.start()
    n, _, tile = out.shape
    scn = fields[0].shape[1]
    part = scn // n
    nslots = index.shape[-1]
    lane = lax.broadcasted_iota(jnp.int32, (scn, tile), 1)
    info = jnp.zeros((scn, tile), F32)
    for k in range(nslots):
        info = jnp.where(lane == SLOT_LANE + k, index[0, 0, k].astype(F32), info)
    info = jnp.where(lane == SLOT_LANE + nslots, live[0, 0].astype(F32), info)
    limited = jnp.broadcast_to(bounded[...].astype(F32), (tile, scn)).T
    info = jnp.where(lane == SLOT_LANE + nslots + 1, limited, info)
    for j, (copy, field) in enumerate(zip(copies, fields)):
        copy.wait()
        turned = field[...].T
        if j < 2:
            for k, values in enumerate(split_parts(jnp.sum(turned * turned, axis=1, keepdims=True))):
                info = jnp.where(lane == PARTS * j + k, values, info)
        half = turned.astype(BF16)
        for d in range(n):
            out[d, j * part : (j + 1) * part, :] = half[d * part : (d + 1) * part, :]
    half = info.astype(BF16)
    for d in range(n):
        out[d, FIELDS * part :, :] = half[d * part : (d + 1) * part, :]


def main_body(n_blk, n_col, shifts, slots, recv, blocks, *refs):
    n = n_blk * n_col
    mine, theirs = refs[: n - 1], refs[n - 1 : 2 * (n - 1)]
    out, mat = refs[2 * (n - 1) :]
    tile = blocks.shape[-1]
    nslots = blocks.shape[2]
    half = mine[0].shape[0] // tile
    part = recv.shape[1] // (FIELDS + 1)
    me_b, me_c, me_r = lax.axis_index("blk"), lax.axis_index("col"), lax.axis_index("rep")
    mat[...] = jnp.zeros(mat.shape, BF16)

    def place(t, s, slot, block):
        blk, col = me_b ^ t, me_c ^ s
        owner = blk * n_col + col
        position = slots[owner, slot]
        row = pl.multiple_of((blk * n_col + position // n_blk) * tile, tile)
        column = pl.multiple_of(((position % n_blk) * n_col + col) * tile, tile)

        @pl.when(slot < slots[owner, nslots])
        def _():
            mat[pl.ds(row, tile), pl.ds(column, tile)] = block()

    for k in range(nslots):
        place(0, 0, k, lambda k=k: blocks[0, 0, k])
    for (t, s), own_part, other_part in zip(shifts, mine, theirs):
        for k in range(half):
            place(t, s, me_r * half + k, lambda k=k, r=own_part: r[k * tile : (k + 1) * tile, :])
            place(t, s, (1 - me_r) * half + k, lambda k=k, r=other_part: r[k * tile : (k + 1) * tile, :])

    def field(j):
        return jnp.concatenate([recv[d, j * part : (j + 1) * part, :] for d in range(n)], axis=1).astype(F32)

    cost, rhs, upper, primal, dual = (field(j) for j in range(FIELDS))
    info = recv[0, FIELDS * part :, :].astype(F32)
    limited = info[:, SLOT_LANE + nslots + 1 : SLOT_LANE + nslots + 2]
    sums = [jnp.zeros((part, 1), F32)] * 2
    for d in range(n):
        info = recv[d, FIELDS * part :, :].astype(F32)
        for j in range(2):
            sums[j] += (info[:, PARTS * j : PARTS * j + 1] + info[:, PARTS * j + 1 : PARTS * j + 2]) + info[
                :, PARTS * j + 2 : PARTS * j + 3
            ]
    weight = jnp.sqrt(sums[0] + EPS) / jnp.sqrt(sums[1] + EPS)
    tau = ETA / weight
    sigma = ETA * weight

    def store(j, values):
        values = values.astype(BF16)
        for d in range(n):
            out[d, j * part : (j + 1) * part, :] = values[:, d * tile : (d + 1) * tile]

    for step in range(ITERS):
        kty = jnp.dot(dual.astype(BF16), mat[...], preferred_element_type=F32)
        store(2 * step, kty)
        x_new = project(primal, cost - kty, tau, upper, limited)
        xbar = (2.0 * x_new - primal).astype(BF16)
        primal = x_new
        kx = lax.dot_general(xbar, mat[...], (((1,), (1,)), ((), ())), preferred_element_type=F32)
        store(2 * step + 1, kx)
        dual = jnp.maximum(dual + sigma * (rhs - kx), 0.0)
    lane = lax.broadcasted_iota(jnp.int32, (part, tile), 1)
    packed = jnp.zeros((part, tile), F32)
    for k, values in enumerate(split_parts(weight)):
        packed = jnp.where(lane == k, values, packed)
    for d in range(n):
        out[d, 2 * ITERS * part :, :] = packed.astype(BF16)


def final_body(recv, cost, rhs, upper, x_in, y_in, bounded, x_out, y_out):
    n, rows, tile = recv.shape
    part = rows // (2 * ITERS + 1)

    def turned(j):
        return recv[:, j * part : (j + 1) * part, :].reshape(n * part, tile).astype(F32).T

    packed = turned(2 * ITERS)
    weight = packed[0:1] + packed[1:2] + packed[2:3]
    tau = ETA / weight
    sigma = ETA * weight
    primal, dual = x_in[...], y_in[...]
    for step in range(ITERS):
        primal = project(primal, cost[...] - turned(2 * step), tau, upper[...], bounded[...])
        dual = jnp.maximum(dual + sigma * (rhs[...] - turned(2 * step + 1)), 0.0)
    x_out[...] = primal
    y_out[...] = dual


def local_plan(blocks, block_index, live, cost, rhs, upper, x_init, y_init, bounded):
    n_blk, n_col = lax.axis_size("blk"), lax.axis_size("col")
    n = n_blk * n_col
    tile, nslots = blocks.shape[-1], blocks.shape[2]
    scn = cost.shape[1]
    part = scn // n
    like = jax.ShapeDtypeStruct
    limits = bounded[None, :]

    def spread(value):
        return lax.all_to_all(value, ("blk", "col"), 0, 0, tiled=True)

    def move(value, t, s):
        pairs = [(b * n_col + c, (b ^ t) * n_col + (c ^ s)) for b in range(n_blk) for c in range(n_col)]
        return lax.ppermute(value, ("blk", "col"), pairs)

    (share,) = call(share_body, [like((nslots // 2 * tile, tile), BF16)], [VMEM], [blocks])
    (sent,) = call(
        prep_body,
        [like((n, (FIELDS + 1) * part, tile), BF16)],
        [SMEM, SMEM] + [ANY] * FIELDS + [VMEM],
        [block_index, live, cost, rhs, upper, x_init, y_init, limits],
        scratch=[pltpu.VMEM((tile, scn), F32)] * FIELDS + [pltpu.SemaphoreType.DMA((FIELDS,))],
        limit=60,
    )
    far = n_blk // 2
    near = [(t, s) for t in range(far) for s in range(n_col) if (t, s) != (0, 0)]
    mine = {(far, 0): move(share, far, 0)}
    for t, s in near:
        mine[t, s] = move(share, t, s)
    recv = spread(sent)
    for t, s in near:
        mine[far + t, s] = move(mine[far, 0], t, s)
    shifts = list(mine)
    theirs = [lax.ppermute(mine[shift], "rep", [(0, 1), (1, 0)]) for shift in shifts]
    slots = recv[:, FIELDS * part, SLOT_LANE : SLOT_LANE + nslots + 1].astype(jnp.int32)
    (products,) = call(
        functools.partial(main_body, n_blk, n_col, shifts),
        [like((n, (2 * ITERS + 1) * part, tile), BF16)],
        [SMEM] + [VMEM] * (2 * n),
        [slots, recv, blocks] + [mine[shift] for shift in shifts] + theirs,
        scratch=[pltpu.VMEM((n * tile, n * tile), BF16)],
        flops=4 * ITERS * n * n * tile * tile * part,
    )
    return call(
        final_body,
        [like((tile, scn), F32)] * 2,
        [VMEM] * (FIELDS + 2),
        [spread(products), cost, rhs, upper, x_init, y_init, limits],
    )


def project_box(value, upper, bounded):
    capped = jnp.where(bounded[None, :] > 0, jnp.minimum(value, upper), value)
    return jnp.maximum(capped, 0.0)


def collectives_plan(blocks, block_index, live, cost, rhs, upper, x_init, y_init, bounded):
    block_mats = blocks[0, 0]
    slots = block_index[0, 0]
    n_blk = lax.axis_size("blk")
    n_col = lax.axis_size("col")
    tile_size = block_mats.shape[1]
    scn_count = cost.shape[1]
    row_block = slots // n_blk
    col_block = slots % n_blk
    keep_mask = (jnp.arange(slots.shape[0]) < live[0, 0]).astype(jnp.float32)[:, None, None]
    totals = lax.psum((jnp.sum(cost * cost, axis=0), jnp.sum(rhs * rhs, axis=0)), ("blk", "col"))
    weight = jnp.sqrt(totals[0] + EPS) / jnp.sqrt(totals[1] + EPS)
    tau = (ETA / weight)[None, :]
    sigma = (ETA * weight)[None, :]
    primal = x_init
    dual = y_init
    for step in range(ITERS):
        gathered = lax.all_gather(dual.astype(jnp.bfloat16), "col", axis=0, tiled=True)
        pieces = gathered.reshape(n_col, tile_size, scn_count)[row_block]
        products = (
            jnp.einsum("bkt,bks->bts", block_mats, pieces, preferred_element_type=jnp.float32)
            * keep_mask
        )
        cols = jnp.zeros((n_blk, tile_size, scn_count), jnp.float32).at[col_block].add(products)
        kty = lax.psum_scatter(
            cols.reshape(n_blk * tile_size, scn_count).astype(jnp.bfloat16),
            "blk",
            scatter_dimension=0,
            tiled=True,
        ).astype(jnp.float32)
        x_new = project_box(primal - tau * (cost - kty), upper, bounded)
        xbar = (2.0 * x_new - primal).astype(jnp.bfloat16)
        whole = lax.all_gather(xbar, "blk", axis=0, tiled=True)
        primal = x_new
        row_pieces = whole.reshape(n_blk, tile_size, scn_count)[col_block]
        row_products = (
            jnp.einsum("bkt,bts->bks", block_mats, row_pieces, preferred_element_type=jnp.float32)
            * keep_mask
        )
        rows = jnp.zeros((n_col, tile_size, scn_count), jnp.float32).at[row_block].add(row_products)
        terms = rows.reshape(n_col * tile_size, scn_count)
        kx = lax.psum_scatter(
            terms.astype(jnp.bfloat16), "col", scatter_dimension=0, tiled=True
        ).astype(jnp.float32)
        dual = jnp.maximum(dual + sigma * (rhs - kx), 0.0)
    return (primal, dual)


def shards(*args):
    n_blk, n_col, n_rep = (lax.axis_size(axis) for axis in ("blk", "col", "rep"))
    blocks, cost = args[0], args[3]
    n, tile, nslots = n_blk * n_col, blocks.shape[-1], blocks.shape[2]
    fits = 2 * (n * tile) ** 2 <= MAX_MATRIX and cost.shape[1] % (16 * n) == 0
    even = n_blk & (n_blk - 1) == 0 and n_col & (n_col - 1) == 0 and n_blk > 1 and n_rep == 2 and nslots % 2 == 0
    x, y = (local_plan if fits and even else collectives_plan)(*args)
    return x, y


def solution(mesh):
    in_specs = (
        P("blk", "col", None, None, None),
        P("blk", "col", None),
        P("blk", "col"),
        P(("blk", "col"), ("groups", "rep")),
        P(("blk", "col"), ("groups", "rep")),
        P(("blk", "col"), ("groups", "rep")),
        P(("blk", "col"), ("groups", "rep")),
        P(("blk", "col"), ("groups", "rep")),
        P(("groups", "rep")),
    )
    out_specs = (P(("blk", "col"), ("groups", "rep")), P(("blk", "col"), ("groups", "rep")))
    return jax.shard_map(shards, mesh=mesh, in_specs=in_specs, out_specs=out_specs, check_vma=False)
```

```python
import functools

import jax
import jax.numpy as jnp
from jax import lax
from jax.experimental import pallas as pl
from jax.experimental.pallas import tpu as pltpu
from jax.sharding import PartitionSpec as P

ITERS = 2


ETA = 0.4
EPS = 1e-06
MAX_MATRIX = 8 * 1024 * 1024
PARTS = 3
FIELDS = 5
SLOT_ROW = 2 * PARTS

MIB = 1024 * 1024
VMEM = pl.BlockSpec(memory_space=pltpu.VMEM)
SMEM = pl.BlockSpec(memory_space=pltpu.SMEM)
ANY = pl.BlockSpec(memory_space=pl.ANY)
F32 = jnp.float32
BF16 = jnp.bfloat16


def call(body, outs, in_specs, args, scratch=(), flops=0, limit=32):
    nbytes = sum(a.size * a.dtype.itemsize for a in list(args) + list(outs))
    return pl.pallas_call(
        body,
        out_shape=list(outs),
        in_specs=in_specs,
        out_specs=[VMEM] * len(outs),
        scratch_shapes=list(scratch),
        compiler_params=pltpu.CompilerParams(vmem_limit_bytes=limit * MIB),
        cost_estimate=pl.CostEstimate(flops=flops, bytes_accessed=nbytes, transcendentals=0),
    )(*args)


def split_parts(values):
    high = values.astype(BF16).astype(F32)
    rest = values - high
    middle = rest.astype(BF16).astype(F32)
    low = (rest - middle).astype(BF16).astype(F32)
    return [high, middle, low]


def project(primal, grad, tau, upper, limited):
    value = primal - tau * grad
    capped = jnp.where(limited > 0, jnp.minimum(value, upper), value)
    return jnp.maximum(capped, 0.0)


def share_body(blocks, out):
    tile = blocks.shape[-1]
    half = out.shape[0] // tile
    first = lax.axis_index("rep") * half
    for k in range(half):
        out[k * tile : (k + 1) * tile, :] = blocks[0, 0, first + k]


def touch_body(part, after, out):
    del part, after, out


def prep_body(index_in, live_in, cost_in, rhs_in, upper_in, x_in, y_in, after, out, token, *scratch):
    del after
    token[...] = jnp.zeros(token.shape, F32)
    *fields, index, live, sems = scratch
    sources = (cost_in, rhs_in, upper_in, x_in, y_in, index_in, live_in)
    copies = [
        pltpu.make_async_copy(source, target, sems.at[k])
        for k, (source, target) in enumerate(zip(sources, (*fields, index, live)))
    ]
    for copy in copies:
        copy.start()
    n, _, tile = out.shape
    scn = fields[0].shape[1]
    part = scn // n
    nslots = index.shape[-1]
    rows = []
    for j, field in enumerate(fields):
        copies[j].wait()
        values = field[...]
        if j < 2:
            rows += split_parts(jnp.sum(values * values, axis=0, keepdims=True))
        half = values.T.astype(BF16)
        for d in range(n):
            out[d, j * part : (j + 1) * part, :] = half[d * part : (d + 1) * part, :]
    copies[FIELDS].wait()
    copies[FIELDS + 1].wait()
    lane = lax.broadcasted_iota(jnp.int32, (1, tile), 1)
    row = jnp.where(lane == nslots, live[0, 0].astype(F32), 0.0)
    for k in range(nslots):
        row = jnp.where(lane == k, index[0, 0, k].astype(F32), row)
    rows += [row, jnp.zeros((part - len(rows) - 1, tile), F32)]
    half = jnp.concatenate(rows, axis=0).astype(BF16)
    for d in range(n):
        out[d, FIELDS * part :, :] = half


def main_body(n_blk, n_col, shifts, slots, recv, bounded, blocks, *refs):
    n = n_blk * n_col
    mine, theirs = refs[: n - 1], refs[n - 1 : 2 * (n - 1)]
    out, scales, mat, turned = refs[2 * (n - 1) :]
    tile = blocks.shape[-1]
    nslots = blocks.shape[2]
    half = mine[0].shape[0] // tile
    part = recv.shape[1] // (FIELDS + 1)
    me_b, me_c, me_r = lax.axis_index("blk"), lax.axis_index("col"), lax.axis_index("rep")
    mat[...] = jnp.zeros(mat.shape, BF16)

    def place(t, s, slot, block):
        blk, col = me_b ^ t, me_c ^ s
        owner = blk * n_col + col
        position = slots[owner, slot]
        row = pl.multiple_of((blk * n_col + position // n_blk) * tile, tile)
        column = pl.multiple_of(((position % n_blk) * n_col + col) * tile, tile)

        @pl.when(slot < slots[owner, nslots])
        def _():
            mat[pl.ds(row, tile), pl.ds(column, tile)] = block()

    for k in range(nslots):
        place(0, 0, k, lambda k=k: blocks[0, 0, k])
    for (t, s), own_part, other_part in zip(shifts, mine, theirs):
        for k in range(half):
            place(t, s, me_r * half + k, lambda k=k, r=own_part: r[k * tile : (k + 1) * tile, :])
            place(t, s, (1 - me_r) * half + k, lambda k=k, r=other_part: r[k * tile : (k + 1) * tile, :])

    def field(j):
        return jnp.concatenate([recv[d, j * part : (j + 1) * part, :] for d in range(n)], axis=1).astype(F32)

    cost, rhs, upper, primal, dual = (field(j) for j in range(FIELDS))
    sums = [jnp.zeros((1, tile), F32)] * 2
    for d in range(n):
        info = recv[d, FIELDS * part :, :].astype(F32)
        for j in range(2):
            first, second, third = (info[PARTS * j + k : PARTS * j + k + 1] for k in range(PARTS))
            sums[j] += (first + second) + third
    weight = jnp.sqrt(sums[0] + EPS) / jnp.sqrt(sums[1] + EPS)
    rows = jnp.concatenate([ETA / weight, ETA * weight, bounded[...].astype(F32), jnp.zeros((5, tile), F32)], axis=0)
    scales[...] = rows
    turned[...] = jnp.concatenate([rows, jnp.zeros((tile - 8, tile), F32)], axis=0).T
    own = turned[pl.ds(pl.multiple_of((me_b * n_col + me_c) * part, part), part), :]
    tau, sigma, limited = own[:, 0:1], own[:, 1:2], own[:, 2:3]

    def store(j, values):
        values = values.astype(BF16)
        for d in range(n):
            out[d, j * part : (j + 1) * part, :] = values[:, d * tile : (d + 1) * tile]

    for step in range(ITERS):
        kty = jnp.dot(dual.astype(BF16), mat[...], preferred_element_type=F32)
        store(2 * step, kty)
        x_new = project(primal, cost - kty, tau, upper, limited)
        xbar = (2.0 * x_new - primal).astype(BF16)
        primal = x_new
        kx = lax.dot_general(xbar, mat[...], (((1,), (1,)), ((), ())), preferred_element_type=F32)
        store(2 * step + 1, kx)
        dual = jnp.maximum(dual + sigma * (rhs - kx), 0.0)


def final_body(recv, scales, cost, rhs, upper, x_in, y_in, bounded, x_out, y_out):
    n, rows, tile = recv.shape
    part = rows // (2 * ITERS)

    def turned(j):
        return recv[:, j * part : (j + 1) * part, :].reshape(n * part, tile).astype(F32).T

    tau, sigma = scales[0:1, :], scales[1:2, :]
    primal, dual = x_in[...], y_in[...]
    for step in range(ITERS):
        primal = project(primal, cost[...] - turned(2 * step), tau, upper[...], bounded[...])
        dual = jnp.maximum(dual + sigma * (rhs[...] - turned(2 * step + 1)), 0.0)
    x_out[...] = primal
    y_out[...] = dual


def local_plan(blocks, block_index, live, cost, rhs, upper, x_init, y_init, bounded):
    n_blk, n_col = lax.axis_size("blk"), lax.axis_size("col")
    n = n_blk * n_col
    tile, nslots = blocks.shape[-1], blocks.shape[2]
    scn = cost.shape[1]
    part = scn // n
    like = jax.ShapeDtypeStruct
    limits = bounded[None, :]

    def spread(value):
        return lax.all_to_all(value, ("blk", "col"), 0, 0, tiled=True)

    def move(value, t, s):
        pairs = [(b * n_col + c, (b ^ t) * n_col + (c ^ s)) for b in range(n_blk) for c in range(n_col)]
        return lax.ppermute(value, ("blk", "col"), pairs)

    (share,) = call(share_body, [like((nslots // 2 * tile, tile), BF16)], [VMEM], [blocks])
    far = n_blk // 2
    near = [(t, s) for t in range(far) for s in range(n_col) if (t, s) != (0, 0)]
    mine = {(far, 0): move(share, far, 0)}
    for t, s in near:
        mine[t, s] = move(share, t, s)
    sent, token = call(
        prep_body,
        [like((n, (FIELDS + 1) * part, tile), BF16), like((8, 128), F32)],
        [ANY] * (FIELDS + 3),
        [block_index, live, cost, rhs, upper, x_init, y_init, mine[near[0]][:16]],
        scratch=[pltpu.VMEM((tile, scn), F32)] * FIELDS
        + [pltpu.SMEM(block_index.shape, jnp.int32), pltpu.SMEM(live.shape, jnp.int32)]
        + [pltpu.SemaphoreType.DMA((FIELDS + 2,))],
        limit=60,
    )
    recv = spread(sent)
    mine[far, 0] = pl.pallas_call(
        touch_body,
        out_shape=like(share.shape, share.dtype),
        in_specs=[ANY, ANY],
        out_specs=ANY,
        input_output_aliases={0: 0},
    )(mine[far, 0], token)
    for t, s in near:
        mine[far + t, s] = move(mine[far, 0], t, s)
    shifts = list(mine)
    theirs = [lax.ppermute(mine[shift], "rep", [(0, 1), (1, 0)]) for shift in shifts]
    slots = recv[:, FIELDS * part + SLOT_ROW, : nslots + 1].astype(jnp.int32)
    products, scales = call(
        functools.partial(main_body, n_blk, n_col, shifts),
        [like((n, 2 * ITERS * part, tile), BF16), like((8, scn), F32)],
        [SMEM] + [VMEM] * (2 * n + 1),
        [slots, recv, limits, blocks] + [mine[shift] for shift in shifts] + theirs,
        scratch=[pltpu.VMEM((n * tile, n * tile), BF16), pltpu.VMEM((tile, scn), F32)],
        flops=4 * ITERS * n * n * tile * tile * part,
    )
    return call(
        final_body,
        [like((tile, scn), F32)] * 2,
        [VMEM] * (FIELDS + 3),
        [spread(products), scales, cost, rhs, upper, x_init, y_init, limits],
    )


def project_box(value, upper, bounded):
    capped = jnp.where(bounded[None, :] > 0, jnp.minimum(value, upper), value)
    return jnp.maximum(capped, 0.0)


def collectives_plan(blocks, block_index, live, cost, rhs, upper, x_init, y_init, bounded):
    block_mats = blocks[0, 0]
    slots = block_index[0, 0]
    n_blk = lax.axis_size("blk")
    n_col = lax.axis_size("col")
    tile_size = block_mats.shape[1]
    scn_count = cost.shape[1]
    row_block = slots // n_blk
    col_block = slots % n_blk
    keep_mask = (jnp.arange(slots.shape[0]) < live[0, 0]).astype(jnp.float32)[:, None, None]
    totals = lax.psum((jnp.sum(cost * cost, axis=0), jnp.sum(rhs * rhs, axis=0)), ("blk", "col"))
    weight = jnp.sqrt(totals[0] + EPS) / jnp.sqrt(totals[1] + EPS)
    tau = (ETA / weight)[None, :]
    sigma = (ETA * weight)[None, :]
    primal = x_init
    dual = y_init
    for step in range(ITERS):
        gathered = lax.all_gather(dual.astype(jnp.bfloat16), "col", axis=0, tiled=True)
        pieces = gathered.reshape(n_col, tile_size, scn_count)[row_block]
        products = (
            jnp.einsum("bkt,bks->bts", block_mats, pieces, preferred_element_type=jnp.float32)
            * keep_mask
        )
        cols = jnp.zeros((n_blk, tile_size, scn_count), jnp.float32).at[col_block].add(products)
        kty = lax.psum_scatter(
            cols.reshape(n_blk * tile_size, scn_count).astype(jnp.bfloat16),
            "blk",
            scatter_dimension=0,
            tiled=True,
        ).astype(jnp.float32)
        x_new = project_box(primal - tau * (cost - kty), upper, bounded)
        xbar = (2.0 * x_new - primal).astype(jnp.bfloat16)
        whole = lax.all_gather(xbar, "blk", axis=0, tiled=True)
        primal = x_new
        row_pieces = whole.reshape(n_blk, tile_size, scn_count)[col_block]
        row_products = (
            jnp.einsum("bkt,bts->bks", block_mats, row_pieces, preferred_element_type=jnp.float32)
            * keep_mask
        )
        rows = jnp.zeros((n_col, tile_size, scn_count), jnp.float32).at[row_block].add(row_products)
        terms = rows.reshape(n_col * tile_size, scn_count)
        kx = lax.psum_scatter(
            terms.astype(jnp.bfloat16), "col", scatter_dimension=0, tiled=True
        ).astype(jnp.float32)
        dual = jnp.maximum(dual + sigma * (rhs - kx), 0.0)
    return (primal, dual)


def shards(*args):
    n_blk, n_col, n_rep = (lax.axis_size(axis) for axis in ("blk", "col", "rep"))
    blocks, cost = args[0], args[3]
    n, tile, nslots = n_blk * n_col, blocks.shape[-1], blocks.shape[2]
    fits = 2 * (n * tile) ** 2 <= MAX_MATRIX and cost.shape[1] % (16 * n) == 0 and cost.shape[1] == tile
    even = n_blk & (n_blk - 1) == 0 and n_col & (n_col - 1) == 0 and n_blk > 1 and n_rep == 2 and nslots % 2 == 0
    x, y = (local_plan if fits and even else collectives_plan)(*args)
    return x, y


def solution(mesh):
    in_specs = (
        P("blk", "col", None, None, None),
        P("blk", "col", None),
        P("blk", "col"),
        P(("blk", "col"), ("groups", "rep")),
        P(("blk", "col"), ("groups", "rep")),
        P(("blk", "col"), ("groups", "rep")),
        P(("blk", "col"), ("groups", "rep")),
        P(("blk", "col"), ("groups", "rep")),
        P(("groups", "rep")),
    )
    out_specs = (P(("blk", "col"), ("groups", "rep")), P(("blk", "col"), ("groups", "rep")))
    return jax.shard_map(shards, mesh=mesh, in_specs=in_specs, out_specs=out_specs, check_vma=False)
```

```python
import functools
import math

import jax
import jax.numpy as jnp
from jax import lax
from jax.experimental import pallas as pl
from jax.experimental.pallas import tpu as pltpu
from jax.sharding import PartitionSpec as P

ITERS = 2


ETA = 0.4
EPS = 1e-06
MAX_MATRIX = 8 * 1024 * 1024
PARTS = 3
FIELDS = 5
SLOT_ROW = 2 * PARTS

MIB = 1024 * 1024
VMEM = pl.BlockSpec(memory_space=pltpu.VMEM)
SMEM = pl.BlockSpec(memory_space=pltpu.SMEM)
ANY = pl.BlockSpec(memory_space=pl.ANY)
F32 = jnp.float32
BF16 = jnp.bfloat16


def held(shape, dtype):
    return pltpu.VMEM(shape, dtype)


def pinned(values):
    return [pltpu.with_memory_space_constraint(v, pltpu.HBM) for v in values]


def call(body, outs, in_specs, args, scratch=(), flops=0, limit=32):
    nbytes = sum(math.prod(a.shape) * jnp.dtype(a.dtype).itemsize for a in list(args) + list(outs))
    return pl.pallas_call(
        body,
        out_shape=list(outs),
        in_specs=in_specs,
        out_specs=[VMEM] * len(outs),
        scratch_shapes=list(scratch),
        compiler_params=pltpu.CompilerParams(vmem_limit_bytes=limit * MIB),
        cost_estimate=pl.CostEstimate(flops=flops, bytes_accessed=nbytes, transcendentals=0),
    )(*args)


def split_parts(values):
    high = values.astype(BF16).astype(F32)
    rest = values - high
    middle = rest.astype(BF16).astype(F32)
    low = (rest - middle).astype(BF16).astype(F32)
    return [high, middle, low]


def project(primal, grad, tau, upper, limited):
    value = primal - tau * grad
    capped = jnp.where(limited > 0, jnp.minimum(value, upper), value)
    return jnp.maximum(capped, 0.0)


def prep_body(n_col, far, near, *refs):
    live, *sources = refs[: FIELDS + 3]
    far_out, *near_outs, own_out = refs[FIELDS + 3 : FIELDS + 5 + len(near)]
    *fields, share, index, turned, sems = refs[FIELDS + 5 + len(near) :]
    half, tile = share.shape[0], share.shape[1]
    first = lax.axis_index("rep") * half
    targets = (*fields, index)
    copies = [
        pltpu.make_async_copy(source, target, sems.at[k])
        for k, (source, target) in enumerate(zip(sources[:-1], targets))
    ]
    copies.append(pltpu.make_async_copy(sources[-1].at[0, 0, pl.ds(first, half)], share, sems.at[FIELDS + 1]))
    for copy in copies:
        copy.start()
    part = own_out.shape[0] // (FIELDS + 1)
    nslots = index.shape[-1]
    rows = []
    for j, field in enumerate(fields):
        copies[j].wait()
        values = field[...]
        if j < 2:
            rows += split_parts(jnp.sum(values * values, axis=0, keepdims=True))
        turned[j] = values.T.astype(BF16)
    for copy in copies[FIELDS:]:
        copy.wait()
    lane = lax.broadcasted_iota(jnp.int32, (1, tile), 1)
    row = jnp.where(lane == nslots, live[0, 0].astype(F32), 0.0)
    for k in range(nslots):
        row = jnp.where(lane == k, index[0, 0, k].astype(F32), row)
    rows += [row, jnp.zeros((part - len(rows) - 1, tile), F32)]
    info = jnp.concatenate(rows, axis=0).astype(BF16)
    me_b, me_c = lax.axis_index("blk"), lax.axis_index("col")

    def piece(out, at, t, s):
        peer = pl.ds(pl.multiple_of(((me_b ^ t) * n_col + (me_c ^ s)) * part, part), part)
        for j in range(FIELDS):
            out[at + j * part : at + (j + 1) * part, :] = turned[j, peer, :]

    top = half * tile
    for out in (far_out, *near_outs):
        for k in range(half):
            out[k * tile : (k + 1) * tile, :] = share[k]
        out[out.shape[0] - part :, :] = info
    for m, (t, s) in enumerate([(0, 0), *near]):
        piece(far_out, top + m * FIELDS * part, far + t, s)
        if m > 0:
            piece(near_outs[m - 1], top, t, s)
    piece(own_out, 0, 0, 0)
    own_out[FIELDS * part :, :] = info


def relay_body(top, part, came, *outs):
    for m, out in enumerate(outs):
        out[0:top, :] = came[0:top, :]
        at = top + (m + 1) * FIELDS * part
        out[top : top + FIELDS * part, :] = came[at : at + FIELDS * part, :]
        out[top + FIELDS * part :, :] = came[came.shape[0] - part :, :]


def main_body(n_blk, n_col, shifts, part, slots, bounded, blocks, own, *refs):
    n = n_blk * n_col
    mine, theirs = refs[: n - 1], refs[n - 1 : 2 * (n - 1)]
    out, scales, mat, fields, turned = refs[2 * (n - 1) :]
    tile = blocks.shape[-1]
    nslots = blocks.shape[2]
    half = nslots // 2
    me_b, me_c, me_r = lax.axis_index("blk"), lax.axis_index("col"), lax.axis_index("rep")
    mat[...] = jnp.zeros(mat.shape, BF16)

    def place(source, t, s, slot, block):
        blk, col = me_b ^ t, me_c ^ s
        position = slots[source, slot]
        row = pl.multiple_of((blk * n_col + position // n_blk) * tile, tile)
        column = pl.multiple_of(((position % n_blk) * n_col + col) * tile, tile)

        @pl.when(slot < slots[source, nslots])
        def _():
            mat[pl.ds(row, tile), pl.ds(column, tile)] = block()

    sums = [jnp.zeros((1, tile), F32)] * 2

    def take(t, s, ref, at):
        lanes = pl.ds(pl.multiple_of(((me_b ^ t) * n_col + (me_c ^ s)) * tile, tile), tile)
        for j in range(FIELDS):
            fields[j, :, lanes] = ref[at + j * part : at + (j + 1) * part, :]
        info = ref[ref.shape[0] - part :, :].astype(F32)
        for j in range(2):
            first, second, third = (info[PARTS * j + k : PARTS * j + k + 1] for k in range(PARTS))
            sums[j] += (first + second) + third

    for k in range(nslots):
        place(0, 0, 0, k, lambda k=k: blocks[0, 0, k])
    take(0, 0, own, 0)
    for m, ((t, s), own_part, other_part) in enumerate(zip(shifts, mine, theirs)):
        for k in range(half):
            place(m + 1, t, s, me_r * half + k, lambda k=k, r=own_part: r[k * tile : (k + 1) * tile, :])
            place(m + 1, t, s, (1 - me_r) * half + k, lambda k=k, r=other_part: r[k * tile : (k + 1) * tile, :])
        take(t, s, own_part, half * tile)
    cost, rhs, upper, primal, dual = (fields[j].astype(F32) for j in range(FIELDS))
    weight = jnp.sqrt(sums[0] + EPS) / jnp.sqrt(sums[1] + EPS)
    rows = jnp.concatenate([ETA / weight, ETA * weight, bounded[...].astype(F32), jnp.zeros((5, tile), F32)], axis=0)
    scales[...] = rows
    turned[...] = jnp.concatenate([rows, jnp.zeros((tile - 8, tile), F32)], axis=0).T
    own = turned[pl.ds(pl.multiple_of((me_b * n_col + me_c) * part, part), part), :]
    tau, sigma, limited = own[:, 0:1], own[:, 1:2], own[:, 2:3]

    def store(j, values):
        values = values.astype(BF16)
        for d in range(n):
            out[d, j * part : (j + 1) * part, :] = values[:, d * tile : (d + 1) * tile]

    for step in range(ITERS):
        kty = jnp.dot(dual.astype(BF16), mat[...], preferred_element_type=F32)
        store(2 * step, kty)
        x_new = project(primal, cost - kty, tau, upper, limited)
        xbar = (2.0 * x_new - primal).astype(BF16)
        primal = x_new
        kx = lax.dot_general(xbar, mat[...], (((1,), (1,)), ((), ())), preferred_element_type=F32)
        store(2 * step + 1, kx)
        dual = jnp.maximum(dual + sigma * (rhs - kx), 0.0)


def final_body(recv, scales, cost, rhs, upper, x_in, y_in, bounded, x_out, y_out):
    n, rows, tile = recv.shape
    part = rows // (2 * ITERS)

    def turned(j):
        return recv[:, j * part : (j + 1) * part, :].reshape(n * part, tile).astype(F32).T

    tau, sigma = scales[0:1, :], scales[1:2, :]
    primal, dual = x_in[...], y_in[...]
    for step in range(ITERS):
        primal = project(primal, cost[...] - turned(2 * step), tau, upper[...], bounded[...])
        dual = jnp.maximum(dual + sigma * (rhs[...] - turned(2 * step + 1)), 0.0)
    x_out[...] = primal
    y_out[...] = dual


def local_plan(blocks, block_index, live, cost, rhs, upper, x_init, y_init, bounded):
    n_blk, n_col = lax.axis_size("blk"), lax.axis_size("col")
    n = n_blk * n_col
    tile, nslots = blocks.shape[-1], blocks.shape[2]
    scn = cost.shape[1]
    part = scn // n
    like = jax.ShapeDtypeStruct
    limits = bounded[None, :]

    def spread(value):
        return lax.all_to_all(value, ("blk", "col"), 0, 0, tiled=True)

    def move(value, t, s):
        pairs = [(b * n_col + c, (b ^ t) * n_col + (c ^ s)) for b in range(n_blk) for c in range(n_col)]
        return lax.ppermute(value, ("blk", "col"), pairs)

    far = n_blk // 2
    near = [(t, s) for t in range(far) for s in range(n_col) if (t, s) != (0, 0)]
    half = nslots // 2
    top = half * tile
    size = top + (FIELDS + 1) * part
    far_out, *near_outs, own = call(
        functools.partial(prep_body, n_col, far, near),
        [held((top + (FIELDS * (len(near) + 1) + 1) * part, tile), BF16)]
        + [held((size, tile), BF16)] * len(near)
        + [held(((FIELDS + 1) * part, tile), BF16)],
        [SMEM] + [ANY] * (FIELDS + 2),
        [live] + pinned([cost, rhs, upper, x_init, y_init, block_index, blocks]),
        scratch=[pltpu.VMEM((tile, scn), F32)] * FIELDS
        + [pltpu.VMEM((half, tile, tile), BF16)]
        + [pltpu.SMEM(block_index.shape, jnp.int32)]
        + [pltpu.VMEM((FIELDS, scn, tile), BF16), pltpu.SemaphoreType.DMA((FIELDS + 2,))],
    )
    mine = {(far, 0): move(far_out, far, 0)}
    for (t, s), out in zip(near, near_outs):
        mine[t, s] = move(out, t, s)
    relayed = call(
        functools.partial(relay_body, top, part),
        [held((size, tile), BF16)] * len(near),
        [VMEM],
        [mine[far, 0]],
    )
    for (t, s), out in zip(near, relayed):
        mine[far + t, s] = move(out, t, s)
    shifts = list(mine)
    theirs = [lax.ppermute(mine[shift], "rep", [(0, 1), (1, 0)]) for shift in shifts]
    rows = [v[v.shape[0] - part + SLOT_ROW, : nslots + 1] for v in [own] + list(mine.values())]
    slots = jnp.stack(rows).astype(jnp.int32)
    products, scales = call(
        functools.partial(main_body, n_blk, n_col, shifts, part),
        [like((n, 2 * ITERS * part, tile), BF16), like((8, scn), F32)],
        [SMEM] + [VMEM] * (2 * n + 1),
        [slots, limits, blocks, own] + [mine[shift] for shift in shifts] + theirs,
        scratch=[
            pltpu.VMEM((n * tile, n * tile), BF16),
            pltpu.VMEM((FIELDS, part, n * tile), BF16),
            pltpu.VMEM((tile, scn), F32),
        ],
        flops=4 * ITERS * n * n * tile * tile * part,
    )
    return call(
        final_body,
        [like((tile, scn), F32)] * 2,
        [VMEM] * (FIELDS + 3),
        [spread(products), scales, cost, rhs, upper, x_init, y_init, limits],
    )


def project_box(value, upper, bounded):
    capped = jnp.where(bounded[None, :] > 0, jnp.minimum(value, upper), value)
    return jnp.maximum(capped, 0.0)


def collectives_plan(blocks, block_index, live, cost, rhs, upper, x_init, y_init, bounded):
    block_mats = blocks[0, 0]
    slots = block_index[0, 0]
    n_blk = lax.axis_size("blk")
    n_col = lax.axis_size("col")
    tile_size = block_mats.shape[1]
    scn_count = cost.shape[1]
    row_block = slots // n_blk
    col_block = slots % n_blk
    keep_mask = (jnp.arange(slots.shape[0]) < live[0, 0]).astype(jnp.float32)[:, None, None]
    totals = lax.psum((jnp.sum(cost * cost, axis=0), jnp.sum(rhs * rhs, axis=0)), ("blk", "col"))
    weight = jnp.sqrt(totals[0] + EPS) / jnp.sqrt(totals[1] + EPS)
    tau = (ETA / weight)[None, :]
    sigma = (ETA * weight)[None, :]
    primal = x_init
    dual = y_init
    for step in range(ITERS):
        gathered = lax.all_gather(dual.astype(jnp.bfloat16), "col", axis=0, tiled=True)
        pieces = gathered.reshape(n_col, tile_size, scn_count)[row_block]
        products = (
            jnp.einsum("bkt,bks->bts", block_mats, pieces, preferred_element_type=jnp.float32)
            * keep_mask
        )
        cols = jnp.zeros((n_blk, tile_size, scn_count), jnp.float32).at[col_block].add(products)
        kty = lax.psum_scatter(
            cols.reshape(n_blk * tile_size, scn_count).astype(jnp.bfloat16),
            "blk",
            scatter_dimension=0,
            tiled=True,
        ).astype(jnp.float32)
        x_new = project_box(primal - tau * (cost - kty), upper, bounded)
        xbar = (2.0 * x_new - primal).astype(jnp.bfloat16)
        whole = lax.all_gather(xbar, "blk", axis=0, tiled=True)
        primal = x_new
        row_pieces = whole.reshape(n_blk, tile_size, scn_count)[col_block]
        row_products = (
            jnp.einsum("bkt,bts->bks", block_mats, row_pieces, preferred_element_type=jnp.float32)
            * keep_mask
        )
        rows = jnp.zeros((n_col, tile_size, scn_count), jnp.float32).at[row_block].add(row_products)
        terms = rows.reshape(n_col * tile_size, scn_count)
        kx = lax.psum_scatter(
            terms.astype(jnp.bfloat16), "col", scatter_dimension=0, tiled=True
        ).astype(jnp.float32)
        dual = jnp.maximum(dual + sigma * (rhs - kx), 0.0)
    return (primal, dual)


def shards(*args):
    n_blk, n_col, n_rep = (lax.axis_size(axis) for axis in ("blk", "col", "rep"))
    blocks, cost = args[0], args[3]
    n, tile, nslots = n_blk * n_col, blocks.shape[-1], blocks.shape[2]
    fits = 2 * (n * tile) ** 2 <= MAX_MATRIX and cost.shape[1] % (16 * n) == 0 and cost.shape[1] == tile
    even = n_blk & (n_blk - 1) == 0 and n_col & (n_col - 1) == 0 and n_blk > 1 and n_rep == 2 and nslots % 2 == 0
    x, y = (local_plan if fits and even else collectives_plan)(*args)
    return x, y


def solution(mesh):
    in_specs = (
        P("blk", "col", None, None, None),
        P("blk", "col", None),
        P("blk", "col"),
        P(("blk", "col"), ("groups", "rep")),
        P(("blk", "col"), ("groups", "rep")),
        P(("blk", "col"), ("groups", "rep")),
        P(("blk", "col"), ("groups", "rep")),
        P(("blk", "col"), ("groups", "rep")),
        P(("groups", "rep")),
    )
    out_specs = (P(("blk", "col"), ("groups", "rep")), P(("blk", "col"), ("groups", "rep")))
    return jax.shard_map(shards, mesh=mesh, in_specs=in_specs, out_specs=out_specs, check_vma=False)
```

```python
import functools
import math

import jax
import jax.numpy as jnp
from jax import lax
from jax.experimental import pallas as pl
from jax.experimental.pallas import tpu as pltpu
from jax.sharding import PartitionSpec as P

ITERS = 2


ETA = 0.4
EPS = 1e-06
MAX_MATRIX = 8 * 1024 * 1024
PARTS = 3
FIELDS = 5
SLOT_ROW = 2 * PARTS

MIB = 1024 * 1024
VMEM = pl.BlockSpec(memory_space=pltpu.VMEM)
SMEM = pl.BlockSpec(memory_space=pltpu.SMEM)
ANY = pl.BlockSpec(memory_space=pl.ANY)
F32 = jnp.float32
BF16 = jnp.bfloat16


def held(shape, dtype):
    return pltpu.VMEM(shape, dtype)


def pinned(values):
    return [pltpu.with_memory_space_constraint(v, pltpu.HBM) for v in values]


def call(body, outs, in_specs, args, scratch=(), flops=0, limit=32):
    nbytes = sum(math.prod(a.shape) * jnp.dtype(a.dtype).itemsize for a in list(args) + list(outs))
    return pl.pallas_call(
        body,
        out_shape=list(outs),
        in_specs=in_specs,
        out_specs=[VMEM] * len(outs),
        scratch_shapes=list(scratch),
        compiler_params=pltpu.CompilerParams(vmem_limit_bytes=limit * MIB),
        cost_estimate=pl.CostEstimate(flops=flops, bytes_accessed=nbytes, transcendentals=0),
    )(*args)


def split_parts(values):
    high = values.astype(BF16).astype(F32)
    rest = values - high
    middle = rest.astype(BF16).astype(F32)
    low = (rest - middle).astype(BF16).astype(F32)
    return [high, middle, low]


def project(primal, grad, tau, upper, limited):
    value = primal - tau * grad
    capped = jnp.where(limited > 0, jnp.minimum(value, upper), value)
    return jnp.maximum(capped, 0.0)


def prep_body(n_col, far, near, *refs):
    live, *sources = refs[: FIELDS + 3]
    far_share, far_out, *near_outs, own_out = refs[FIELDS + 3 : FIELDS + 6 + len(near)]
    *fields, share, index, turned, sems = refs[FIELDS + 6 + len(near) :]
    half, tile = share.shape[0], share.shape[1]
    first = lax.axis_index("rep") * half
    targets = (*fields, index)
    copies = [
        pltpu.make_async_copy(source, target, sems.at[k])
        for k, (source, target) in enumerate(zip(sources[:-1], targets))
    ]
    copies.append(pltpu.make_async_copy(sources[-1].at[0, 0, pl.ds(first, half)], share, sems.at[FIELDS + 1]))
    for copy in copies:
        copy.start()
    part = own_out.shape[0] // (FIELDS + 1)
    nslots = index.shape[-1]
    rows = []
    for j, field in enumerate(fields):
        copies[j].wait()
        values = field[...]
        if j < 2:
            rows += split_parts(jnp.sum(values * values, axis=0, keepdims=True))
        turned[j] = values.T.astype(BF16)
    for copy in copies[FIELDS:]:
        copy.wait()
    lane = lax.broadcasted_iota(jnp.int32, (1, tile), 1)
    row = jnp.where(lane == nslots, live[0, 0].astype(F32), 0.0)
    for k in range(nslots):
        row = jnp.where(lane == k, index[0, 0, k].astype(F32), row)
    rows += [row, jnp.zeros((part - len(rows) - 1, tile), F32)]
    info = jnp.concatenate(rows, axis=0).astype(BF16)
    me_b, me_c = lax.axis_index("blk"), lax.axis_index("col")

    def piece(out, at, t, s):
        peer = pl.ds(pl.multiple_of(((me_b ^ t) * n_col + (me_c ^ s)) * part, part), part)
        for j in range(FIELDS):
            out[at + j * part : at + (j + 1) * part, :] = turned[j, peer, :]

    top = half * tile
    for out in (far_share, *near_outs):
        for k in range(half):
            out[k * tile : (k + 1) * tile, :] = share[k]
    for m, (t, s) in enumerate([(0, 0), *near]):
        piece(far_out, m * FIELDS * part, far + t, s)
        if m > 0:
            piece(near_outs[m - 1], top, t, s)
    piece(own_out, 0, 0, 0)
    for out in (far_out, *near_outs, own_out):
        out[out.shape[0] - part :, :] = info


def relay_body(part, came, *outs):
    for m, out in enumerate(outs):
        at = (m + 1) * FIELDS * part
        out[0 : FIELDS * part, :] = came[at : at + FIELDS * part, :]
        out[FIELDS * part :, :] = came[came.shape[0] - part :, :]


def main_body(n_blk, n_col, shifts, part, slots, bounded, blocks, own, *refs):
    n = n_blk * n_col
    mine, theirs, pieces = refs[: n - 1], refs[n - 1 : 2 * (n - 1)], refs[2 * (n - 1) : 3 * (n - 1)]
    out, scales, mat, fields, turned = refs[3 * (n - 1) :]
    tile = blocks.shape[-1]
    nslots = blocks.shape[2]
    half = nslots // 2
    me_b, me_c, me_r = lax.axis_index("blk"), lax.axis_index("col"), lax.axis_index("rep")
    mat[...] = jnp.zeros(mat.shape, BF16)

    def place(source, t, s, slot, block):
        blk, col = me_b ^ t, me_c ^ s
        position = slots[source, slot]
        row = pl.multiple_of((blk * n_col + position // n_blk) * tile, tile)
        column = pl.multiple_of(((position % n_blk) * n_col + col) * tile, tile)

        @pl.when(slot < slots[source, nslots])
        def _():
            mat[pl.ds(row, tile), pl.ds(column, tile)] = block()

    sums = [jnp.zeros((1, tile), F32)] * 2

    def take(t, s, ref, at):
        lanes = pl.ds(pl.multiple_of(((me_b ^ t) * n_col + (me_c ^ s)) * tile, tile), tile)
        for j in range(FIELDS):
            fields[j, :, lanes] = ref[at + j * part : at + (j + 1) * part, :]
        info = ref[ref.shape[0] - part :, :].astype(F32)
        for j in range(2):
            first, second, third = (info[PARTS * j + k : PARTS * j + k + 1] for k in range(PARTS))
            sums[j] += (first + second) + third

    for k in range(nslots):
        place(0, 0, 0, k, lambda k=k: blocks[0, 0, k])
    take(0, 0, own, 0)
    for m, ((t, s), own_part, other_part, piece) in enumerate(zip(shifts, mine, theirs, pieces)):
        for k in range(half):
            place(m + 1, t, s, me_r * half + k, lambda k=k, r=own_part: r[k * tile : (k + 1) * tile, :])
            place(m + 1, t, s, (1 - me_r) * half + k, lambda k=k, r=other_part: r[k * tile : (k + 1) * tile, :])
        take(t, s, piece, half * tile if piece.shape[0] > half * tile else 0)
    cost, rhs, upper, primal, dual = (fields[j].astype(F32) for j in range(FIELDS))
    weight = jnp.sqrt(sums[0] + EPS) / jnp.sqrt(sums[1] + EPS)
    rows = jnp.concatenate([ETA / weight, ETA * weight, bounded[...].astype(F32), jnp.zeros((5, tile), F32)], axis=0)
    scales[...] = rows
    turned[...] = jnp.concatenate([rows, jnp.zeros((tile - 8, tile), F32)], axis=0).T
    own = turned[pl.ds(pl.multiple_of((me_b * n_col + me_c) * part, part), part), :]
    tau, sigma, limited = own[:, 0:1], own[:, 1:2], own[:, 2:3]

    def store(j, values):
        values = values.astype(BF16)
        for d in range(n):
            out[d, j * part : (j + 1) * part, :] = values[:, d * tile : (d + 1) * tile]

    for step in range(ITERS):
        kty = jnp.dot(dual.astype(BF16), mat[...], preferred_element_type=F32)
        store(2 * step, kty)
        x_new = project(primal, cost - kty, tau, upper, limited)
        xbar = (2.0 * x_new - primal).astype(BF16)
        primal = x_new
        kx = lax.dot_general(xbar, mat[...], (((1,), (1,)), ((), ())), preferred_element_type=F32)
        store(2 * step + 1, kx)
        dual = jnp.maximum(dual + sigma * (rhs - kx), 0.0)


def final_body(recv, scales, cost, rhs, upper, x_in, y_in, bounded, x_out, y_out):
    n, rows, tile = recv.shape
    part = rows // (2 * ITERS)

    def turned(j):
        return recv[:, j * part : (j + 1) * part, :].reshape(n * part, tile).astype(F32).T

    tau, sigma = scales[0:1, :], scales[1:2, :]
    primal, dual = x_in[...], y_in[...]
    for step in range(ITERS):
        primal = project(primal, cost[...] - turned(2 * step), tau, upper[...], bounded[...])
        dual = jnp.maximum(dual + sigma * (rhs[...] - turned(2 * step + 1)), 0.0)
    x_out[...] = primal
    y_out[...] = dual


def local_plan(blocks, block_index, live, cost, rhs, upper, x_init, y_init, bounded):
    n_blk, n_col = lax.axis_size("blk"), lax.axis_size("col")
    n = n_blk * n_col
    tile, nslots = blocks.shape[-1], blocks.shape[2]
    scn = cost.shape[1]
    part = scn // n
    like = jax.ShapeDtypeStruct
    limits = bounded[None, :]

    def spread(value):
        return lax.all_to_all(value, ("blk", "col"), 0, 0, tiled=True)

    def move(value, t, s):
        pairs = [(b * n_col + c, (b ^ t) * n_col + (c ^ s)) for b in range(n_blk) for c in range(n_col)]
        return lax.ppermute(value, ("blk", "col"), pairs)

    far = n_blk // 2
    near = [(t, s) for t in range(far) for s in range(n_col) if (t, s) != (0, 0)]
    half = nslots // 2
    top = half * tile
    size = top + (FIELDS + 1) * part
    far_share, far_out, *near_outs, own = call(
        functools.partial(prep_body, n_col, far, near),
        [held((top, tile), BF16), held(((FIELDS * (len(near) + 1) + 1) * part, tile), BF16)]
        + [held((size, tile), BF16)] * len(near)
        + [held((size - top, tile), BF16)],
        [SMEM] + [ANY] * (FIELDS + 2),
        [live] + pinned([cost, rhs, upper, x_init, y_init, block_index, blocks]),
        scratch=[pltpu.VMEM((tile, scn), F32)] * FIELDS
        + [pltpu.VMEM((half, tile, tile), BF16)]
        + [pltpu.SMEM(block_index.shape, jnp.int32)]
        + [pltpu.VMEM((FIELDS, scn, tile), BF16), pltpu.SemaphoreType.DMA((FIELDS + 2,))],
    )
    mine = {(far, 0): move(far_share, far, 0)}
    for (t, s), out in zip(near, near_outs):
        mine[t, s] = move(out, t, s)
    pieces = dict(mine)
    pieces[far, 0] = move(far_out, far, 0)
    for t, s in near:
        mine[far + t, s] = move(mine[far, 0], t, s)
    relayed = call(
        functools.partial(relay_body, part),
        [held((size - top, tile), BF16)] * len(near),
        [VMEM],
        [pieces[far, 0]],
    )
    for (t, s), out in zip(near, relayed):
        pieces[far + t, s] = move(out, t, s)
    shifts = list(mine)
    theirs = [lax.ppermute(mine[shift], "rep", [(0, 1), (1, 0)]) for shift in shifts]
    pieces = [pieces[shift] for shift in shifts]
    rows = [v[v.shape[0] - part + SLOT_ROW, : nslots + 1] for v in [own] + pieces]
    slots = jnp.stack(rows).astype(jnp.int32)
    products, scales = call(
        functools.partial(main_body, n_blk, n_col, shifts, part),
        [like((n, 2 * ITERS * part, tile), BF16), like((8, scn), F32)],
        [SMEM] + [VMEM] * (3 * n),
        [slots, limits, blocks, own] + [mine[shift] for shift in shifts] + theirs + pieces,
        scratch=[
            pltpu.VMEM((n * tile, n * tile), BF16),
            pltpu.VMEM((FIELDS, part, n * tile), BF16),
            pltpu.VMEM((tile, scn), F32),
        ],
        flops=4 * ITERS * n * n * tile * tile * part,
    )
    return call(
        final_body,
        [like((tile, scn), F32)] * 2,
        [VMEM] * (FIELDS + 3),
        [spread(products), scales, cost, rhs, upper, x_init, y_init, limits],
    )


def project_box(value, upper, bounded):
    capped = jnp.where(bounded[None, :] > 0, jnp.minimum(value, upper), value)
    return jnp.maximum(capped, 0.0)


def collectives_plan(blocks, block_index, live, cost, rhs, upper, x_init, y_init, bounded):
    block_mats = blocks[0, 0]
    slots = block_index[0, 0]
    n_blk = lax.axis_size("blk")
    n_col = lax.axis_size("col")
    tile_size = block_mats.shape[1]
    scn_count = cost.shape[1]
    row_block = slots // n_blk
    col_block = slots % n_blk
    keep_mask = (jnp.arange(slots.shape[0]) < live[0, 0]).astype(jnp.float32)[:, None, None]
    totals = lax.psum((jnp.sum(cost * cost, axis=0), jnp.sum(rhs * rhs, axis=0)), ("blk", "col"))
    weight = jnp.sqrt(totals[0] + EPS) / jnp.sqrt(totals[1] + EPS)
    tau = (ETA / weight)[None, :]
    sigma = (ETA * weight)[None, :]
    primal = x_init
    dual = y_init
    for step in range(ITERS):
        gathered = lax.all_gather(dual.astype(jnp.bfloat16), "col", axis=0, tiled=True)
        pieces = gathered.reshape(n_col, tile_size, scn_count)[row_block]
        products = (
            jnp.einsum("bkt,bks->bts", block_mats, pieces, preferred_element_type=jnp.float32)
            * keep_mask
        )
        cols = jnp.zeros((n_blk, tile_size, scn_count), jnp.float32).at[col_block].add(products)
        kty = lax.psum_scatter(
            cols.reshape(n_blk * tile_size, scn_count).astype(jnp.bfloat16),
            "blk",
            scatter_dimension=0,
            tiled=True,
        ).astype(jnp.float32)
        x_new = project_box(primal - tau * (cost - kty), upper, bounded)
        xbar = (2.0 * x_new - primal).astype(jnp.bfloat16)
        whole = lax.all_gather(xbar, "blk", axis=0, tiled=True)
        primal = x_new
        row_pieces = whole.reshape(n_blk, tile_size, scn_count)[col_block]
        row_products = (
            jnp.einsum("bkt,bts->bks", block_mats, row_pieces, preferred_element_type=jnp.float32)
            * keep_mask
        )
        rows = jnp.zeros((n_col, tile_size, scn_count), jnp.float32).at[row_block].add(row_products)
        terms = rows.reshape(n_col * tile_size, scn_count)
        kx = lax.psum_scatter(
            terms.astype(jnp.bfloat16), "col", scatter_dimension=0, tiled=True
        ).astype(jnp.float32)
        dual = jnp.maximum(dual + sigma * (rhs - kx), 0.0)
    return (primal, dual)


def shards(*args):
    n_blk, n_col, n_rep = (lax.axis_size(axis) for axis in ("blk", "col", "rep"))
    blocks, cost = args[0], args[3]
    n, tile, nslots = n_blk * n_col, blocks.shape[-1], blocks.shape[2]
    fits = 2 * (n * tile) ** 2 <= MAX_MATRIX and cost.shape[1] % (16 * n) == 0 and cost.shape[1] == tile
    even = n_blk & (n_blk - 1) == 0 and n_col & (n_col - 1) == 0 and n_blk > 1 and n_rep == 2 and nslots % 2 == 0
    x, y = (local_plan if fits and even else collectives_plan)(*args)
    return x, y


def solution(mesh):
    in_specs = (
        P("blk", "col", None, None, None),
        P("blk", "col", None),
        P("blk", "col"),
        P(("blk", "col"), ("groups", "rep")),
        P(("blk", "col"), ("groups", "rep")),
        P(("blk", "col"), ("groups", "rep")),
        P(("blk", "col"), ("groups", "rep")),
        P(("blk", "col"), ("groups", "rep")),
        P(("groups", "rep")),
    )
    out_specs = (P(("blk", "col"), ("groups", "rep")), P(("blk", "col"), ("groups", "rep")))
    return jax.shard_map(shards, mesh=mesh, in_specs=in_specs, out_specs=out_specs, check_vma=False)
```

```python
import functools
import math

import jax
import jax.numpy as jnp
from jax import lax
from jax.experimental import pallas as pl
from jax.experimental.pallas import tpu as pltpu
from jax.sharding import PartitionSpec as P

ITERS = 2


ETA = 0.4
EPS = 1e-06
MAX_MATRIX = 8 * 1024 * 1024
PARTS = 3
FIELDS = 5
SLOT_ROW = 2 * PARTS

MIB = 1024 * 1024
VMEM = pl.BlockSpec(memory_space=pltpu.VMEM)
SMEM = pl.BlockSpec(memory_space=pltpu.SMEM)
ANY = pl.BlockSpec(memory_space=pl.ANY)
F32 = jnp.float32
BF16 = jnp.bfloat16


def held(shape, dtype):
    return pltpu.VMEM(shape, dtype)


def pinned(values):
    return [pltpu.with_memory_space_constraint(v, pltpu.HBM) for v in values]


def call(body, outs, in_specs, args, scratch=(), flops=0, limit=32, aliases=None):
    nbytes = sum(math.prod(a.shape) * jnp.dtype(a.dtype).itemsize for a in list(args) + list(outs))
    return pl.pallas_call(
        body,
        out_shape=list(outs),
        in_specs=in_specs,
        out_specs=[VMEM] * len(outs),
        scratch_shapes=list(scratch),
        input_output_aliases=aliases or {},
        compiler_params=pltpu.CompilerParams(vmem_limit_bytes=limit * MIB),
        cost_estimate=pl.CostEstimate(flops=flops, bytes_accessed=nbytes, transcendentals=0),
    )(*args)


def split_parts(values):
    high = values.astype(BF16).astype(F32)
    rest = values - high
    middle = rest.astype(BF16).astype(F32)
    low = (rest - middle).astype(BF16).astype(F32)
    return [high, middle, low]


def project(primal, grad, tau, upper, limited):
    value = primal - tau * grad
    capped = jnp.where(limited > 0, jnp.minimum(value, upper), value)
    return jnp.maximum(capped, 0.0)


def prep_body(n_col, far, near, first_near, *refs):
    live, *sources = refs[: FIELDS + 3]
    far_out, *near_outs, own_out = refs[FIELDS + 3 : FIELDS + 5 + len(first_near)]
    *fields, share, index, turned, sems = refs[FIELDS + 5 + len(first_near) :]
    half, tile = share.shape[0], share.shape[1]
    first = lax.axis_index("rep") * half
    targets = (*fields, index)
    copies = [
        pltpu.make_async_copy(source, target, sems.at[k])
        for k, (source, target) in enumerate(zip(sources[:-1], targets))
    ]
    copies.append(pltpu.make_async_copy(sources[-1].at[0, 0, pl.ds(first, half)], share, sems.at[FIELDS + 1]))
    for copy in copies:
        copy.start()
    part = own_out.shape[0] // (FIELDS + 1)
    nslots = index.shape[-1]
    rows = []
    for j, field in enumerate(fields):
        copies[j].wait()
        values = field[...]
        if j < 2:
            rows += split_parts(jnp.sum(values * values, axis=0, keepdims=True))
        turned[j] = values.T.astype(BF16)
    for copy in copies[FIELDS:]:
        copy.wait()
    lane = lax.broadcasted_iota(jnp.int32, (1, tile), 1)
    row = jnp.where(lane == nslots, live[0, 0].astype(F32), 0.0)
    for k in range(nslots):
        row = jnp.where(lane == k, index[0, 0, k].astype(F32), row)
    rows += [row, jnp.zeros((part - len(rows) - 1, tile), F32)]
    info = jnp.concatenate(rows, axis=0).astype(BF16)
    me_b, me_c = lax.axis_index("blk"), lax.axis_index("col")

    def piece(out, at, t, s):
        peer = pl.ds(pl.multiple_of(((me_b ^ t) * n_col + (me_c ^ s)) * part, part), part)
        for j in range(FIELDS):
            out[at + j * part : at + (j + 1) * part, :] = turned[j, peer, :]

    top = half * tile
    for out in (far_out, *near_outs):
        for k in range(half):
            out[k * tile : (k + 1) * tile, :] = share[k]
        out[out.shape[0] - part :, :] = info
    for m, (t, s) in enumerate([(0, 0), *near]):
        piece(far_out, top + m * FIELDS * part, far + t, s)
    for out, (t, s) in zip(near_outs, first_near):
        for m in range(1 if t == 0 else n_col):
            piece(out, top + m * FIELDS * part, t, s ^ m)
    piece(own_out, 0, 0, 0)
    own_out[FIELDS * part :, :] = info


def relay_body(top, part, came, *outs):
    for m, out in enumerate(outs):
        out[0:top, :] = came[0:top, :]
        at = top + (m + 1) * FIELDS * part
        out[top : top + FIELDS * part, :] = came[at : at + FIELDS * part, :]
        out[top + FIELDS * part :, :] = came[came.shape[0] - part :, :]


def place(n_blk, n_col, mat, slots, source, shift, slot, block, nslots):
    tile = block.shape[-1]
    blk, col = lax.axis_index("blk") ^ shift[0], lax.axis_index("col") ^ shift[1]
    position = slots[source, slot]
    row = pl.multiple_of((blk * n_col + position // n_blk) * tile, tile)
    column = pl.multiple_of(((position % n_blk) * n_col + col) * tile, tile)

    @pl.when(slot < slots[source, nslots])
    def _():
        mat[pl.ds(row, tile), pl.ds(column, tile)] = block[...]


def place_shares(n_blk, n_col, mat, slots, source, shift, own_part, other_part, nslots):
    half = nslots // 2
    tile = own_part.shape[1]
    core = lax.axis_index("rep")
    for part, which in ((own_part, core), (other_part, 1 - core)):
        for k in range(half):
            block = part.at[k * tile : (k + 1) * tile, :]
            place(n_blk, n_col, mat, slots, source, shift, which * half + k, block, nslots)


def take(n_col, fields, shift, ref, at):
    part, tile = fields.shape[1], ref.shape[1]
    blk, col = lax.axis_index("blk") ^ shift[0], lax.axis_index("col") ^ shift[1]
    lanes = pl.ds(pl.multiple_of((blk * n_col + col) * tile, tile), tile)
    for j in range(FIELDS):
        fields[j, :, lanes] = ref[at + j * part : at + (j + 1) * part, :]
    info = ref[ref.shape[0] - part :, :].astype(F32)
    sums = []
    for j in range(2):
        first, second, third = (info[PARTS * j + k : PARTS * j + k + 1] for k in range(PARTS))
        sums.append((first + second) + third)
    return sums


def early_body(n_blk, n_col, shifts, slots, blocks_in, own, *refs):
    count = len(shifts)
    mine, theirs = refs[:count], refs[count : 2 * count]
    mat, fields, sums_out, blocks, sem = refs[2 * count :]
    copy = pltpu.make_async_copy(blocks_in, blocks, sem)
    copy.start()
    nslots = blocks.shape[2]
    mat[...] = jnp.zeros(mat.shape, BF16)
    fields[...] = jnp.zeros(fields.shape, BF16)
    sums = take(n_col, fields, (0, 0), own, 0)
    for m, (shift, own_part, other_part) in enumerate(zip(shifts, mine, theirs)):
        place_shares(n_blk, n_col, mat, slots, m + 1, shift, own_part, other_part, nslots)
        more = take(n_col, fields, shift, own_part, nslots // 2 * own_part.shape[1])
        sums = [a + b for a, b in zip(sums, more)]
    copy.wait()
    for k in range(nslots):
        place(n_blk, n_col, mat, slots, 0, (0, 0), k, blocks.at[0, 0, k], nslots)
    sums_out[...] = jnp.concatenate(sums + [jnp.zeros((6, own.shape[1]), F32)], axis=0)


def main_body(n_blk, n_col, shifts, nslots, slots, bounded, mat, fields, sums_in, *refs):
    n = n_blk * n_col
    count = len(shifts)
    mine, theirs = refs[:count], refs[count : 2 * count]
    out, scales, _, _, turned = refs[2 * count :]
    part, tile = fields.shape[1], mine[0].shape[1]
    me_b, me_c = lax.axis_index("blk"), lax.axis_index("col")
    sums = [sums_in[0:1, :], sums_in[1:2, :]]
    for m, (shift, own_part, other_part) in enumerate(zip(shifts, mine, theirs)):
        place_shares(n_blk, n_col, mat, slots, m, shift, own_part, other_part, nslots)
        more = take(n_col, fields, shift, own_part, nslots // 2 * tile)
        sums = [a + b for a, b in zip(sums, more)]
    cost, rhs, upper, primal, dual = (fields[j].astype(F32) for j in range(FIELDS))
    weight = jnp.sqrt(sums[0] + EPS) / jnp.sqrt(sums[1] + EPS)
    rows = jnp.concatenate([ETA / weight, ETA * weight, bounded[...].astype(F32), jnp.zeros((5, tile), F32)], axis=0)
    scales[...] = rows
    turned[...] = jnp.concatenate([rows, jnp.zeros((tile - 8, tile), F32)], axis=0).T
    own = turned[pl.ds(pl.multiple_of((me_b * n_col + me_c) * part, part), part), :]
    tau, sigma, limited = own[:, 0:1], own[:, 1:2], own[:, 2:3]

    def store(j, values):
        values = values.astype(BF16)
        for d in range(n):
            out[d, j * part : (j + 1) * part, :] = values[:, d * tile : (d + 1) * tile]

    for step in range(ITERS):
        kty = jnp.dot(dual.astype(BF16), mat[...], preferred_element_type=F32)
        store(2 * step, kty)
        x_new = project(primal, cost - kty, tau, upper, limited)
        xbar = (2.0 * x_new - primal).astype(BF16)
        primal = x_new
        kx = lax.dot_general(xbar, mat[...], (((1,), (1,)), ((), ())), preferred_element_type=F32)
        store(2 * step + 1, kx)
        dual = jnp.maximum(dual + sigma * (rhs - kx), 0.0)


def final_body(recv, scales, cost, rhs, upper, x_in, y_in, bounded, x_out, y_out):
    n, rows, tile = recv.shape
    part = rows // (2 * ITERS)

    def turned(j):
        return recv[:, j * part : (j + 1) * part, :].reshape(n * part, tile).astype(F32).T

    tau, sigma = scales[0:1, :], scales[1:2, :]
    primal, dual = x_in[...], y_in[...]
    for step in range(ITERS):
        primal = project(primal, cost[...] - turned(2 * step), tau, upper[...], bounded[...])
        dual = jnp.maximum(dual + sigma * (rhs[...] - turned(2 * step + 1)), 0.0)
    x_out[...] = primal
    y_out[...] = dual


def local_plan(blocks, block_index, live, cost, rhs, upper, x_init, y_init, bounded):
    n_blk, n_col = lax.axis_size("blk"), lax.axis_size("col")
    n = n_blk * n_col
    tile, nslots = blocks.shape[-1], blocks.shape[2]
    scn = cost.shape[1]
    part = scn // n
    like = jax.ShapeDtypeStruct
    limits = bounded[None, :]

    def spread(value):
        return lax.all_to_all(value, ("blk", "col"), 0, 0, tiled=True)

    def move(value, t, s):
        pairs = [(b * n_col + c, (b ^ t) * n_col + (c ^ s)) for b in range(n_blk) for c in range(n_col)]
        return lax.ppermute(value, ("blk", "col"), pairs)

    far = n_blk // 2
    near = [(t, s) for t in range(far) for s in range(n_col) if (t, s) != (0, 0)]
    half = nslots // 2
    top = half * tile
    size = top + (FIELDS + 1) * part
    first_near = [(0, s) for s in range(1, n_col)] + [(t, 0) for t in range(1, far)]
    far_out, *near_outs, own = call(
        functools.partial(prep_body, n_col, far, near, first_near),
        [held((top + (FIELDS * (len(near) + 1) + 1) * part, tile), BF16)]
        + [held((size + (n_col - 1) * FIELDS * part * (t > 0), tile), BF16) for t, s in first_near]
        + [held(((FIELDS + 1) * part, tile), BF16)],
        [SMEM] + [ANY] * (FIELDS + 2),
        [live] + pinned([cost, rhs, upper, x_init, y_init, block_index, blocks]),
        scratch=[pltpu.VMEM((tile, scn), F32)] * FIELDS
        + [pltpu.VMEM((half, tile, tile), BF16)]
        + [pltpu.SMEM(block_index.shape, jnp.int32)]
        + [pltpu.VMEM((FIELDS, scn, tile), BF16), pltpu.SemaphoreType.DMA((FIELDS + 2,))],
    )

    def relay(came, count):
        return call(functools.partial(relay_body, top, part), [held((size, tile), BF16)] * count, [VMEM], [came])

    def other_core(values):
        return [lax.ppermute(v, "rep", [(0, 1), (1, 0)]) for v in values]

    def slots_of(values):
        rows = [v[v.shape[0] - part + SLOT_ROW, : nslots + 1] for v in values]
        return jnp.stack(rows).astype(jnp.int32)

    early = {(far, 0): move(far_out, far, 0)}
    for (t, s), out in zip(first_near, near_outs):
        early[t, s] = move(out, t, s)
    for t in range(1, far):
        for s, out in zip(range(1, n_col), relay(early[t, 0], n_col - 1)):
            early[t, s] = move(out, 0, s)
    late = {}
    for (t, s), out in zip(near, relay(early[far, 0], len(near))):
        late[far + t, s] = move(out, t, s)
    shifts, mine = list(early), list(early.values())
    mat, fields, sums = call(
        functools.partial(early_body, n_blk, n_col, shifts),
        [held((n * tile, n * tile), BF16), held((FIELDS, part, n * tile), BF16), held((8, scn), F32)],
        [SMEM, ANY] + [VMEM] * (1 + 2 * len(mine)),
        [slots_of([own] + mine), *pinned([blocks]), own] + mine + other_core(mine),
        scratch=[pltpu.VMEM(blocks.shape, BF16), pltpu.SemaphoreType.DMA],
    )
    shifts, mine = list(late), list(late.values())
    products, scales, _, _ = call(
        functools.partial(main_body, n_blk, n_col, shifts, nslots),
        [like((n, 2 * ITERS * part, tile), BF16), like((8, scn), F32)]
        + [held(mat.shape, BF16), held(fields.shape, BF16)],
        [SMEM] + [VMEM] * (4 + 2 * len(mine)),
        [slots_of(mine), limits, mat, fields, sums] + mine + other_core(mine),
        scratch=[pltpu.VMEM((tile, scn), F32)],
        flops=4 * ITERS * n * n * tile * tile * part,
        aliases={2: 2, 3: 3},
    )
    return call(
        final_body,
        [like((tile, scn), F32)] * 2,
        [VMEM] * (FIELDS + 3),
        [spread(products), scales, cost, rhs, upper, x_init, y_init, limits],
    )


def project_box(value, upper, bounded):
    capped = jnp.where(bounded[None, :] > 0, jnp.minimum(value, upper), value)
    return jnp.maximum(capped, 0.0)


def collectives_plan(blocks, block_index, live, cost, rhs, upper, x_init, y_init, bounded):
    block_mats = blocks[0, 0]
    slots = block_index[0, 0]
    n_blk = lax.axis_size("blk")
    n_col = lax.axis_size("col")
    tile_size = block_mats.shape[1]
    scn_count = cost.shape[1]
    row_block = slots // n_blk
    col_block = slots % n_blk
    keep_mask = (jnp.arange(slots.shape[0]) < live[0, 0]).astype(jnp.float32)[:, None, None]
    totals = lax.psum((jnp.sum(cost * cost, axis=0), jnp.sum(rhs * rhs, axis=0)), ("blk", "col"))
    weight = jnp.sqrt(totals[0] + EPS) / jnp.sqrt(totals[1] + EPS)
    tau = (ETA / weight)[None, :]
    sigma = (ETA * weight)[None, :]
    primal = x_init
    dual = y_init
    for step in range(ITERS):
        gathered = lax.all_gather(dual.astype(jnp.bfloat16), "col", axis=0, tiled=True)
        pieces = gathered.reshape(n_col, tile_size, scn_count)[row_block]
        products = (
            jnp.einsum("bkt,bks->bts", block_mats, pieces, preferred_element_type=jnp.float32)
            * keep_mask
        )
        cols = jnp.zeros((n_blk, tile_size, scn_count), jnp.float32).at[col_block].add(products)
        kty = lax.psum_scatter(
            cols.reshape(n_blk * tile_size, scn_count).astype(jnp.bfloat16),
            "blk",
            scatter_dimension=0,
            tiled=True,
        ).astype(jnp.float32)
        x_new = project_box(primal - tau * (cost - kty), upper, bounded)
        xbar = (2.0 * x_new - primal).astype(jnp.bfloat16)
        whole = lax.all_gather(xbar, "blk", axis=0, tiled=True)
        primal = x_new
        row_pieces = whole.reshape(n_blk, tile_size, scn_count)[col_block]
        row_products = (
            jnp.einsum("bkt,bts->bks", block_mats, row_pieces, preferred_element_type=jnp.float32)
            * keep_mask
        )
        rows = jnp.zeros((n_col, tile_size, scn_count), jnp.float32).at[row_block].add(row_products)
        terms = rows.reshape(n_col * tile_size, scn_count)
        kx = lax.psum_scatter(
            terms.astype(jnp.bfloat16), "col", scatter_dimension=0, tiled=True
        ).astype(jnp.float32)
        dual = jnp.maximum(dual + sigma * (rhs - kx), 0.0)
    return (primal, dual)


def shards(*args):
    n_blk, n_col, n_rep = (lax.axis_size(axis) for axis in ("blk", "col", "rep"))
    blocks, cost = args[0], args[3]
    n, tile, nslots = n_blk * n_col, blocks.shape[-1], blocks.shape[2]
    fits = 2 * (n * tile) ** 2 <= MAX_MATRIX and cost.shape[1] % (16 * n) == 0 and cost.shape[1] == tile
    even = n_blk & (n_blk - 1) == 0 and n_col & (n_col - 1) == 0 and n_blk > 1 and n_rep == 2 and nslots % 2 == 0
    x, y = (local_plan if fits and even else collectives_plan)(*args)
    return x, y


def solution(mesh):
    in_specs = (
        P("blk", "col", None, None, None),
        P("blk", "col", None),
        P("blk", "col"),
        P(("blk", "col"), ("groups", "rep")),
        P(("blk", "col"), ("groups", "rep")),
        P(("blk", "col"), ("groups", "rep")),
        P(("blk", "col"), ("groups", "rep")),
        P(("blk", "col"), ("groups", "rep")),
        P(("groups", "rep")),
    )
    out_specs = (P(("blk", "col"), ("groups", "rep")), P(("blk", "col"), ("groups", "rep")))
    return jax.shard_map(shards, mesh=mesh, in_specs=in_specs, out_specs=out_specs, check_vma=False)
```

```python
import functools
import math

import jax
import jax.numpy as jnp
from jax import lax
from jax.experimental import pallas as pl
from jax.experimental.pallas import tpu as pltpu
from jax.sharding import PartitionSpec as P

ITERS = 2


ETA = 0.4
EPS = 1e-06
MAX_MATRIX = 8 * 1024 * 1024
PARTS = 3
FIELDS = 5
SLOT_ROW = 2 * PARTS

MIB = 1024 * 1024
VMEM = pl.BlockSpec(memory_space=pltpu.VMEM)
SMEM = pl.BlockSpec(memory_space=pltpu.SMEM)
ANY = pl.BlockSpec(memory_space=pl.ANY)
F32 = jnp.float32
BF16 = jnp.bfloat16


def held(shape, dtype):
    return pltpu.VMEM(shape, dtype)


def pinned(values):
    return [pltpu.with_memory_space_constraint(v, pltpu.HBM) for v in values]


def call(body, outs, in_specs, args, scratch=(), flops=0, limit=32, aliases=None, spec=VMEM):
    nbytes = sum(math.prod(a.shape) * jnp.dtype(a.dtype).itemsize for a in list(args) + list(outs))
    return pl.pallas_call(
        body,
        out_shape=list(outs),
        in_specs=in_specs,
        out_specs=[spec] * len(outs),
        scratch_shapes=list(scratch),
        input_output_aliases=aliases or {},
        compiler_params=pltpu.CompilerParams(vmem_limit_bytes=limit * MIB),
        cost_estimate=pl.CostEstimate(flops=flops, bytes_accessed=nbytes, transcendentals=0),
    )(*args)


def split_parts(values):
    high = values.astype(BF16).astype(F32)
    rest = values - high
    middle = rest.astype(BF16).astype(F32)
    low = (rest - middle).astype(BF16).astype(F32)
    return [high, middle, low]


def project(primal, grad, tau, upper, limited):
    value = primal - tau * grad
    capped = jnp.where(limited > 0, jnp.minimum(value, upper), value)
    return jnp.maximum(capped, 0.0)


def prep_body(n_col, far, near, first_near, *refs):
    live, *sources = refs[: FIELDS + 3]
    far_out, *near_outs, own_out = refs[FIELDS + 3 : FIELDS + 5 + len(first_near)]
    *fields, share, index, turned, sems = refs[FIELDS + 5 + len(first_near) :]
    half, tile = share.shape[0], share.shape[1]
    first = lax.axis_index("rep") * half
    targets = (*fields, index)
    copies = [
        pltpu.make_async_copy(source, target, sems.at[k])
        for k, (source, target) in enumerate(zip(sources[:-1], targets))
    ]
    copies.append(pltpu.make_async_copy(sources[-1].at[0, 0, pl.ds(first, half)], share, sems.at[FIELDS + 1]))
    for copy in copies:
        copy.start()
    part = own_out.shape[0] // (FIELDS + 1)
    nslots = index.shape[-1]
    rows = []
    for j, field in enumerate(fields):
        copies[j].wait()
        values = field[...]
        if j < 2:
            rows += split_parts(jnp.sum(values * values, axis=0, keepdims=True))
        turned[j] = values.T.astype(BF16)
    for copy in copies[FIELDS:]:
        copy.wait()
    lane = lax.broadcasted_iota(jnp.int32, (1, tile), 1)
    row = jnp.where(lane == nslots, live[0, 0].astype(F32), 0.0)
    for k in range(nslots):
        row = jnp.where(lane == k, index[0, 0, k].astype(F32), row)
    rows += [row, jnp.zeros((part - len(rows) - 1, tile), F32)]
    info = jnp.concatenate(rows, axis=0).astype(BF16)
    me_b, me_c = lax.axis_index("blk"), lax.axis_index("col")

    def piece(out, at, t, s):
        peer = pl.ds(pl.multiple_of(((me_b ^ t) * n_col + (me_c ^ s)) * part, part), part)
        for j in range(FIELDS):
            out[at + j * part : at + (j + 1) * part, :] = turned[j, peer, :]

    top = half * tile
    for out in (far_out, *near_outs):
        for k in range(half):
            out[k * tile : (k + 1) * tile, :] = share[k]
        out[out.shape[0] - part :, :] = info
    for m, (t, s) in enumerate([(0, 0), *near]):
        piece(far_out, top + m * FIELDS * part, far + t, s)
    for out, (t, s) in zip(near_outs, first_near):
        for m in range(1 if t == 0 else n_col):
            piece(out, top + m * FIELDS * part, t, s ^ m)
    piece(own_out, 0, 0, 0)
    own_out[FIELDS * part :, :] = info


def touch_body(part, after, out):
    del part, after, out


def relay_body(top, part, came, *outs):
    for m, out in enumerate(outs):
        out[0:top, :] = came[0:top, :]
        at = top + (m + 1) * FIELDS * part
        out[top : top + FIELDS * part, :] = came[at : at + FIELDS * part, :]
        out[top + FIELDS * part :, :] = came[came.shape[0] - part :, :]


def place(n_blk, n_col, mat, slots, source, shift, slot, block, nslots):
    tile = block.shape[-1]
    blk, col = lax.axis_index("blk") ^ shift[0], lax.axis_index("col") ^ shift[1]
    position = slots[source, slot]
    row = pl.multiple_of((blk * n_col + position // n_blk) * tile, tile)
    column = pl.multiple_of(((position % n_blk) * n_col + col) * tile, tile)

    @pl.when(slot < slots[source, nslots])
    def _():
        mat[pl.ds(row, tile), pl.ds(column, tile)] = block[...]


def place_shares(n_blk, n_col, mat, slots, source, shift, own_part, other_part, nslots):
    half = nslots // 2
    tile = own_part.shape[1]
    core = lax.axis_index("rep")
    for part, which in ((own_part, core), (other_part, 1 - core)):
        for k in range(half):
            block = part.at[k * tile : (k + 1) * tile, :]
            place(n_blk, n_col, mat, slots, source, shift, which * half + k, block, nslots)


def take(n_col, fields, shift, ref, at):
    part, tile = fields.shape[1], ref.shape[1]
    blk, col = lax.axis_index("blk") ^ shift[0], lax.axis_index("col") ^ shift[1]
    lanes = pl.ds(pl.multiple_of((blk * n_col + col) * tile, tile), tile)
    for j in range(FIELDS):
        fields[j, :, lanes] = ref[at + j * part : at + (j + 1) * part, :]
    info = ref[ref.shape[0] - part :, :].astype(F32)
    sums = []
    for j in range(2):
        first, second, third = (info[PARTS * j + k : PARTS * j + k + 1] for k in range(PARTS))
        sums.append((first + second) + third)
    return sums


def early_body(n_blk, n_col, shifts, slots, blocks_in, own, *refs):
    count = len(shifts)
    mine, theirs = refs[:count], refs[count : 2 * count]
    mat, fields, sums_out, blocks, sem = refs[2 * count :]
    copy = pltpu.make_async_copy(blocks_in, blocks, sem)
    copy.start()
    nslots = blocks.shape[2]
    mat[...] = jnp.zeros(mat.shape, BF16)
    fields[...] = jnp.zeros(fields.shape, BF16)
    sums = take(n_col, fields, (0, 0), own, 0)
    for m, (shift, own_part, other_part) in enumerate(zip(shifts, mine, theirs)):
        place_shares(n_blk, n_col, mat, slots, m + 1, shift, own_part, other_part, nslots)
        more = take(n_col, fields, shift, own_part, nslots // 2 * own_part.shape[1])
        sums = [a + b for a, b in zip(sums, more)]
    copy.wait()
    for k in range(nslots):
        place(n_blk, n_col, mat, slots, 0, (0, 0), k, blocks.at[0, 0, k], nslots)
    sums_out[...] = jnp.concatenate(sums + [jnp.zeros((6, own.shape[1]), F32)], axis=0)


def main_body(n_blk, n_col, shifts, nslots, slots, bounded, mat, fields, sums_in, *refs):
    n = n_blk * n_col
    count = len(shifts)
    mine, theirs = refs[:count], refs[count : 2 * count]
    out, scales, _, _, turned = refs[2 * count :]
    part, tile = fields.shape[1], mine[0].shape[1]
    me_b, me_c = lax.axis_index("blk"), lax.axis_index("col")
    sums = [sums_in[0:1, :], sums_in[1:2, :]]
    for m, (shift, own_part, other_part) in enumerate(zip(shifts, mine, theirs)):
        place_shares(n_blk, n_col, mat, slots, m, shift, own_part, other_part, nslots)
        more = take(n_col, fields, shift, own_part, nslots // 2 * tile)
        sums = [a + b for a, b in zip(sums, more)]
    cost, rhs, upper, primal, dual = (fields[j].astype(F32) for j in range(FIELDS))
    weight = jnp.sqrt(sums[0] + EPS) / jnp.sqrt(sums[1] + EPS)
    rows = jnp.concatenate([ETA / weight, ETA * weight, bounded[...].astype(F32), jnp.zeros((5, tile), F32)], axis=0)
    scales[...] = rows
    turned[...] = jnp.concatenate([rows, jnp.zeros((tile - 8, tile), F32)], axis=0).T
    own = turned[pl.ds(pl.multiple_of((me_b * n_col + me_c) * part, part), part), :]
    tau, sigma, limited = own[:, 0:1], own[:, 1:2], own[:, 2:3]

    def store(j, values):
        values = values.astype(BF16)
        for d in range(n):
            out[d, j * part : (j + 1) * part, :] = values[:, d * tile : (d + 1) * tile]

    for step in range(ITERS):
        kty = jnp.dot(dual.astype(BF16), mat[...], preferred_element_type=F32)
        store(2 * step, kty)
        x_new = project(primal, cost - kty, tau, upper, limited)
        xbar = (2.0 * x_new - primal).astype(BF16)
        primal = x_new
        kx = lax.dot_general(xbar, mat[...], (((1,), (1,)), ((), ())), preferred_element_type=F32)
        store(2 * step + 1, kx)
        dual = jnp.maximum(dual + sigma * (rhs - kx), 0.0)


def final_body(recv, scales, cost, rhs, upper, x_in, y_in, bounded, x_out, y_out):
    n, rows, tile = recv.shape
    part = rows // (2 * ITERS)

    def turned(j):
        return recv[:, j * part : (j + 1) * part, :].reshape(n * part, tile).astype(F32).T

    tau, sigma = scales[0:1, :], scales[1:2, :]
    primal, dual = x_in[...], y_in[...]
    for step in range(ITERS):
        primal = project(primal, cost[...] - turned(2 * step), tau, upper[...], bounded[...])
        dual = jnp.maximum(dual + sigma * (rhs[...] - turned(2 * step + 1)), 0.0)
    x_out[...] = primal
    y_out[...] = dual


def local_plan(blocks, block_index, live, cost, rhs, upper, x_init, y_init, bounded):
    n_blk, n_col = lax.axis_size("blk"), lax.axis_size("col")
    n = n_blk * n_col
    tile, nslots = blocks.shape[-1], blocks.shape[2]
    scn = cost.shape[1]
    part = scn // n
    like = jax.ShapeDtypeStruct
    limits = bounded[None, :]

    def spread(value):
        return lax.all_to_all(value, ("blk", "col"), 0, 0, tiled=True)

    def move(value, t, s):
        pairs = [(b * n_col + c, (b ^ t) * n_col + (c ^ s)) for b in range(n_blk) for c in range(n_col)]
        return lax.ppermute(value, ("blk", "col"), pairs)

    far = n_blk // 2
    near = [(t, s) for t in range(far) for s in range(n_col) if (t, s) != (0, 0)]
    half = nslots // 2
    top = half * tile
    size = top + (FIELDS + 1) * part
    first_near = [(0, s) for s in range(1, n_col)] + [(t, 0) for t in range(1, far)]
    far_out, *near_outs, own = call(
        functools.partial(prep_body, n_col, far, near, first_near),
        [held((top + (FIELDS * (len(near) + 1) + 1) * part, tile), BF16)]
        + [held((size + (n_col - 1) * FIELDS * part * (t > 0), tile), BF16) for t, s in first_near]
        + [held(((FIELDS + 1) * part, tile), BF16)],
        [SMEM] + [ANY] * (FIELDS + 2),
        [live] + pinned([cost, rhs, upper, x_init, y_init, block_index, blocks]),
        scratch=[pltpu.VMEM((tile, scn), F32)] * FIELDS
        + [pltpu.VMEM((half, tile, tile), BF16)]
        + [pltpu.SMEM(block_index.shape, jnp.int32)]
        + [pltpu.VMEM((FIELDS, scn, tile), BF16), pltpu.SemaphoreType.DMA((FIELDS + 2,))],
    )

    def relay(came, count, flops=0):
        outs = [held((size, tile), BF16)] * count
        return call(functools.partial(relay_body, top, part), outs, [VMEM], [came], flops=flops)

    def other_core(values):
        return [lax.ppermute(v, "rep", [(0, 1), (1, 0)]) for v in values]

    def slots_of(values):
        rows = [v[v.shape[0] - part + SLOT_ROW, : nslots + 1] for v in values]
        return jnp.stack(rows).astype(jnp.int32)

    early = {(far, 0): move(far_out, far, 0)}
    for (t, s), out in zip(first_near, near_outs):
        early[t, s] = move(out, t, s)
    for t in range(1, far):
        for s, out in zip(range(1, n_col), relay(early[t, 0], n_col - 1)):
            early[t, s] = move(out, 0, s)
    late = {}
    for (t, s), out in zip(near, relay(early[far, 0], len(near), flops=10**10)):
        late[far + t, s] = move(out, t, s)
    shifts, mine = list(early), list(early.values())
    mat, fields, sums = call(
        functools.partial(early_body, n_blk, n_col, shifts),
        [held((n * tile, n * tile), BF16), held((FIELDS, part, n * tile), BF16), held((8, scn), F32)],
        [SMEM, ANY] + [VMEM] * (1 + 2 * len(mine)),
        [slots_of([own] + mine), *pinned([blocks]), own] + mine + other_core(mine),
        scratch=[pltpu.VMEM(blocks.shape, BF16), pltpu.SemaphoreType.DMA],
    )
    last = near[-1][0] + far, near[-1][1]
    late[last] = call(touch_body, [held(late[last].shape, BF16)], [ANY, ANY], [late[last], sums], aliases={0: 0}, spec=ANY)[0]
    shifts, mine = list(late), list(late.values())
    products, scales, _, _ = call(
        functools.partial(main_body, n_blk, n_col, shifts, nslots),
        [like((n, 2 * ITERS * part, tile), BF16), like((8, scn), F32)]
        + [held(mat.shape, BF16), held(fields.shape, BF16)],
        [SMEM] + [VMEM] * (4 + 2 * len(mine)),
        [slots_of(mine), limits, mat, fields, sums] + mine + other_core(mine),
        scratch=[pltpu.VMEM((tile, scn), F32)],
        flops=4 * ITERS * n * n * tile * tile * part,
        aliases={2: 2, 3: 3},
    )
    return call(
        final_body,
        [like((tile, scn), F32)] * 2,
        [VMEM] * (FIELDS + 3),
        [spread(products), scales, cost, rhs, upper, x_init, y_init, limits],
    )


def project_box(value, upper, bounded):
    capped = jnp.where(bounded[None, :] > 0, jnp.minimum(value, upper), value)
    return jnp.maximum(capped, 0.0)


def collectives_plan(blocks, block_index, live, cost, rhs, upper, x_init, y_init, bounded):
    block_mats = blocks[0, 0]
    slots = block_index[0, 0]
    n_blk = lax.axis_size("blk")
    n_col = lax.axis_size("col")
    tile_size = block_mats.shape[1]
    scn_count = cost.shape[1]
    row_block = slots // n_blk
    col_block = slots % n_blk
    keep_mask = (jnp.arange(slots.shape[0]) < live[0, 0]).astype(jnp.float32)[:, None, None]
    totals = lax.psum((jnp.sum(cost * cost, axis=0), jnp.sum(rhs * rhs, axis=0)), ("blk", "col"))
    weight = jnp.sqrt(totals[0] + EPS) / jnp.sqrt(totals[1] + EPS)
    tau = (ETA / weight)[None, :]
    sigma = (ETA * weight)[None, :]
    primal = x_init
    dual = y_init
    for step in range(ITERS):
        gathered = lax.all_gather(dual.astype(jnp.bfloat16), "col", axis=0, tiled=True)
        pieces = gathered.reshape(n_col, tile_size, scn_count)[row_block]
        products = (
            jnp.einsum("bkt,bks->bts", block_mats, pieces, preferred_element_type=jnp.float32)
            * keep_mask
        )
        cols = jnp.zeros((n_blk, tile_size, scn_count), jnp.float32).at[col_block].add(products)
        kty = lax.psum_scatter(
            cols.reshape(n_blk * tile_size, scn_count).astype(jnp.bfloat16),
            "blk",
            scatter_dimension=0,
            tiled=True,
        ).astype(jnp.float32)
        x_new = project_box(primal - tau * (cost - kty), upper, bounded)
        xbar = (2.0 * x_new - primal).astype(jnp.bfloat16)
        whole = lax.all_gather(xbar, "blk", axis=0, tiled=True)
        primal = x_new
        row_pieces = whole.reshape(n_blk, tile_size, scn_count)[col_block]
        row_products = (
            jnp.einsum("bkt,bts->bks", block_mats, row_pieces, preferred_element_type=jnp.float32)
            * keep_mask
        )
        rows = jnp.zeros((n_col, tile_size, scn_count), jnp.float32).at[row_block].add(row_products)
        terms = rows.reshape(n_col * tile_size, scn_count)
        kx = lax.psum_scatter(
            terms.astype(jnp.bfloat16), "col", scatter_dimension=0, tiled=True
        ).astype(jnp.float32)
        dual = jnp.maximum(dual + sigma * (rhs - kx), 0.0)
    return (primal, dual)


def shards(*args):
    n_blk, n_col, n_rep = (lax.axis_size(axis) for axis in ("blk", "col", "rep"))
    blocks, cost = args[0], args[3]
    n, tile, nslots = n_blk * n_col, blocks.shape[-1], blocks.shape[2]
    fits = 2 * (n * tile) ** 2 <= MAX_MATRIX and cost.shape[1] % (16 * n) == 0 and cost.shape[1] == tile
    even = n_blk & (n_blk - 1) == 0 and n_col & (n_col - 1) == 0 and n_blk > 1 and n_rep == 2 and nslots % 2 == 0
    x, y = (local_plan if fits and even else collectives_plan)(*args)
    return x, y


def solution(mesh):
    in_specs = (
        P("blk", "col", None, None, None),
        P("blk", "col", None),
        P("blk", "col"),
        P(("blk", "col"), ("groups", "rep")),
        P(("blk", "col"), ("groups", "rep")),
        P(("blk", "col"), ("groups", "rep")),
        P(("blk", "col"), ("groups", "rep")),
        P(("blk", "col"), ("groups", "rep")),
        P(("groups", "rep")),
    )
    out_specs = (P(("blk", "col"), ("groups", "rep")), P(("blk", "col"), ("groups", "rep")))
    return jax.shard_map(shards, mesh=mesh, in_specs=in_specs, out_specs=out_specs, check_vma=False)
```

```python
import functools
import math

import jax
import jax.numpy as jnp
from jax import lax
from jax.experimental import pallas as pl
from jax.experimental.pallas import tpu as pltpu
from jax.sharding import PartitionSpec as P

ITERS = 2


ETA = 0.4
EPS = 1e-06
MAX_MATRIX = 8 * 1024 * 1024
PARTS = 3
FIELDS = 5
SLOT_ROW = 2 * PARTS

MIB = 1024 * 1024
VMEM = pl.BlockSpec(memory_space=pltpu.VMEM)
SMEM = pl.BlockSpec(memory_space=pltpu.SMEM)
ANY = pl.BlockSpec(memory_space=pl.ANY)
F32 = jnp.float32
BF16 = jnp.bfloat16


def held(shape, dtype):
    return pltpu.VMEM(shape, dtype)


def pinned(values):
    return [pltpu.with_memory_space_constraint(v, pltpu.HBM) for v in values]


def call(body, outs, in_specs, args, scratch=(), flops=0, limit=32, aliases=None, spec=VMEM):
    nbytes = sum(math.prod(a.shape) * jnp.dtype(a.dtype).itemsize for a in list(args) + list(outs))
    return pl.pallas_call(
        body,
        out_shape=list(outs),
        in_specs=in_specs,
        out_specs=[spec] * len(outs),
        scratch_shapes=list(scratch),
        input_output_aliases=aliases or {},
        compiler_params=pltpu.CompilerParams(vmem_limit_bytes=limit * MIB),
        cost_estimate=pl.CostEstimate(flops=flops, bytes_accessed=nbytes, transcendentals=0),
    )(*args)


def split_parts(values):
    high = values.astype(BF16).astype(F32)
    rest = values - high
    middle = rest.astype(BF16).astype(F32)
    low = (rest - middle).astype(BF16).astype(F32)
    return [high, middle, low]


def project(primal, grad, tau, upper, limited):
    value = primal - tau * grad
    capped = jnp.where(limited > 0, jnp.minimum(value, upper), value)
    return jnp.maximum(capped, 0.0)


def prep_body(n_col, far, near, first_near, *refs):
    live, *sources = refs[: FIELDS + 3]
    far_out, *near_outs, own_out = refs[FIELDS + 3 : FIELDS + 5 + len(first_near)]
    *fields, share, index, turned, sems = refs[FIELDS + 5 + len(first_near) :]
    half, tile = share.shape[0], share.shape[1]
    first = lax.axis_index("rep") * half
    targets = (*fields, index)
    copies = [
        pltpu.make_async_copy(source, target, sems.at[k])
        for k, (source, target) in enumerate(zip(sources[:-1], targets))
    ]
    copies.append(pltpu.make_async_copy(sources[-1].at[0, 0, pl.ds(first, half)], share, sems.at[FIELDS + 1]))
    for copy in copies:
        copy.start()
    part = own_out.shape[0] // (FIELDS + 1)
    nslots = index.shape[-1]
    rows = []
    for j, field in enumerate(fields):
        copies[j].wait()
        values = field[...]
        if j < 2:
            rows += split_parts(jnp.sum(values * values, axis=0, keepdims=True))
        turned[j] = values.T.astype(BF16)
    for copy in copies[FIELDS:]:
        copy.wait()
    lane = lax.broadcasted_iota(jnp.int32, (1, tile), 1)
    row = jnp.where(lane == nslots, live[0, 0].astype(F32), 0.0)
    for k in range(nslots):
        row = jnp.where(lane == k, index[0, 0, k].astype(F32), row)
    rows += [row, jnp.zeros((part - len(rows) - 1, tile), F32)]
    info = jnp.concatenate(rows, axis=0).astype(BF16)
    me_b, me_c = lax.axis_index("blk"), lax.axis_index("col")

    def piece(out, at, t, s):
        peer = pl.ds(pl.multiple_of(((me_b ^ t) * n_col + (me_c ^ s)) * part, part), part)
        for j in range(FIELDS):
            out[at + j * part : at + (j + 1) * part, :] = turned[j, peer, :]

    top = half * tile
    for out in (far_out, *near_outs):
        for k in range(half):
            out[k * tile : (k + 1) * tile, :] = share[k]
        out[out.shape[0] - part :, :] = info
    for m, (t, s) in enumerate([(0, 0), *near]):
        piece(far_out, top + m * FIELDS * part, far + t, s)
    for out, (t, s) in zip(near_outs, first_near):
        for m in range(1 if t == 0 else n_col):
            piece(out, top + m * FIELDS * part, t, s ^ m)
    piece(own_out, 0, 0, 0)
    own_out[FIELDS * part :, :] = info


def touch_body(part, after, out):
    del part, after, out


def relay_body(top, part, came, *outs):
    for m, out in enumerate(outs):
        out[0:top, :] = came[0:top, :]
        at = top + (m + 1) * FIELDS * part
        out[top : top + FIELDS * part, :] = came[at : at + FIELDS * part, :]
        out[top + FIELDS * part :, :] = came[came.shape[0] - part :, :]


def pack_body(top, *refs):
    *parts, out = refs
    for k, part in enumerate(parts):
        out[k * top : (k + 1) * top, :] = part[0:top, :]


def place(n_blk, n_col, mat, slots, source, shift, slot, block, nslots):
    tile = block.shape[-1]
    blk, col = lax.axis_index("blk") ^ shift[0], lax.axis_index("col") ^ shift[1]
    position = slots[source, slot]
    row = pl.multiple_of((blk * n_col + position // n_blk) * tile, tile)
    column = pl.multiple_of(((position % n_blk) * n_col + col) * tile, tile)

    @pl.when(slot < slots[source, nslots])
    def _():
        mat[pl.ds(row, tile), pl.ds(column, tile)] = block[...]


def place_shares(n_blk, n_col, mat, slots, source, shift, own_part, other_parts, at, nslots):
    half = nslots // 2
    tile = own_part.shape[1]
    core = lax.axis_index("rep")
    for part, start, which in ((own_part, 0, core), (other_parts, at * half * tile, 1 - core)):
        for k in range(half):
            block = part.at[start + k * tile : start + (k + 1) * tile, :]
            place(n_blk, n_col, mat, slots, source, shift, which * half + k, block, nslots)


def take(n_col, fields, shift, ref, at):
    part, tile = fields.shape[1], ref.shape[1]
    blk, col = lax.axis_index("blk") ^ shift[0], lax.axis_index("col") ^ shift[1]
    lanes = pl.ds(pl.multiple_of((blk * n_col + col) * tile, tile), tile)
    for j in range(FIELDS):
        fields[j, :, lanes] = ref[at + j * part : at + (j + 1) * part, :]
    info = ref[ref.shape[0] - part :, :].astype(F32)
    sums = []
    for j in range(2):
        first, second, third = (info[PARTS * j + k : PARTS * j + k + 1] for k in range(PARTS))
        sums.append((first + second) + third)
    return sums


def early_body(n_blk, n_col, shifts, slots, blocks_in, own, *refs):
    count = len(shifts)
    mine, theirs = refs[:count], refs[count]
    mat, fields, sums_out, blocks, sem = refs[count + 1 :]
    copy = pltpu.make_async_copy(blocks_in, blocks, sem)
    copy.start()
    nslots = blocks.shape[2]
    mat[...] = jnp.zeros(mat.shape, BF16)
    fields[...] = jnp.zeros(fields.shape, BF16)
    sums = take(n_col, fields, (0, 0), own, 0)
    for m, (shift, own_part) in enumerate(zip(shifts, mine)):
        place_shares(n_blk, n_col, mat, slots, m + 1, shift, own_part, theirs, m, nslots)
        more = take(n_col, fields, shift, own_part, nslots // 2 * own_part.shape[1])
        sums = [a + b for a, b in zip(sums, more)]
    copy.wait()
    for k in range(nslots):
        place(n_blk, n_col, mat, slots, 0, (0, 0), k, blocks.at[0, 0, k], nslots)
    sums_out[...] = jnp.concatenate(sums + [jnp.zeros((6, own.shape[1]), F32)], axis=0)


def main_body(n_blk, n_col, shifts, nslots, slots, bounded, mat, fields, sums_in, *refs):
    n = n_blk * n_col
    count = len(shifts)
    mine, theirs = refs[:count], refs[count : 2 * count]
    out, scales, _, _, turned = refs[2 * count :]
    part, tile = fields.shape[1], mine[0].shape[1]
    me_b, me_c = lax.axis_index("blk"), lax.axis_index("col")
    sums = [sums_in[0:1, :], sums_in[1:2, :]]
    for m, (shift, own_part, other_part) in enumerate(zip(shifts, mine, theirs)):
        place_shares(n_blk, n_col, mat, slots, m, shift, own_part, other_part, 0, nslots)
        more = take(n_col, fields, shift, own_part, nslots // 2 * tile)
        sums = [a + b for a, b in zip(sums, more)]
    cost, rhs, upper, primal, dual = (fields[j].astype(F32) for j in range(FIELDS))
    weight = jnp.sqrt(sums[0] + EPS) / jnp.sqrt(sums[1] + EPS)
    rows = jnp.concatenate([ETA / weight, ETA * weight, bounded[...].astype(F32), jnp.zeros((5, tile), F32)], axis=0)
    scales[...] = rows
    turned[...] = jnp.concatenate([rows, jnp.zeros((tile - 8, tile), F32)], axis=0).T
    own = turned[pl.ds(pl.multiple_of((me_b * n_col + me_c) * part, part), part), :]
    tau, sigma, limited = own[:, 0:1], own[:, 1:2], own[:, 2:3]

    def store(j, values):
        values = values.astype(BF16)
        for d in range(n):
            out[d, j * part : (j + 1) * part, :] = values[:, d * tile : (d + 1) * tile]

    for step in range(ITERS):
        kty = jnp.dot(dual.astype(BF16), mat[...], preferred_element_type=F32)
        store(2 * step, kty)
        x_new = project(primal, cost - kty, tau, upper, limited)
        xbar = (2.0 * x_new - primal).astype(BF16)
        primal = x_new
        kx = lax.dot_general(xbar, mat[...], (((1,), (1,)), ((), ())), preferred_element_type=F32)
        store(2 * step + 1, kx)
        dual = jnp.maximum(dual + sigma * (rhs - kx), 0.0)


def final_body(recv, scales, cost, rhs, upper, x_in, y_in, bounded, x_out, y_out):
    n, rows, tile = recv.shape
    part = rows // (2 * ITERS)

    def turned(j):
        return recv[:, j * part : (j + 1) * part, :].reshape(n * part, tile).astype(F32).T

    tau, sigma = scales[0:1, :], scales[1:2, :]
    primal, dual = x_in[...], y_in[...]
    for step in range(ITERS):
        primal = project(primal, cost[...] - turned(2 * step), tau, upper[...], bounded[...])
        dual = jnp.maximum(dual + sigma * (rhs[...] - turned(2 * step + 1)), 0.0)
    x_out[...] = primal
    y_out[...] = dual


def local_plan(blocks, block_index, live, cost, rhs, upper, x_init, y_init, bounded):
    n_blk, n_col = lax.axis_size("blk"), lax.axis_size("col")
    n = n_blk * n_col
    tile, nslots = blocks.shape[-1], blocks.shape[2]
    scn = cost.shape[1]
    part = scn // n
    like = jax.ShapeDtypeStruct
    limits = bounded[None, :]

    def spread(value):
        return lax.all_to_all(value, ("blk", "col"), 0, 0, tiled=True)

    def move(value, t, s):
        pairs = [(b * n_col + c, (b ^ t) * n_col + (c ^ s)) for b in range(n_blk) for c in range(n_col)]
        return lax.ppermute(value, ("blk", "col"), pairs)

    far = n_blk // 2
    near = [(t, s) for t in range(far) for s in range(n_col) if (t, s) != (0, 0)]
    half = nslots // 2
    top = half * tile
    size = top + (FIELDS + 1) * part
    first_near = [(0, s) for s in range(1, n_col)] + [(t, 0) for t in range(1, far)]
    far_out, *near_outs, own = call(
        functools.partial(prep_body, n_col, far, near, first_near),
        [held((top + (FIELDS * (len(near) + 1) + 1) * part, tile), BF16)]
        + [held((size + (n_col - 1) * FIELDS * part * (t > 0), tile), BF16) for t, s in first_near]
        + [held(((FIELDS + 1) * part, tile), BF16)],
        [SMEM] + [ANY] * (FIELDS + 2),
        [live] + pinned([cost, rhs, upper, x_init, y_init, block_index, blocks]),
        scratch=[pltpu.VMEM((tile, scn), F32)] * FIELDS
        + [pltpu.VMEM((half, tile, tile), BF16)]
        + [pltpu.SMEM(block_index.shape, jnp.int32)]
        + [pltpu.VMEM((FIELDS, scn, tile), BF16), pltpu.SemaphoreType.DMA((FIELDS + 2,))],
    )

    def relay(came, count, flops=0):
        outs = [held((size, tile), BF16)] * count
        return call(functools.partial(relay_body, top, part), outs, [VMEM], [came], flops=flops)

    def other_core(values):
        return [lax.ppermute(v, "rep", [(0, 1), (1, 0)]) for v in values]

    def slots_of(values):
        rows = [v[v.shape[0] - part + SLOT_ROW, : nslots + 1] for v in values]
        return jnp.stack(rows).astype(jnp.int32)

    early = {(far, 0): move(far_out, far, 0)}
    for (t, s), out in zip(first_near, near_outs):
        early[t, s] = move(out, t, s)
    late = {}
    for t in range(1, far):
        for s, out in zip(range(1, n_col), relay(early[t, 0], n_col - 1)):
            late[t, s] = move(out, 0, s)
    for (t, s), out in zip(near, relay(early[far, 0], len(near), flops=10**10)):
        late[far + t, s] = move(out, t, s)
    shifts, mine = list(early), list(early.values())
    packed_shape = held((len(mine) * top, tile), BF16)
    (packed,) = call(functools.partial(pack_body, top), [packed_shape], [VMEM] * len(mine), mine)
    mat, fields, sums = call(
        functools.partial(early_body, n_blk, n_col, shifts),
        [held((n * tile, n * tile), BF16), held((FIELDS, part, n * tile), BF16), held((8, scn), F32)],
        [SMEM, ANY] + [VMEM] * (2 + len(mine)),
        [slots_of([own] + mine), *pinned([blocks]), own] + mine + other_core([packed]),
        scratch=[pltpu.VMEM(blocks.shape, BF16), pltpu.SemaphoreType.DMA],
    )
    last = near[-1][0] + far, near[-1][1]
    late[last] = call(touch_body, [held(late[last].shape, BF16)], [ANY, ANY], [late[last], sums], aliases={0: 0}, spec=ANY)[0]
    shifts, mine = list(late), list(late.values())
    products, scales, _, _ = call(
        functools.partial(main_body, n_blk, n_col, shifts, nslots),
        [like((n, 2 * ITERS * part, tile), BF16), like((8, scn), F32)]
        + [held(mat.shape, BF16), held(fields.shape, BF16)],
        [SMEM] + [VMEM] * (4 + 2 * len(mine)),
        [slots_of(mine), limits, mat, fields, sums] + mine + other_core(mine),
        scratch=[pltpu.VMEM((tile, scn), F32)],
        flops=4 * ITERS * n * n * tile * tile * part,
        aliases={2: 2, 3: 3},
    )
    return call(
        final_body,
        [like((tile, scn), F32)] * 2,
        [VMEM] * (FIELDS + 3),
        [spread(products), scales, cost, rhs, upper, x_init, y_init, limits],
    )


def project_box(value, upper, bounded):
    capped = jnp.where(bounded[None, :] > 0, jnp.minimum(value, upper), value)
    return jnp.maximum(capped, 0.0)


def collectives_plan(blocks, block_index, live, cost, rhs, upper, x_init, y_init, bounded):
    block_mats = blocks[0, 0]
    slots = block_index[0, 0]
    n_blk = lax.axis_size("blk")
    n_col = lax.axis_size("col")
    tile_size = block_mats.shape[1]
    scn_count = cost.shape[1]
    row_block = slots // n_blk
    col_block = slots % n_blk
    keep_mask = (jnp.arange(slots.shape[0]) < live[0, 0]).astype(jnp.float32)[:, None, None]
    totals = lax.psum((jnp.sum(cost * cost, axis=0), jnp.sum(rhs * rhs, axis=0)), ("blk", "col"))
    weight = jnp.sqrt(totals[0] + EPS) / jnp.sqrt(totals[1] + EPS)
    tau = (ETA / weight)[None, :]
    sigma = (ETA * weight)[None, :]
    primal = x_init
    dual = y_init
    for step in range(ITERS):
        gathered = lax.all_gather(dual.astype(jnp.bfloat16), "col", axis=0, tiled=True)
        pieces = gathered.reshape(n_col, tile_size, scn_count)[row_block]
        products = (
            jnp.einsum("bkt,bks->bts", block_mats, pieces, preferred_element_type=jnp.float32)
            * keep_mask
        )
        cols = jnp.zeros((n_blk, tile_size, scn_count), jnp.float32).at[col_block].add(products)
        kty = lax.psum_scatter(
            cols.reshape(n_blk * tile_size, scn_count).astype(jnp.bfloat16),
            "blk",
            scatter_dimension=0,
            tiled=True,
        ).astype(jnp.float32)
        x_new = project_box(primal - tau * (cost - kty), upper, bounded)
        xbar = (2.0 * x_new - primal).astype(jnp.bfloat16)
        whole = lax.all_gather(xbar, "blk", axis=0, tiled=True)
        primal = x_new
        row_pieces = whole.reshape(n_blk, tile_size, scn_count)[col_block]
        row_products = (
            jnp.einsum("bkt,bts->bks", block_mats, row_pieces, preferred_element_type=jnp.float32)
            * keep_mask
        )
        rows = jnp.zeros((n_col, tile_size, scn_count), jnp.float32).at[row_block].add(row_products)
        terms = rows.reshape(n_col * tile_size, scn_count)
        kx = lax.psum_scatter(
            terms.astype(jnp.bfloat16), "col", scatter_dimension=0, tiled=True
        ).astype(jnp.float32)
        dual = jnp.maximum(dual + sigma * (rhs - kx), 0.0)
    return (primal, dual)


def shards(*args):
    n_blk, n_col, n_rep = (lax.axis_size(axis) for axis in ("blk", "col", "rep"))
    blocks, cost = args[0], args[3]
    n, tile, nslots = n_blk * n_col, blocks.shape[-1], blocks.shape[2]
    fits = 2 * (n * tile) ** 2 <= MAX_MATRIX and cost.shape[1] % (16 * n) == 0 and cost.shape[1] == tile
    even = n_blk & (n_blk - 1) == 0 and n_col & (n_col - 1) == 0 and n_blk > 1 and n_rep == 2 and nslots % 2 == 0
    x, y = (local_plan if fits and even else collectives_plan)(*args)
    return x, y


def solution(mesh):
    in_specs = (
        P("blk", "col", None, None, None),
        P("blk", "col", None),
        P("blk", "col"),
        P(("blk", "col"), ("groups", "rep")),
        P(("blk", "col"), ("groups", "rep")),
        P(("blk", "col"), ("groups", "rep")),
        P(("blk", "col"), ("groups", "rep")),
        P(("blk", "col"), ("groups", "rep")),
        P(("groups", "rep")),
    )
    out_specs = (P(("blk", "col"), ("groups", "rep")), P(("blk", "col"), ("groups", "rep")))
    return jax.shard_map(shards, mesh=mesh, in_specs=in_specs, out_specs=out_specs, check_vma=False)
```

```python
import functools
import math

import jax
import jax.numpy as jnp
from jax import lax
from jax.experimental import pallas as pl
from jax.experimental.pallas import tpu as pltpu
from jax.sharding import PartitionSpec as P

ITERS = 2


ETA = 0.4
EPS = 1e-06
MAX_MATRIX = 8 * 1024 * 1024
PARTS = 3
FIELDS = 5
SLOT_ROW = 2 * PARTS

MIB = 1024 * 1024
VMEM = pl.BlockSpec(memory_space=pltpu.VMEM)
SMEM = pl.BlockSpec(memory_space=pltpu.SMEM)
ANY = pl.BlockSpec(memory_space=pl.ANY)
F32 = jnp.float32
BF16 = jnp.bfloat16


def held(shape, dtype):
    return pltpu.VMEM(shape, dtype)


def pinned(values):
    return [pltpu.with_memory_space_constraint(v, pltpu.HBM) for v in values]


def call(body, outs, in_specs, args, scratch=(), flops=0, limit=32, aliases=None, spec=VMEM):
    nbytes = sum(math.prod(a.shape) * jnp.dtype(a.dtype).itemsize for a in list(args) + list(outs))
    return pl.pallas_call(
        body,
        out_shape=list(outs),
        in_specs=in_specs,
        out_specs=[spec] * len(outs),
        scratch_shapes=list(scratch),
        input_output_aliases=aliases or {},
        compiler_params=pltpu.CompilerParams(vmem_limit_bytes=limit * MIB),
        cost_estimate=pl.CostEstimate(flops=flops, bytes_accessed=nbytes, transcendentals=0),
    )(*args)


def split_parts(values):
    high = values.astype(BF16).astype(F32)
    rest = values - high
    middle = rest.astype(BF16).astype(F32)
    low = (rest - middle).astype(BF16).astype(F32)
    return [high, middle, low]


def project(primal, grad, tau, upper, limited):
    value = primal - tau * grad
    capped = jnp.where(limited > 0, jnp.minimum(value, upper), value)
    return jnp.maximum(capped, 0.0)


def prep_body(n_col, far, near, first_near, *refs):
    live, *sources = refs[: FIELDS + 3]
    far_out, *near_outs, own_out = refs[FIELDS + 3 : FIELDS + 5 + len(first_near)]
    *fields, share, index, turned, sems = refs[FIELDS + 5 + len(first_near) :]
    half, tile = share.shape[0], share.shape[1]
    first = lax.axis_index("rep") * half
    targets = (*fields, index)
    copies = [
        pltpu.make_async_copy(source, target, sems.at[k])
        for k, (source, target) in enumerate(zip(sources[:-1], targets))
    ]
    copies.append(pltpu.make_async_copy(sources[-1].at[0, 0, pl.ds(first, half)], share, sems.at[FIELDS + 1]))
    for copy in copies:
        copy.start()
    part = own_out.shape[0] // (FIELDS + 1)
    nslots = index.shape[-1]
    rows = []
    for j, field in enumerate(fields):
        copies[j].wait()
        values = field[...]
        if j < 2:
            rows += split_parts(jnp.sum(values * values, axis=0, keepdims=True))
        turned[j] = values.T.astype(BF16)
    for copy in copies[FIELDS:]:
        copy.wait()
    lane = lax.broadcasted_iota(jnp.int32, (1, tile), 1)
    row = jnp.where(lane == nslots, live[0, 0].astype(F32), 0.0)
    for k in range(nslots):
        row = jnp.where(lane == k, index[0, 0, k].astype(F32), row)
    rows += [row, jnp.zeros((part - len(rows) - 1, tile), F32)]
    info = jnp.concatenate(rows, axis=0).astype(BF16)
    me_b, me_c = lax.axis_index("blk"), lax.axis_index("col")

    def piece(out, at, t, s):
        peer = pl.ds(pl.multiple_of(((me_b ^ t) * n_col + (me_c ^ s)) * part, part), part)
        for j in range(FIELDS):
            out[at + j * part : at + (j + 1) * part, :] = turned[j, peer, :]

    top = half * tile
    for out in (far_out, *near_outs):
        for k in range(half):
            out[k * tile : (k + 1) * tile, :] = share[k]
        out[out.shape[0] - part :, :] = info
    for m, (t, s) in enumerate([(0, 0), *near]):
        piece(far_out, top + m * FIELDS * part, far + t, s)
    for out, (t, s) in zip(near_outs, first_near):
        for m in range(1 if t == 0 else n_col):
            piece(out, top + m * FIELDS * part, t, s ^ m)
    piece(own_out, 0, 0, 0)
    own_out[FIELDS * part :, :] = info


def touch_body(part, after, out):
    del part, after, out


def relay_body(top, part, came, *outs):
    for m, out in enumerate(outs):
        out[0:top, :] = came[0:top, :]
        at = top + (m + 1) * FIELDS * part
        out[top : top + FIELDS * part, :] = came[at : at + FIELDS * part, :]
        out[top + FIELDS * part :, :] = came[came.shape[0] - part :, :]


def pack_body(top, *refs):
    *parts, out = refs
    for k, part in enumerate(parts):
        out[k * top : (k + 1) * top, :] = part[0:top, :]


def place(n_blk, n_col, mat, slots, source, shift, slot, block, nslots):
    tile = block.shape[-1]
    blk, col = lax.axis_index("blk") ^ shift[0], lax.axis_index("col") ^ shift[1]
    position = slots[source, slot]
    row = pl.multiple_of((blk * n_col + position // n_blk) * tile, tile)
    column = pl.multiple_of(((position % n_blk) * n_col + col) * tile, tile)

    @pl.when(slot < slots[source, nslots])
    def _():
        mat[pl.ds(row, tile), pl.ds(column, tile)] = block[...]


def place_shares(n_blk, n_col, mat, slots, source, shift, own_part, other_parts, at, nslots):
    half = nslots // 2
    tile = own_part.shape[1]
    core = lax.axis_index("rep")
    for part, start, which in ((own_part, 0, core), (other_parts, at * half * tile, 1 - core)):
        for k in range(half):
            block = part.at[start + k * tile : start + (k + 1) * tile, :]
            place(n_blk, n_col, mat, slots, source, shift, which * half + k, block, nslots)


def take(n_col, fields, shift, ref, at):
    part, tile = fields.shape[1], ref.shape[1]
    blk, col = lax.axis_index("blk") ^ shift[0], lax.axis_index("col") ^ shift[1]
    lanes = pl.ds(pl.multiple_of((blk * n_col + col) * tile, tile), tile)
    for j in range(FIELDS):
        fields[j, :, lanes] = ref[at + j * part : at + (j + 1) * part, :]
    info = ref[ref.shape[0] - part :, :].astype(F32)
    sums = []
    for j in range(2):
        first, second, third = (info[PARTS * j + k : PARTS * j + k + 1] for k in range(PARTS))
        sums.append((first + second) + third)
    return sums


def early_body(n_blk, n_col, shifts, slots, blocks_in, own, *refs):
    count = len(shifts)
    mine, theirs = refs[:count], refs[count]
    mat, fields, sums_out, blocks, sem = refs[count + 1 :]
    copy = pltpu.make_async_copy(blocks_in, blocks, sem)
    copy.start()
    nslots = blocks.shape[2]
    mat[...] = jnp.zeros(mat.shape, BF16)
    fields[...] = jnp.zeros(fields.shape, BF16)
    sums = take(n_col, fields, (0, 0), own, 0)
    for m, (shift, own_part) in enumerate(zip(shifts, mine)):
        place_shares(n_blk, n_col, mat, slots, m + 1, shift, own_part, theirs, m, nslots)
        more = take(n_col, fields, shift, own_part, nslots // 2 * own_part.shape[1])
        sums = [a + b for a, b in zip(sums, more)]
    copy.wait()
    for k in range(nslots):
        place(n_blk, n_col, mat, slots, 0, (0, 0), k, blocks.at[0, 0, k], nslots)
    sums_out[...] = jnp.concatenate(sums + [jnp.zeros((6, own.shape[1]), F32)], axis=0)


def main_body(n_blk, n_col, shifts, nslots, slots, bounded, mat, fields, sums_in, *refs):
    n = n_blk * n_col
    count = len(shifts)
    mine, theirs = refs[:count], refs[count : 2 * count]
    out, scales, _, _, turned = refs[2 * count :]
    part, tile = fields.shape[1], mine[0].shape[1]
    me_b, me_c = lax.axis_index("blk"), lax.axis_index("col")
    sums = [sums_in[0:1, :], sums_in[1:2, :]]
    for m, (shift, own_part, other_part) in enumerate(zip(shifts, mine, theirs)):
        place_shares(n_blk, n_col, mat, slots, m, shift, own_part, other_part, 0, nslots)
        more = take(n_col, fields, shift, own_part, nslots // 2 * tile)
        sums = [a + b for a, b in zip(sums, more)]
    cost, rhs, upper, primal, dual = (fields[j].astype(F32) for j in range(FIELDS))
    weight = jnp.sqrt(sums[0] + EPS) / jnp.sqrt(sums[1] + EPS)
    rows = jnp.concatenate([ETA / weight, ETA * weight, bounded[...].astype(F32), jnp.zeros((5, tile), F32)], axis=0)
    scales[...] = rows
    turned[...] = jnp.concatenate([rows, jnp.zeros((tile - 8, tile), F32)], axis=0).T
    own = turned[pl.ds(pl.multiple_of((me_b * n_col + me_c) * part, part), part), :]
    tau, sigma, limited = own[:, 0:1], own[:, 1:2], own[:, 2:3]

    def store(j, values):
        values = values.astype(BF16)
        for d in range(n):
            out[d, j * part : (j + 1) * part, :] = values[:, d * tile : (d + 1) * tile]

    for step in range(ITERS):
        kty = jnp.dot(dual.astype(BF16), mat[...], preferred_element_type=F32)
        store(2 * step, kty)
        x_new = project(primal, cost - kty, tau, upper, limited)
        xbar = (2.0 * x_new - primal).astype(BF16)
        primal = x_new
        kx = lax.dot_general(xbar, mat[...], (((1,), (1,)), ((), ())), preferred_element_type=F32)
        store(2 * step + 1, kx)
        dual = jnp.maximum(dual + sigma * (rhs - kx), 0.0)


def final_body(recv, scales, cost, rhs, upper, x_in, y_in, bounded, x_out, y_out):
    n, rows, tile = recv.shape
    part = rows // (2 * ITERS)

    def turned(j):
        return recv[:, j * part : (j + 1) * part, :].reshape(n * part, tile).astype(F32).T

    tau, sigma = scales[0:1, :], scales[1:2, :]
    primal, dual = x_in[...], y_in[...]
    for step in range(ITERS):
        primal = project(primal, cost[...] - turned(2 * step), tau, upper[...], bounded[...])
        dual = jnp.maximum(dual + sigma * (rhs[...] - turned(2 * step + 1)), 0.0)
    x_out[...] = primal
    y_out[...] = dual


def local_plan(blocks, block_index, live, cost, rhs, upper, x_init, y_init, bounded):
    n_blk, n_col = lax.axis_size("blk"), lax.axis_size("col")
    n = n_blk * n_col
    tile, nslots = blocks.shape[-1], blocks.shape[2]
    scn = cost.shape[1]
    part = scn // n
    like = jax.ShapeDtypeStruct
    limits = bounded[None, :]

    def spread(value):
        return lax.all_to_all(value, ("blk", "col"), 0, 0, tiled=True)

    def move(value, t, s):
        pairs = [(b * n_col + c, (b ^ t) * n_col + (c ^ s)) for b in range(n_blk) for c in range(n_col)]
        return lax.ppermute(value, ("blk", "col"), pairs)

    far = n_blk // 2
    near = [(t, s) for t in range(far) for s in range(n_col) if (t, s) != (0, 0)]
    half = nslots // 2
    top = half * tile
    size = top + (FIELDS + 1) * part
    first_near = [(0, s) for s in range(1, n_col)] + [(t, 0) for t in range(1, far)]
    far_out, *near_outs, own = call(
        functools.partial(prep_body, n_col, far, near, first_near),
        [held((top + (FIELDS * (len(near) + 1) + 1) * part, tile), BF16)]
        + [held((size + (n_col - 1) * FIELDS * part * (t > 0), tile), BF16) for t, s in first_near]
        + [held(((FIELDS + 1) * part, tile), BF16)],
        [SMEM] + [ANY] * (FIELDS + 2),
        [live] + pinned([cost, rhs, upper, x_init, y_init, block_index, blocks]),
        scratch=[pltpu.VMEM((tile, scn), F32)] * FIELDS
        + [pltpu.VMEM((half, tile, tile), BF16)]
        + [pltpu.SMEM(block_index.shape, jnp.int32)]
        + [pltpu.VMEM((FIELDS, scn, tile), BF16), pltpu.SemaphoreType.DMA((FIELDS + 2,))],
    )

    def relay(came, count, flops):
        outs = [held((size, tile), BF16)] * count
        return call(functools.partial(relay_body, top, part), outs, [VMEM], [came], flops=flops)

    def other_core(values):
        return [lax.ppermute(v, "rep", [(0, 1), (1, 0)]) for v in values]

    def slots_of(values):
        rows = [v[v.shape[0] - part + SLOT_ROW, : nslots + 1] for v in values]
        return jnp.stack(rows).astype(jnp.int32)

    early = {(far, 0): move(far_out, far, 0)}
    for (t, s), out in zip(first_near, near_outs):
        early[t, s] = move(out, t, s)
    late = {}
    for t in range(1, far):
        for s, out in zip(range(1, n_col), relay(early[t, 0], n_col - 1, 10**10)):
            late[t, s] = move(out, 0, s)
    for (t, s), out in zip(near, relay(early[far, 0], len(near), 5 * 10**9)):
        late[far + t, s] = move(out, t, s)
    shifts, mine = list(early), list(early.values())
    packed_shape = held((len(mine) * top, tile), BF16)
    (packed,) = call(functools.partial(pack_body, top), [packed_shape], [VMEM] * len(mine), mine)
    mat, fields, sums = call(
        functools.partial(early_body, n_blk, n_col, shifts),
        [held((n * tile, n * tile), BF16), held((FIELDS, part, n * tile), BF16), held((8, scn), F32)],
        [SMEM, ANY] + [VMEM] * (2 + len(mine)),
        [slots_of([own] + mine), *pinned([blocks]), own] + mine + other_core([packed]),
        scratch=[pltpu.VMEM(blocks.shape, BF16), pltpu.SemaphoreType.DMA],
    )
    last = near[-1][0] + far, near[-1][1]
    late[last] = call(touch_body, [held(late[last].shape, BF16)], [ANY, ANY], [late[last], sums], aliases={0: 0}, spec=ANY)[0]
    shifts, mine = list(late), list(late.values())
    products, scales, _, _ = call(
        functools.partial(main_body, n_blk, n_col, shifts, nslots),
        [like((n, 2 * ITERS * part, tile), BF16), like((8, scn), F32)]
        + [held(mat.shape, BF16), held(fields.shape, BF16)],
        [SMEM] + [VMEM] * (4 + 2 * len(mine)),
        [slots_of(mine), limits, mat, fields, sums] + mine + other_core(mine),
        scratch=[pltpu.VMEM((tile, scn), F32)],
        flops=4 * ITERS * n * n * tile * tile * part,
        aliases={2: 2, 3: 3},
    )
    return call(
        final_body,
        [like((tile, scn), F32)] * 2,
        [VMEM] * (FIELDS + 3),
        [spread(products), scales, cost, rhs, upper, x_init, y_init, limits],
    )


def project_box(value, upper, bounded):
    capped = jnp.where(bounded[None, :] > 0, jnp.minimum(value, upper), value)
    return jnp.maximum(capped, 0.0)


def collectives_plan(blocks, block_index, live, cost, rhs, upper, x_init, y_init, bounded):
    block_mats = blocks[0, 0]
    slots = block_index[0, 0]
    n_blk = lax.axis_size("blk")
    n_col = lax.axis_size("col")
    tile_size = block_mats.shape[1]
    scn_count = cost.shape[1]
    row_block = slots // n_blk
    col_block = slots % n_blk
    keep_mask = (jnp.arange(slots.shape[0]) < live[0, 0]).astype(jnp.float32)[:, None, None]
    totals = lax.psum((jnp.sum(cost * cost, axis=0), jnp.sum(rhs * rhs, axis=0)), ("blk", "col"))
    weight = jnp.sqrt(totals[0] + EPS) / jnp.sqrt(totals[1] + EPS)
    tau = (ETA / weight)[None, :]
    sigma = (ETA * weight)[None, :]
    primal = x_init
    dual = y_init
    for step in range(ITERS):
        gathered = lax.all_gather(dual.astype(jnp.bfloat16), "col", axis=0, tiled=True)
        pieces = gathered.reshape(n_col, tile_size, scn_count)[row_block]
        products = (
            jnp.einsum("bkt,bks->bts", block_mats, pieces, preferred_element_type=jnp.float32)
            * keep_mask
        )
        cols = jnp.zeros((n_blk, tile_size, scn_count), jnp.float32).at[col_block].add(products)
        kty = lax.psum_scatter(
            cols.reshape(n_blk * tile_size, scn_count).astype(jnp.bfloat16),
            "blk",
            scatter_dimension=0,
            tiled=True,
        ).astype(jnp.float32)
        x_new = project_box(primal - tau * (cost - kty), upper, bounded)
        xbar = (2.0 * x_new - primal).astype(jnp.bfloat16)
        whole = lax.all_gather(xbar, "blk", axis=0, tiled=True)
        primal = x_new
        row_pieces = whole.reshape(n_blk, tile_size, scn_count)[col_block]
        row_products = (
            jnp.einsum("bkt,bts->bks", block_mats, row_pieces, preferred_element_type=jnp.float32)
            * keep_mask
        )
        rows = jnp.zeros((n_col, tile_size, scn_count), jnp.float32).at[row_block].add(row_products)
        terms = rows.reshape(n_col * tile_size, scn_count)
        kx = lax.psum_scatter(
            terms.astype(jnp.bfloat16), "col", scatter_dimension=0, tiled=True
        ).astype(jnp.float32)
        dual = jnp.maximum(dual + sigma * (rhs - kx), 0.0)
    return (primal, dual)


def shards(*args):
    n_blk, n_col, n_rep = (lax.axis_size(axis) for axis in ("blk", "col", "rep"))
    blocks, cost = args[0], args[3]
    n, tile, nslots = n_blk * n_col, blocks.shape[-1], blocks.shape[2]
    fits = 2 * (n * tile) ** 2 <= MAX_MATRIX and cost.shape[1] % (16 * n) == 0 and cost.shape[1] == tile
    even = n_blk & (n_blk - 1) == 0 and n_col & (n_col - 1) == 0 and n_blk > 1 and n_rep == 2 and nslots % 2 == 0
    x, y = (local_plan if fits and even else collectives_plan)(*args)
    return x, y


def solution(mesh):
    in_specs = (
        P("blk", "col", None, None, None),
        P("blk", "col", None),
        P("blk", "col"),
        P(("blk", "col"), ("groups", "rep")),
        P(("blk", "col"), ("groups", "rep")),
        P(("blk", "col"), ("groups", "rep")),
        P(("blk", "col"), ("groups", "rep")),
        P(("blk", "col"), ("groups", "rep")),
        P(("groups", "rep")),
    )
    out_specs = (P(("blk", "col"), ("groups", "rep")), P(("blk", "col"), ("groups", "rep")))
    return jax.shard_map(shards, mesh=mesh, in_specs=in_specs, out_specs=out_specs, check_vma=False)
```

```python
import functools
import math

import jax
import jax.numpy as jnp
from jax import lax
from jax.experimental import pallas as pl
from jax.experimental.pallas import tpu as pltpu
from jax.sharding import PartitionSpec as P

ITERS = 2


ETA = 0.4
EPS = 1e-06
MAX_MATRIX = 8 * 1024 * 1024
PARTS = 3
FIELDS = 5
SLOT_ROW = 2 * PARTS
INFO = 16

MIB = 1024 * 1024
VMEM = pl.BlockSpec(memory_space=pltpu.VMEM)
SMEM = pl.BlockSpec(memory_space=pltpu.SMEM)
ANY = pl.BlockSpec(memory_space=pl.ANY)
F32 = jnp.float32
BF16 = jnp.bfloat16


def held(shape, dtype):
    return pltpu.VMEM(shape, dtype)


def pinned(values):
    return [pltpu.with_memory_space_constraint(v, pltpu.HBM) for v in values]


def call(body, outs, in_specs, args, scratch=(), flops=0, limit=32, aliases=None):
    nbytes = sum(math.prod(a.shape) * jnp.dtype(a.dtype).itemsize for a in list(args) + list(outs))
    return pl.pallas_call(
        body,
        out_shape=list(outs),
        in_specs=in_specs,
        out_specs=[VMEM] * len(outs),
        scratch_shapes=list(scratch),
        input_output_aliases=aliases or {},
        compiler_params=pltpu.CompilerParams(vmem_limit_bytes=limit * MIB),
        cost_estimate=pl.CostEstimate(flops=flops, bytes_accessed=nbytes, transcendentals=0),
    )(*args)


def split_parts(values):
    high = values.astype(BF16).astype(F32)
    rest = values - high
    middle = rest.astype(BF16).astype(F32)
    low = (rest - middle).astype(BF16).astype(F32)
    return [high, middle, low]


def project(primal, grad, tau, upper, limited):
    value = primal - tau * grad
    capped = jnp.where(limited > 0, jnp.minimum(value, upper), value)
    return jnp.maximum(capped, 0.0)


def prep_body(far, first_near, *refs):
    live, *sources = refs[: FIELDS + 3]
    far_out, *near_outs, own_out = refs[FIELDS + 3 : FIELDS + 5 + len(first_near)]
    *fields, share, index, turned, sems = refs[FIELDS + 5 + len(first_near) :]
    half, tile = share.shape[0], share.shape[1]
    first = lax.axis_index("rep") * half
    targets = (*fields, index)
    copies = [
        pltpu.make_async_copy(source, target, sems.at[k])
        for k, (source, target) in enumerate(zip(sources[:-1], targets))
    ]
    copies.append(pltpu.make_async_copy(sources[-1].at[0, 0, pl.ds(first, half)], share, sems.at[FIELDS + 1]))
    for copy in copies:
        copy.start()
    part = (own_out.shape[0] - INFO) // FIELDS
    nslots = index.shape[-1]
    rows = []
    for j, field in enumerate(fields):
        copies[j].wait()
        values = field[...]
        if j < 2:
            rows += split_parts(jnp.sum(values * values, axis=0, keepdims=True))
        turned[j] = values.T.astype(BF16)
    for copy in copies[FIELDS:]:
        copy.wait()
    lane = lax.broadcasted_iota(jnp.int32, (1, tile), 1)
    row = jnp.where(lane == nslots, live[0, 0].astype(F32), 0.0)
    for k in range(nslots):
        row = jnp.where(lane == k, index[0, 0, k].astype(F32), row)
    rows += [row, jnp.zeros((INFO - len(rows) - 1, tile), F32)]
    info = jnp.concatenate(rows, axis=0).astype(BF16)
    me_b = lax.axis_index("blk")

    def piece(out, at, t):
        rows = pl.ds(pl.multiple_of((me_b ^ t) * part, part), part)
        for j in range(FIELDS):
            out[at + j * part : at + (j + 1) * part, :] = turned[j, rows, :]

    top = half * tile
    for out in (far_out, *near_outs):
        for k in range(half):
            out[k * tile : (k + 1) * tile, :] = share[k]
    for t in range(far):
        piece(far_out, top + t * FIELDS * part, far + t)
    for out, (t, _) in zip(near_outs, first_near):
        piece(out, top, t)
    piece(own_out, 0, 0)
    for out in (far_out, *near_outs, own_out):
        out[out.shape[0] - INFO :, :] = info


def relay_body(top, part, came, *outs):
    for t, out in enumerate(outs):
        out[0:top, :] = came[0:top, :]
        at = top + t * FIELDS * part
        out[top : top + FIELDS * part, :] = came[at : at + FIELDS * part, :]
        out[top + FIELDS * part :, :] = came[came.shape[0] - INFO :, :]


def place(n_blk, n_col, mat, slots, source, shift, slot, block, nslots):
    tile = block.shape[-1]
    blk, col = lax.axis_index("blk") ^ shift[0], lax.axis_index("col") ^ shift[1]
    position = slots[source, slot]
    row = pl.multiple_of((blk * n_col + position // n_blk) * tile, tile)
    column = pl.multiple_of(((position % n_blk) * n_col + col) * tile, tile)

    @pl.when(slot < slots[source, nslots])
    def _():
        mat[pl.ds(row, tile), pl.ds(column, tile)] = block[...]


def place_shares(n_blk, n_col, mat, slots, source, shift, own_part, other_part, nslots):
    half = nslots // 2
    tile = own_part.shape[1]
    core = lax.axis_index("rep")
    for part, which in ((own_part, core), (other_part, 1 - core)):
        for k in range(half):
            block = part.at[k * tile : (k + 1) * tile, :]
            place(n_blk, n_col, mat, slots, source, shift, which * half + k, block, nslots)


def take(n_col, fields, shift, ref, at):
    part, tile = fields.shape[1], ref.shape[1]
    blk, col = lax.axis_index("blk") ^ shift[0], lax.axis_index("col") ^ shift[1]
    lanes = pl.ds(pl.multiple_of((blk * n_col + col) * tile, tile), tile)
    for j in range(FIELDS):
        fields[j, :, lanes] = ref[at + j * part : at + (j + 1) * part, :]
    info = ref[ref.shape[0] - INFO :, :].astype(F32)
    sums = []
    for j in range(2):
        first, second, third = (info[PARTS * j + k : PARTS * j + k + 1] for k in range(PARTS))
        sums.append((first + second) + third)
    return sums


def early_body(n_blk, n_col, shifts, slots, blocks_in, own, *refs):
    count = len(shifts)
    mine, theirs = refs[:count], refs[count : 2 * count]
    mat, fields, sums_out, blocks, sem = refs[2 * count :]
    copy = pltpu.make_async_copy(blocks_in, blocks, sem)
    copy.start()
    nslots = blocks.shape[2]
    mat[...] = jnp.zeros(mat.shape, BF16)
    fields[...] = jnp.zeros(fields.shape, BF16)
    sums = take(n_col, fields, (0, 0), own, 0)
    for m, (shift, own_part, other_part) in enumerate(zip(shifts, mine, theirs)):
        place_shares(n_blk, n_col, mat, slots, m + 1, shift, own_part, other_part, nslots)
        more = take(n_col, fields, shift, own_part, nslots // 2 * own_part.shape[1])
        sums = [a + b for a, b in zip(sums, more)]
    copy.wait()
    for k in range(nslots):
        place(n_blk, n_col, mat, slots, 0, (0, 0), k, blocks.at[0, 0, k], nslots)
    sums_out[...] = jnp.concatenate(sums + [jnp.zeros((6, own.shape[1]), F32)], axis=0)


def main_body(n_blk, n_col, shifts, nslots, slots, bounded, mat, fields, sums_in, *refs):
    count = len(shifts)
    mine, theirs = refs[:count], refs[count : 2 * count]
    *outs, scales, _, _, products, turned = refs[2 * count :]
    part, tile = fields.shape[1], mine[0].shape[1]
    me_b, me_c = lax.axis_index("blk"), lax.axis_index("col")
    sums = [sums_in[0:1, :], sums_in[1:2, :]]
    for m, (shift, own_part, other_part) in enumerate(zip(shifts, mine, theirs)):
        place_shares(n_blk, n_col, mat, slots, m, shift, own_part, other_part, nslots)
        more = take(n_col, fields, shift, own_part, nslots // 2 * tile)
        sums = [a + b for a, b in zip(sums, more)]
    cost, rhs, upper, primal, dual = (fields[j].astype(F32) for j in range(FIELDS))
    weight = jnp.sqrt(sums[0] + EPS) / jnp.sqrt(sums[1] + EPS)
    rows = jnp.concatenate([ETA / weight, ETA * weight, bounded[...].astype(F32), jnp.zeros((5, tile), F32)], axis=0)
    scales[...] = rows
    turned[...] = jnp.concatenate([rows, jnp.zeros((tile - 8, tile), F32)], axis=0).T
    own = turned[pl.ds(pl.multiple_of(me_b * part, part), part), :]
    tau, sigma, limited = own[:, 0:1], own[:, 1:2], own[:, 2:3]

    for step in range(ITERS):
        kty = jnp.dot(dual.astype(BF16), mat[...], preferred_element_type=F32)
        products[2 * step] = kty.astype(BF16)
        x_new = project(primal, cost - kty, tau, upper, limited)
        xbar = (2.0 * x_new - primal).astype(BF16)
        primal = x_new
        kx = lax.dot_general(xbar, mat[...], (((1,), (1,)), ((), ())), preferred_element_type=F32)
        products[2 * step + 1] = kx.astype(BF16)
        dual = jnp.maximum(dual + sigma * (rhs - kx), 0.0)
    for t, out in enumerate(outs):
        lanes = pl.ds(pl.multiple_of(((me_b ^ t) * n_col + me_c) * tile, tile), tile)
        for j in range(2 * ITERS):
            out[j * part : (j + 1) * part, :] = products[j, :, lanes]


def final_body(order, *refs):
    parts = refs[: len(order)]
    scales, cost, rhs, upper, x_in, y_in, bounded, x_out, y_out, products = refs[len(order) :]
    part = parts[0].shape[0] // (2 * ITERS)
    me_b = lax.axis_index("blk")
    for t, recv in zip(order, parts):
        rows = pl.ds(pl.multiple_of((me_b ^ t) * part, part), part)
        for j in range(2 * ITERS):
            products[j, rows, :] = recv[j * part : (j + 1) * part, :]

    def turned(j):
        return products[j].astype(F32).T

    tau, sigma = scales[0:1, :], scales[1:2, :]
    primal, dual = x_in[...], y_in[...]
    for step in range(ITERS):
        primal = project(primal, cost[...] - turned(2 * step), tau, upper[...], bounded[...])
        dual = jnp.maximum(dual + sigma * (rhs[...] - turned(2 * step + 1)), 0.0)
    x_out[...] = primal
    y_out[...] = dual


def local_plan(blocks, block_index, live, cost, rhs, upper, x_init, y_init, bounded):
    n_blk, n_col = lax.axis_size("blk"), lax.axis_size("col")
    n = n_blk * n_col
    tile, nslots = blocks.shape[-1], blocks.shape[2]
    scn = cost.shape[1]
    part = scn // n_blk
    like = jax.ShapeDtypeStruct
    limits = bounded[None, :]

    def move(value, t, s):
        pairs = [(b * n_col + c, (b ^ t) * n_col + (c ^ s)) for b in range(n_blk) for c in range(n_col)]
        return lax.ppermute(value, ("blk", "col"), pairs)

    far = n_blk // 2
    near = [(t, s) for t in range(far) for s in range(n_col) if (t, s) != (0, 0)]
    half = nslots // 2
    top = half * tile
    size = top + FIELDS * part + INFO
    first_near = [(0, s) for s in range(1, n_col)] + [(t, 0) for t in range(1, far)]
    far_out, *near_outs, own = call(
        functools.partial(prep_body, far, first_near),
        [held((top + FIELDS * far * part + INFO, tile), BF16)]
        + [held((size, tile), BF16)] * len(first_near)
        + [held((size - top, tile), BF16)],
        [SMEM] + [ANY] * (FIELDS + 2),
        [live] + pinned([cost, rhs, upper, x_init, y_init, block_index, blocks]),
        scratch=[pltpu.VMEM((tile, scn), F32)] * FIELDS
        + [pltpu.VMEM((half, tile, tile), BF16)]
        + [pltpu.SMEM(block_index.shape, jnp.int32)]
        + [pltpu.VMEM((FIELDS, scn, tile), BF16), pltpu.SemaphoreType.DMA((FIELDS + 2,))],
    )

    def other_core(values):
        return [lax.ppermute(v[:top], "rep", [(0, 1), (1, 0)]) for v in values]

    def slots_of(values):
        rows = [v[v.shape[0] - INFO + SLOT_ROW, : nslots + 1] for v in values]
        return jnp.stack(rows).astype(jnp.int32)

    early = {(far, 0): move(far_out, far, 0)}
    for (t, s), out in zip(first_near, near_outs):
        early[t, s] = move(out, t, s)
    for t in range(1, far):
        for s in range(1, n_col):
            early[t, s] = move(early[t, 0], 0, s)
    relayed = call(
        functools.partial(relay_body, top, part), [held((size, tile), BF16)] * far, [VMEM], [early[far, 0]]
    )
    late = {(far + t, s): move(relayed[t], t, s) for t, s in near}
    shifts, mine = list(early), list(early.values())
    mat, fields, sums = call(
        functools.partial(early_body, n_blk, n_col, shifts),
        [held((n * tile, n * tile), BF16), held((FIELDS, part, n * tile), BF16), held((8, scn), F32)],
        [SMEM, ANY] + [VMEM] * (1 + 2 * len(mine)),
        [slots_of([own] + mine), *pinned([blocks]), own] + mine + other_core(mine),
        scratch=[pltpu.VMEM(blocks.shape, BF16), pltpu.SemaphoreType.DMA],
    )
    shifts, mine = list(late), list(late.values())
    *products, scales, _, _ = call(
        functools.partial(main_body, n_blk, n_col, shifts, nslots),
        [held((2 * ITERS * part, tile), BF16)] * n_blk
        + [like((8, scn), F32), held(mat.shape, BF16), held(fields.shape, BF16)],
        [SMEM] + [VMEM] * (4 + 2 * len(mine)),
        [slots_of(mine), limits, mat, fields, sums] + mine + other_core(mine),
        scratch=[pltpu.VMEM((2 * ITERS, part, n * tile), BF16), pltpu.VMEM((tile, scn), F32)],
        flops=4 * ITERS * n * n * tile * tile * part,
        aliases={2: n_blk + 1, 3: n_blk + 2},
    )
    order = [0, *range(n_blk - 1, 0, -1)]
    parts = [products[t] if t == 0 else move(products[t], t, 0) for t in order]
    return call(
        functools.partial(final_body, order),
        [like((tile, scn), F32)] * 2,
        [VMEM] * (n_blk + FIELDS + 2),
        parts + [scales, cost, rhs, upper, x_init, y_init, limits],
        scratch=[pltpu.VMEM((2 * ITERS, scn, tile), BF16)],
    )


def project_box(value, upper, bounded):
    capped = jnp.where(bounded[None, :] > 0, jnp.minimum(value, upper), value)
    return jnp.maximum(capped, 0.0)


def collectives_plan(blocks, block_index, live, cost, rhs, upper, x_init, y_init, bounded):
    block_mats = blocks[0, 0]
    slots = block_index[0, 0]
    n_blk = lax.axis_size("blk")
    n_col = lax.axis_size("col")
    tile_size = block_mats.shape[1]
    scn_count = cost.shape[1]
    row_block = slots // n_blk
    col_block = slots % n_blk
    keep_mask = (jnp.arange(slots.shape[0]) < live[0, 0]).astype(jnp.float32)[:, None, None]
    totals = lax.psum((jnp.sum(cost * cost, axis=0), jnp.sum(rhs * rhs, axis=0)), ("blk", "col"))
    weight = jnp.sqrt(totals[0] + EPS) / jnp.sqrt(totals[1] + EPS)
    tau = (ETA / weight)[None, :]
    sigma = (ETA * weight)[None, :]
    primal = x_init
    dual = y_init
    for step in range(ITERS):
        gathered = lax.all_gather(dual.astype(jnp.bfloat16), "col", axis=0, tiled=True)
        pieces = gathered.reshape(n_col, tile_size, scn_count)[row_block]
        products = (
            jnp.einsum("bkt,bks->bts", block_mats, pieces, preferred_element_type=jnp.float32)
            * keep_mask
        )
        cols = jnp.zeros((n_blk, tile_size, scn_count), jnp.float32).at[col_block].add(products)
        kty = lax.psum_scatter(
            cols.reshape(n_blk * tile_size, scn_count).astype(jnp.bfloat16),
            "blk",
            scatter_dimension=0,
            tiled=True,
        ).astype(jnp.float32)
        x_new = project_box(primal - tau * (cost - kty), upper, bounded)
        xbar = (2.0 * x_new - primal).astype(jnp.bfloat16)
        whole = lax.all_gather(xbar, "blk", axis=0, tiled=True)
        primal = x_new
        row_pieces = whole.reshape(n_blk, tile_size, scn_count)[col_block]
        row_products = (
            jnp.einsum("bkt,bts->bks", block_mats, row_pieces, preferred_element_type=jnp.float32)
            * keep_mask
        )
        rows = jnp.zeros((n_col, tile_size, scn_count), jnp.float32).at[row_block].add(row_products)
        terms = rows.reshape(n_col * tile_size, scn_count)
        kx = lax.psum_scatter(
            terms.astype(jnp.bfloat16), "col", scatter_dimension=0, tiled=True
        ).astype(jnp.float32)
        dual = jnp.maximum(dual + sigma * (rhs - kx), 0.0)
    return (primal, dual)


def shards(*args):
    n_blk, n_col, n_rep = (lax.axis_size(axis) for axis in ("blk", "col", "rep"))
    blocks, cost = args[0], args[3]
    n, tile, nslots = n_blk * n_col, blocks.shape[-1], blocks.shape[2]
    fits = 2 * (n * tile) ** 2 <= MAX_MATRIX and cost.shape[1] % (16 * n_blk) == 0 and cost.shape[1] == tile
    even = n_blk & (n_blk - 1) == 0 and n_col & (n_col - 1) == 0 and n_blk > 1 and n_rep == 2 and nslots % 2 == 0
    x, y = (local_plan if fits and even else collectives_plan)(*args)
    return x, y


def solution(mesh):
    in_specs = (
        P("blk", "col", None, None, None),
        P("blk", "col", None),
        P("blk", "col"),
        P(("blk", "col"), ("groups", "rep")),
        P(("blk", "col"), ("groups", "rep")),
        P(("blk", "col"), ("groups", "rep")),
        P(("blk", "col"), ("groups", "rep")),
        P(("blk", "col"), ("groups", "rep")),
        P(("groups", "rep")),
    )
    out_specs = (P(("blk", "col"), ("groups", "rep")), P(("blk", "col"), ("groups", "rep")))
    return jax.shard_map(shards, mesh=mesh, in_specs=in_specs, out_specs=out_specs, check_vma=False)
```

```python
import functools
import math

import jax
import jax.numpy as jnp
from jax import lax
from jax.experimental import pallas as pl
from jax.experimental.pallas import tpu as pltpu
from jax.sharding import PartitionSpec as P

ITERS = 2


ETA = 0.4
EPS = 1e-06
MAX_MATRIX = 8 * 1024 * 1024
PARTS = 3
FIELDS = 5
SLOT_ROW = 2 * PARTS
INFO = 16

MIB = 1024 * 1024
VMEM = pl.BlockSpec(memory_space=pltpu.VMEM)
SMEM = pl.BlockSpec(memory_space=pltpu.SMEM)
ANY = pl.BlockSpec(memory_space=pl.ANY)
F32 = jnp.float32
BF16 = jnp.bfloat16


def held(shape, dtype):
    return pltpu.VMEM(shape, dtype)


def pinned(values):
    return [pltpu.with_memory_space_constraint(v, pltpu.HBM) for v in values]


def call(body, outs, in_specs, args, scratch=(), flops=0, limit=32, aliases=None, spec=VMEM):
    nbytes = sum(math.prod(a.shape) * jnp.dtype(a.dtype).itemsize for a in list(args) + list(outs))
    return pl.pallas_call(
        body,
        out_shape=list(outs),
        in_specs=in_specs,
        out_specs=[spec] * len(outs),
        scratch_shapes=list(scratch),
        input_output_aliases=aliases or {},
        compiler_params=pltpu.CompilerParams(vmem_limit_bytes=limit * MIB),
        cost_estimate=pl.CostEstimate(flops=flops, bytes_accessed=nbytes, transcendentals=0),
    )(*args)


def split_parts(values):
    high = values.astype(BF16).astype(F32)
    rest = values - high
    middle = rest.astype(BF16).astype(F32)
    low = (rest - middle).astype(BF16).astype(F32)
    return [high, middle, low]


def project(primal, grad, tau, upper, limited):
    value = primal - tau * grad
    capped = jnp.where(limited > 0, jnp.minimum(value, upper), value)
    return jnp.maximum(capped, 0.0)


def touch_body(part, after, out):
    del part, after, out


def prep_body(far, first_near, *refs):
    live, *sources = refs[: FIELDS + 3]
    far_out, *near_outs, own_out = refs[FIELDS + 3 : FIELDS + 5 + len(first_near)]
    *fields, share, index, turned, sems = refs[FIELDS + 5 + len(first_near) :]
    half, tile = share.shape[0], share.shape[1]
    first = lax.axis_index("rep") * half
    targets = (*fields, index)
    copies = [
        pltpu.make_async_copy(source, target, sems.at[k])
        for k, (source, target) in enumerate(zip(sources[:-1], targets))
    ]
    copies.append(pltpu.make_async_copy(sources[-1].at[0, 0, pl.ds(first, half)], share, sems.at[FIELDS + 1]))
    for copy in copies:
        copy.start()
    part = (own_out.shape[0] - INFO) // FIELDS
    nslots = index.shape[-1]
    rows = []
    for j, field in enumerate(fields):
        copies[j].wait()
        values = field[...]
        if j < 2:
            rows += split_parts(jnp.sum(values * values, axis=0, keepdims=True))
        turned[j] = values.T.astype(BF16)
    for copy in copies[FIELDS:]:
        copy.wait()
    lane = lax.broadcasted_iota(jnp.int32, (1, tile), 1)
    row = jnp.where(lane == nslots, live[0, 0].astype(F32), 0.0)
    for k in range(nslots):
        row = jnp.where(lane == k, index[0, 0, k].astype(F32), row)
    rows += [row, jnp.zeros((INFO - len(rows) - 1, tile), F32)]
    info = jnp.concatenate(rows, axis=0).astype(BF16)
    me_b = lax.axis_index("blk")

    def piece(out, at, t):
        rows = pl.ds(pl.multiple_of((me_b ^ t) * part, part), part)
        for j in range(FIELDS):
            out[at + j * part : at + (j + 1) * part, :] = turned[j, rows, :]

    top = half * tile
    for out in (far_out, *near_outs):
        for k in range(half):
            out[k * tile : (k + 1) * tile, :] = share[k]
    for t in range(far):
        piece(far_out, top + t * FIELDS * part, far + t)
    for out, (t, _) in zip(near_outs, first_near):
        piece(out, top, t)
    piece(own_out, 0, 0)
    for out in (far_out, *near_outs, own_out):
        out[out.shape[0] - INFO :, :] = info


def relay_body(top, part, came, *outs):
    for t, out in enumerate(outs):
        out[0:top, :] = came[0:top, :]
        at = top + t * FIELDS * part
        out[top : top + FIELDS * part, :] = came[at : at + FIELDS * part, :]
        out[top + FIELDS * part :, :] = came[came.shape[0] - INFO :, :]


def place(n_blk, n_col, mat, slots, source, shift, slot, block, nslots):
    tile = block.shape[-1]
    blk, col = lax.axis_index("blk") ^ shift[0], lax.axis_index("col") ^ shift[1]
    position = slots[source, slot]
    row = pl.multiple_of((blk * n_col + position // n_blk) * tile, tile)
    column = pl.multiple_of(((position % n_blk) * n_col + col) * tile, tile)

    @pl.when(slot < slots[source, nslots])
    def _():
        mat[pl.ds(row, tile), pl.ds(column, tile)] = block[...]


def place_share(n_blk, n_col, mat, slots, source, shift, share, core, nslots):
    half = nslots // 2
    tile = share.shape[1]
    for k in range(half):
        block = share.at[k * tile : (k + 1) * tile, :]
        place(n_blk, n_col, mat, slots, source, shift, core * half + k, block, nslots)


def take(n_col, fields, shift, ref, at):
    part, tile = fields.shape[1], ref.shape[1]
    blk, col = lax.axis_index("blk") ^ shift[0], lax.axis_index("col") ^ shift[1]
    lanes = pl.ds(pl.multiple_of((blk * n_col + col) * tile, tile), tile)
    for j in range(FIELDS):
        fields[j, :, lanes] = ref[at + j * part : at + (j + 1) * part, :]
    info = ref[ref.shape[0] - INFO :, :].astype(F32)
    sums = []
    for j in range(2):
        first, second, third = (info[PARTS * j + k : PARTS * j + k + 1] for k in range(PARTS))
        sums.append((first + second) + third)
    return sums


def early_body(n_blk, n_col, shifts, slots, blocks_in, own, *refs):
    count = len(shifts)
    mine, theirs = refs[:count], refs[count : 2 * count]
    mat, fields, sums_out, blocks, sem = refs[2 * count :]
    copy = pltpu.make_async_copy(blocks_in, blocks, sem)
    copy.start()
    nslots = blocks.shape[2]
    core = lax.axis_index("rep")
    mat[...] = jnp.zeros(mat.shape, BF16)
    fields[...] = jnp.zeros(fields.shape, BF16)
    sums = take(n_col, fields, (0, 0), own, 0)
    for m, (shift, own_part, other_part) in enumerate(zip(shifts, mine, theirs)):
        place_share(n_blk, n_col, mat, slots, m + 1, shift, own_part, core, nslots)
        place_share(n_blk, n_col, mat, slots, m + 1, shift, other_part, 1 - core, nslots)
        more = take(n_col, fields, shift, own_part, nslots // 2 * own_part.shape[1])
        sums = [a + b for a, b in zip(sums, more)]
    copy.wait()
    for k in range(nslots):
        place(n_blk, n_col, mat, slots, 0, (0, 0), k, blocks.at[0, 0, k], nslots)
    sums_out[...] = jnp.concatenate(sums + [jnp.zeros((6, own.shape[1]), F32)], axis=0)


def relayed_body(n_blk, n_col, shifts, nslots, slots, bounded, mat, fields, sums_in, *refs):
    mine = refs[: len(shifts)]
    scales, own, _, _, turned = refs[len(shifts) :]
    part, tile = fields.shape[1], mine[0].shape[1]
    sums = [sums_in[0:1, :], sums_in[1:2, :]]
    for m, (shift, own_part) in enumerate(zip(shifts, mine)):
        place_share(n_blk, n_col, mat, slots, m, shift, own_part, lax.axis_index("rep"), nslots)
        more = take(n_col, fields, shift, own_part, nslots // 2 * tile)
        sums = [a + b for a, b in zip(sums, more)]
    weight = jnp.sqrt(sums[0] + EPS) / jnp.sqrt(sums[1] + EPS)
    rows = jnp.concatenate([ETA / weight, ETA * weight, bounded[...].astype(F32), jnp.zeros((5, tile), F32)], axis=0)
    scales[...] = rows
    turned[...] = jnp.concatenate([rows, jnp.zeros((tile - 8, tile), F32)], axis=0).T
    own[...] = turned[pl.ds(pl.multiple_of(lax.axis_index("blk") * part, part), part), :]


def main_body(n_blk, n_col, shifts, nslots, slots, mat, fields, own, *refs):
    theirs = refs[: len(shifts)]
    *outs, _, products = refs[len(shifts) :]
    part, tile = fields.shape[1], theirs[0].shape[1]
    me_b, me_c = lax.axis_index("blk"), lax.axis_index("col")
    for m, (shift, other_part) in enumerate(zip(shifts, theirs)):
        place_share(n_blk, n_col, mat, slots, m, shift, other_part, 1 - lax.axis_index("rep"), nslots)
    cost, rhs, upper, primal, dual = (fields[j].astype(F32) for j in range(FIELDS))
    tau, sigma, limited = own[:, 0:1], own[:, 1:2], own[:, 2:3]
    for step in range(ITERS):
        kty = jnp.dot(dual.astype(BF16), mat[...], preferred_element_type=F32)
        products[2 * step] = kty.astype(BF16)
        x_new = project(primal, cost - kty, tau, upper, limited)
        xbar = (2.0 * x_new - primal).astype(BF16)
        primal = x_new
        kx = lax.dot_general(xbar, mat[...], (((1,), (1,)), ((), ())), preferred_element_type=F32)
        products[2 * step + 1] = kx.astype(BF16)
        dual = jnp.maximum(dual + sigma * (rhs - kx), 0.0)
    for t, out in enumerate(outs):
        lanes = pl.ds(pl.multiple_of(((me_b ^ t) * n_col + me_c) * tile, tile), tile)
        for j in range(2 * ITERS):
            out[j * part : (j + 1) * part, :] = products[j, :, lanes]


def final_body(order, *refs):
    parts = refs[: len(order)]
    scales, cost, rhs, upper, x_in, y_in, bounded, x_out, y_out, products = refs[len(order) :]
    part = parts[0].shape[0] // (2 * ITERS)
    me_b = lax.axis_index("blk")
    for t, recv in zip(order, parts):
        rows = pl.ds(pl.multiple_of((me_b ^ t) * part, part), part)
        for j in range(2 * ITERS):
            products[j, rows, :] = recv[j * part : (j + 1) * part, :]

    def turned(j):
        return products[j].astype(F32).T

    tau, sigma = scales[0:1, :], scales[1:2, :]
    primal, dual = x_in[...], y_in[...]
    for step in range(ITERS):
        primal = project(primal, cost[...] - turned(2 * step), tau, upper[...], bounded[...])
        dual = jnp.maximum(dual + sigma * (rhs[...] - turned(2 * step + 1)), 0.0)
    x_out[...] = primal
    y_out[...] = dual


def local_plan(blocks, block_index, live, cost, rhs, upper, x_init, y_init, bounded):
    n_blk, n_col = lax.axis_size("blk"), lax.axis_size("col")
    n = n_blk * n_col
    tile, nslots = blocks.shape[-1], blocks.shape[2]
    scn = cost.shape[1]
    part = scn // n_blk
    like = jax.ShapeDtypeStruct
    limits = bounded[None, :]

    def move(value, t, s):
        pairs = [(b * n_col + c, (b ^ t) * n_col + (c ^ s)) for b in range(n_blk) for c in range(n_col)]
        return lax.ppermute(value, ("blk", "col"), pairs)

    far = n_blk // 2
    near = [(t, s) for t in range(far) for s in range(n_col) if (t, s) != (0, 0)]
    half = nslots // 2
    top = half * tile
    size = top + FIELDS * part + INFO
    first_near = [(0, s) for s in range(1, n_col)] + [(t, 0) for t in range(1, far)]
    far_out, *near_outs, own = call(
        functools.partial(prep_body, far, first_near),
        [held((top + FIELDS * far * part + INFO, tile), BF16)]
        + [held((size, tile), BF16)] * len(first_near)
        + [held((size - top, tile), BF16)],
        [SMEM] + [ANY] * (FIELDS + 2),
        [live] + pinned([cost, rhs, upper, x_init, y_init, block_index, blocks]),
        scratch=[pltpu.VMEM((tile, scn), F32)] * FIELDS
        + [pltpu.VMEM((half, tile, tile), BF16)]
        + [pltpu.SMEM(block_index.shape, jnp.int32)]
        + [pltpu.VMEM((FIELDS, scn, tile), BF16), pltpu.SemaphoreType.DMA((FIELDS + 2,))],
    )

    def other_core(values):
        return [lax.ppermute(v[:top], "rep", [(0, 1), (1, 0)]) for v in values]

    def slots_of(values):
        rows = [v[v.shape[0] - INFO + SLOT_ROW, : nslots + 1] for v in values]
        return jnp.stack(rows).astype(jnp.int32)

    early = {(far, 0): move(far_out, far, 0)}
    for (t, s), out in zip(first_near, near_outs):
        early[t, s] = move(out, t, s)
    for t in range(1, far):
        for s in range(1, n_col):
            early[t, s] = move(early[t, 0], 0, s)
    relayed = call(
        functools.partial(relay_body, top, part), [held((size, tile), BF16)] * far, [VMEM], [early[far, 0]]
    )
    late = {(far + t, s): move(relayed[t], t, s) for t, s in near}
    shifts, mine = list(early), list(early.values())
    mat, fields, sums = call(
        functools.partial(early_body, n_blk, n_col, shifts),
        [held((n * tile, n * tile), BF16), held((FIELDS, part, n * tile), BF16), held((8, scn), F32)],
        [SMEM, ANY] + [VMEM] * (1 + 2 * len(mine)),
        [slots_of([own] + mine), *pinned([blocks]), own] + mine + other_core(mine),
        scratch=[pltpu.VMEM(blocks.shape, BF16), pltpu.SemaphoreType.DMA],
    )
    last = list(late)[-1]
    late[last] = call(touch_body, [held(late[last].shape, BF16)], [ANY, ANY], [late[last], sums], aliases={0: 0}, spec=ANY)[0]
    shifts, mine = list(late), list(late.values())
    slots = slots_of(mine)
    scales, own_scales, mat, fields = call(
        functools.partial(relayed_body, n_blk, n_col, shifts, nslots),
        [held((8, scn), F32), held((part, tile), F32), held(mat.shape, BF16), held(fields.shape, BF16)],
        [SMEM] + [VMEM] * (4 + len(mine)),
        [slots, limits, mat, fields, sums] + mine,
        scratch=[pltpu.VMEM((tile, scn), F32)],
        aliases={2: 2, 3: 3},
    )
    *products, _ = call(
        functools.partial(main_body, n_blk, n_col, shifts, nslots),
        [held((2 * ITERS * part, tile), BF16)] * n_blk + [held(mat.shape, BF16)],
        [SMEM] + [VMEM] * (3 + len(mine)),
        [slots, mat, fields, own_scales] + other_core(mine),
        scratch=[pltpu.VMEM((2 * ITERS, part, n * tile), BF16)],
        flops=4 * ITERS * n * n * tile * tile * part,
        aliases={1: n_blk},
    )
    order = [0, *range(n_blk - 1, 0, -1)]
    parts = [products[t] if t == 0 else move(products[t], t, 0) for t in order]
    return call(
        functools.partial(final_body, order),
        [like((tile, scn), F32)] * 2,
        [VMEM] * (n_blk + FIELDS + 2),
        parts + [scales, cost, rhs, upper, x_init, y_init, limits],
        scratch=[pltpu.VMEM((2 * ITERS, scn, tile), BF16)],
    )


def project_box(value, upper, bounded):
    capped = jnp.where(bounded[None, :] > 0, jnp.minimum(value, upper), value)
    return jnp.maximum(capped, 0.0)


def collectives_plan(blocks, block_index, live, cost, rhs, upper, x_init, y_init, bounded):
    block_mats = blocks[0, 0]
    slots = block_index[0, 0]
    n_blk = lax.axis_size("blk")
    n_col = lax.axis_size("col")
    tile_size = block_mats.shape[1]
    scn_count = cost.shape[1]
    row_block = slots // n_blk
    col_block = slots % n_blk
    keep_mask = (jnp.arange(slots.shape[0]) < live[0, 0]).astype(jnp.float32)[:, None, None]
    totals = lax.psum((jnp.sum(cost * cost, axis=0), jnp.sum(rhs * rhs, axis=0)), ("blk", "col"))
    weight = jnp.sqrt(totals[0] + EPS) / jnp.sqrt(totals[1] + EPS)
    tau = (ETA / weight)[None, :]
    sigma = (ETA * weight)[None, :]
    primal = x_init
    dual = y_init
    for step in range(ITERS):
        gathered = lax.all_gather(dual.astype(jnp.bfloat16), "col", axis=0, tiled=True)
        pieces = gathered.reshape(n_col, tile_size, scn_count)[row_block]
        products = (
            jnp.einsum("bkt,bks->bts", block_mats, pieces, preferred_element_type=jnp.float32)
            * keep_mask
        )
        cols = jnp.zeros((n_blk, tile_size, scn_count), jnp.float32).at[col_block].add(products)
        kty = lax.psum_scatter(
            cols.reshape(n_blk * tile_size, scn_count).astype(jnp.bfloat16),
            "blk",
            scatter_dimension=0,
            tiled=True,
        ).astype(jnp.float32)
        x_new = project_box(primal - tau * (cost - kty), upper, bounded)
        xbar = (2.0 * x_new - primal).astype(jnp.bfloat16)
        whole = lax.all_gather(xbar, "blk", axis=0, tiled=True)
        primal = x_new
        row_pieces = whole.reshape(n_blk, tile_size, scn_count)[col_block]
        row_products = (
            jnp.einsum("bkt,bts->bks", block_mats, row_pieces, preferred_element_type=jnp.float32)
            * keep_mask
        )
        rows = jnp.zeros((n_col, tile_size, scn_count), jnp.float32).at[row_block].add(row_products)
        terms = rows.reshape(n_col * tile_size, scn_count)
        kx = lax.psum_scatter(
            terms.astype(jnp.bfloat16), "col", scatter_dimension=0, tiled=True
        ).astype(jnp.float32)
        dual = jnp.maximum(dual + sigma * (rhs - kx), 0.0)
    return (primal, dual)


def shards(*args):
    n_blk, n_col, n_rep = (lax.axis_size(axis) for axis in ("blk", "col", "rep"))
    blocks, cost = args[0], args[3]
    n, tile, nslots = n_blk * n_col, blocks.shape[-1], blocks.shape[2]
    fits = 2 * (n * tile) ** 2 <= MAX_MATRIX and cost.shape[1] % (16 * n_blk) == 0 and cost.shape[1] == tile
    even = n_blk & (n_blk - 1) == 0 and n_col & (n_col - 1) == 0 and n_blk > 1 and n_rep == 2 and nslots % 2 == 0
    x, y = (local_plan if fits and even else collectives_plan)(*args)
    return x, y


def solution(mesh):
    in_specs = (
        P("blk", "col", None, None, None),
        P("blk", "col", None),
        P("blk", "col"),
        P(("blk", "col"), ("groups", "rep")),
        P(("blk", "col"), ("groups", "rep")),
        P(("blk", "col"), ("groups", "rep")),
        P(("blk", "col"), ("groups", "rep")),
        P(("blk", "col"), ("groups", "rep")),
        P(("groups", "rep")),
    )
    out_specs = (P(("blk", "col"), ("groups", "rep")), P(("blk", "col"), ("groups", "rep")))
    return jax.shard_map(shards, mesh=mesh, in_specs=in_specs, out_specs=out_specs, check_vma=False)
```

```python
import functools
import math

import jax
import jax.numpy as jnp
from jax import lax
from jax.experimental import pallas as pl
from jax.experimental.pallas import tpu as pltpu
from jax.sharding import PartitionSpec as P

ITERS = 2


ETA = 0.4
EPS = 1e-06
MAX_MATRIX = 8 * 1024 * 1024
PARTS = 3
FIELDS = 5
SLOT_ROW = 2 * PARTS
INFO = 16

MIB = 1024 * 1024
VMEM = pl.BlockSpec(memory_space=pltpu.VMEM)
SMEM = pl.BlockSpec(memory_space=pltpu.SMEM)
ANY = pl.BlockSpec(memory_space=pl.ANY)
F32 = jnp.float32
BF16 = jnp.bfloat16


def held(shape, dtype):
    return pltpu.VMEM(shape, dtype)


def pinned(values):
    return [pltpu.with_memory_space_constraint(v, pltpu.HBM) for v in values]


def call(body, outs, in_specs, args, scratch=(), flops=0, limit=32, aliases=None, specs=None):
    nbytes = sum(math.prod(a.shape) * jnp.dtype(a.dtype).itemsize for a in list(args) + list(outs))
    return pl.pallas_call(
        body,
        out_shape=list(outs),
        in_specs=in_specs,
        out_specs=specs or [VMEM] * len(outs),
        scratch_shapes=list(scratch),
        input_output_aliases=aliases or {},
        compiler_params=pltpu.CompilerParams(vmem_limit_bytes=limit * MIB),
        cost_estimate=pl.CostEstimate(flops=flops, bytes_accessed=nbytes, transcendentals=0),
    )(*args)


def split_parts(values):
    high = values.astype(BF16).astype(F32)
    rest = values - high
    middle = rest.astype(BF16).astype(F32)
    low = (rest - middle).astype(BF16).astype(F32)
    return [high, middle, low]


def project(primal, grad, tau, upper, limited):
    value = primal - tau * grad
    capped = jnp.where(limited > 0, jnp.minimum(value, upper), value)
    return jnp.maximum(capped, 0.0)


def prep_body(far, first_near, *refs):
    live, *sources = refs[: FIELDS + 3]
    far_out, *near_outs, own_out = refs[FIELDS + 3 : FIELDS + 5 + len(first_near)]
    *fields, share, index, turned, sems = refs[FIELDS + 5 + len(first_near) :]
    half, tile = share.shape[0], share.shape[1]
    first = lax.axis_index("rep") * half
    targets = (*fields, index)
    copies = [
        pltpu.make_async_copy(source, target, sems.at[k])
        for k, (source, target) in enumerate(zip(sources[:-1], targets))
    ]
    copies.append(pltpu.make_async_copy(sources[-1].at[0, 0, pl.ds(first, half)], share, sems.at[FIELDS + 1]))
    for copy in copies:
        copy.start()
    part = (own_out.shape[0] - INFO) // FIELDS
    nslots = index.shape[-1]
    rows = []
    for j, field in enumerate(fields):
        copies[j].wait()
        values = field[...]
        if j < 2:
            rows += split_parts(jnp.sum(values * values, axis=0, keepdims=True))
        turned[j] = values.T.astype(BF16)
    for copy in copies[FIELDS:]:
        copy.wait()
    lane = lax.broadcasted_iota(jnp.int32, (1, tile), 1)
    row = jnp.where(lane == nslots, live[0, 0].astype(F32), 0.0)
    for k in range(nslots):
        row = jnp.where(lane == k, index[0, 0, k].astype(F32), row)
    rows += [row, jnp.zeros((INFO - len(rows) - 1, tile), F32)]
    info = jnp.concatenate(rows, axis=0).astype(BF16)
    me_b = lax.axis_index("blk")

    def piece(out, at, t):
        rows = pl.ds(pl.multiple_of((me_b ^ t) * part, part), part)
        for j in range(FIELDS):
            out[at + j * part : at + (j + 1) * part, :] = turned[j, rows, :]

    top = half * tile
    for out in (far_out, *near_outs):
        for k in range(half):
            out[k * tile : (k + 1) * tile, :] = share[k]
    for t in range(far):
        piece(far_out, top + t * FIELDS * part, far + t)
    for out, (t, _) in zip(near_outs, first_near):
        piece(out, top, t)
    piece(own_out, 0, 0)
    for out in (far_out, *near_outs, own_out):
        out[out.shape[0] - INFO :, :] = info


def relay_body(top, part, came, after, *outs):
    del after
    for t, out in enumerate(outs):
        out[0:top, :] = came[0:top, :]
        at = top + t * FIELDS * part
        out[top : top + FIELDS * part, :] = came[at : at + FIELDS * part, :]
        out[top + FIELDS * part :, :] = came[came.shape[0] - INFO :, :]


def place(n_blk, n_col, mat, slots, source, shift, slot, block, nslots):
    tile = block.shape[-1]
    blk, col = lax.axis_index("blk") ^ shift[0], lax.axis_index("col") ^ shift[1]
    position = slots[source, slot]
    row = pl.multiple_of((blk * n_col + position // n_blk) * tile, tile)
    column = pl.multiple_of(((position % n_blk) * n_col + col) * tile, tile)

    @pl.when(slot < slots[source, nslots])
    def _():
        mat[pl.ds(row, tile), pl.ds(column, tile)] = block[...]


def place_shares(n_blk, n_col, mat, slots, source, shift, own_part, other_part, nslots):
    half = nslots // 2
    tile = own_part.shape[1]
    core = lax.axis_index("rep")
    for part, which in ((own_part, core), (other_part, 1 - core)):
        for k in range(half):
            block = part.at[k * tile : (k + 1) * tile, :]
            place(n_blk, n_col, mat, slots, source, shift, which * half + k, block, nslots)


def take(n_col, fields, shift, ref, at):
    part, tile = fields.shape[1], ref.shape[1]
    blk, col = lax.axis_index("blk") ^ shift[0], lax.axis_index("col") ^ shift[1]
    lanes = pl.ds(pl.multiple_of((blk * n_col + col) * tile, tile), tile)
    for j in range(FIELDS):
        fields[j, :, lanes] = ref[at + j * part : at + (j + 1) * part, :]
    info = ref[ref.shape[0] - INFO :, :].astype(F32)
    sums = []
    for j in range(2):
        first, second, third = (info[PARTS * j + k : PARTS * j + k + 1] for k in range(PARTS))
        sums.append((first + second) + third)
    return sums


def base_body(n_blk, n_col, slots, blocks_in, own, mat, fields, sums_out, blocks, sem):
    copy = pltpu.make_async_copy(blocks_in, blocks, sem)
    copy.start()
    nslots = blocks.shape[2]
    mat[...] = jnp.zeros(mat.shape, BF16)
    fields[...] = jnp.zeros(fields.shape, BF16)
    sums = take(n_col, fields, (0, 0), own, 0)
    sums_out[...] = jnp.concatenate(sums + [jnp.zeros((6, own.shape[1]), F32)], axis=0)
    copy.wait()
    for k in range(nslots):
        place(n_blk, n_col, mat, slots, 0, (0, 0), k, blocks.at[0, 0, k], nslots)


def early_body(n_blk, n_col, shifts, nslots, slots, late_slots, mat, fields, sums_in, *refs):
    count = len(shifts)
    mine, theirs = refs[:count], refs[count : 2 * count]
    _, _, sums_out, slots_out = refs[2 * count :]
    for source in range(slots_out.shape[0]):
        for k in range(slots_out.shape[1]):
            slots_out[source, k] = late_slots[source, k]
    sums = [sums_in[0:1, :], sums_in[1:2, :]]
    for m, (shift, own_part, other_part) in enumerate(zip(shifts, mine, theirs)):
        place_shares(n_blk, n_col, mat, slots, m, shift, own_part, other_part, nslots)
        more = take(n_col, fields, shift, own_part, nslots // 2 * own_part.shape[1])
        sums = [a + b for a, b in zip(sums, more)]
    sums_out[...] = jnp.concatenate(sums + [jnp.zeros((6, sums_in.shape[1]), F32)], axis=0)


def main_body(n_blk, n_col, shifts, nslots, slots, bounded, mat, fields, sums_in, *refs):
    count = len(shifts)
    mine, theirs = refs[:count], refs[count : 2 * count]
    *outs, scales, _, _, products, turned = refs[2 * count :]
    part, tile = fields.shape[1], mine[0].shape[1]
    me_b, me_c = lax.axis_index("blk"), lax.axis_index("col")
    sums = [sums_in[0:1, :], sums_in[1:2, :]]
    for m, (shift, own_part, other_part) in enumerate(zip(shifts, mine, theirs)):
        place_shares(n_blk, n_col, mat, slots, m, shift, own_part, other_part, nslots)
        more = take(n_col, fields, shift, own_part, nslots // 2 * tile)
        sums = [a + b for a, b in zip(sums, more)]
    cost, rhs, upper, primal, dual = (fields[j].astype(F32) for j in range(FIELDS))
    weight = jnp.sqrt(sums[0] + EPS) / jnp.sqrt(sums[1] + EPS)
    rows = jnp.concatenate([ETA / weight, ETA * weight, bounded[...].astype(F32), jnp.zeros((5, tile), F32)], axis=0)
    scales[...] = rows
    turned[...] = jnp.concatenate([rows, jnp.zeros((tile - 8, tile), F32)], axis=0).T
    own = turned[pl.ds(pl.multiple_of(me_b * part, part), part), :]
    tau, sigma, limited = own[:, 0:1], own[:, 1:2], own[:, 2:3]

    for step in range(ITERS):
        kty = jnp.dot(dual.astype(BF16), mat[...], preferred_element_type=F32)
        products[2 * step] = kty.astype(BF16)
        x_new = project(primal, cost - kty, tau, upper, limited)
        xbar = (2.0 * x_new - primal).astype(BF16)
        primal = x_new
        kx = lax.dot_general(xbar, mat[...], (((1,), (1,)), ((), ())), preferred_element_type=F32)
        products[2 * step + 1] = kx.astype(BF16)
        dual = jnp.maximum(dual + sigma * (rhs - kx), 0.0)
    for t, out in enumerate(outs):
        lanes = pl.ds(pl.multiple_of(((me_b ^ t) * n_col + me_c) * tile, tile), tile)
        for j in range(2 * ITERS):
            out[j * part : (j + 1) * part, :] = products[j, :, lanes]


def final_body(order, *refs):
    parts = refs[: len(order)]
    scales, cost, rhs, upper, x_in, y_in, bounded, x_out, y_out, products = refs[len(order) :]
    part = parts[0].shape[0] // (2 * ITERS)
    me_b = lax.axis_index("blk")
    for t, recv in zip(order, parts):
        rows = pl.ds(pl.multiple_of((me_b ^ t) * part, part), part)
        for j in range(2 * ITERS):
            products[j, rows, :] = recv[j * part : (j + 1) * part, :]

    def turned(j):
        return products[j].astype(F32).T

    tau, sigma = scales[0:1, :], scales[1:2, :]
    primal, dual = x_in[...], y_in[...]
    for step in range(ITERS):
        primal = project(primal, cost[...] - turned(2 * step), tau, upper[...], bounded[...])
        dual = jnp.maximum(dual + sigma * (rhs[...] - turned(2 * step + 1)), 0.0)
    x_out[...] = primal
    y_out[...] = dual


def local_plan(blocks, block_index, live, cost, rhs, upper, x_init, y_init, bounded):
    n_blk, n_col = lax.axis_size("blk"), lax.axis_size("col")
    n = n_blk * n_col
    tile, nslots = blocks.shape[-1], blocks.shape[2]
    scn = cost.shape[1]
    part = scn // n_blk
    like = jax.ShapeDtypeStruct
    limits = bounded[None, :]

    def move(value, t, s):
        pairs = [(b * n_col + c, (b ^ t) * n_col + (c ^ s)) for b in range(n_blk) for c in range(n_col)]
        return lax.ppermute(value, ("blk", "col"), pairs)

    far = n_blk // 2
    near = [(t, s) for t in range(far) for s in range(n_col) if (t, s) != (0, 0)]
    half = nslots // 2
    top = half * tile
    size = top + FIELDS * part + INFO
    first_near = [(0, s) for s in range(1, n_col)] + [(t, 0) for t in range(1, far)]
    far_out, *near_outs, own = call(
        functools.partial(prep_body, far, first_near),
        [held((top + FIELDS * far * part + INFO, tile), BF16)]
        + [held((size, tile), BF16)] * len(first_near)
        + [held((size - top, tile), BF16)],
        [SMEM] + [ANY] * (FIELDS + 2),
        [live] + pinned([cost, rhs, upper, x_init, y_init, block_index, blocks]),
        scratch=[pltpu.VMEM((tile, scn), F32)] * FIELDS
        + [pltpu.VMEM((half, tile, tile), BF16)]
        + [pltpu.SMEM(block_index.shape, jnp.int32)]
        + [pltpu.VMEM((FIELDS, scn, tile), BF16), pltpu.SemaphoreType.DMA((FIELDS + 2,))],
    )

    def other_core(values):
        return [lax.ppermute(v[:top], "rep", [(0, 1), (1, 0)]) for v in values]

    def slots_of(values):
        rows = [v[v.shape[0] - INFO + SLOT_ROW, : nslots + 1] for v in values]
        return jnp.stack(rows).astype(jnp.int32)

    early = {(far, 0): move(far_out, far, 0)}
    for (t, s), out in zip(first_near, near_outs):
        early[t, s] = move(out, t, s)
    for t in range(1, far):
        for s in range(1, n_col):
            early[t, s] = move(early[t, 0], 0, s)
    mat, fields, sums = call(
        functools.partial(base_body, n_blk, n_col),
        [held((n * tile, n * tile), BF16), held((FIELDS, part, n * tile), BF16), held((8, scn), F32)],
        [SMEM, ANY, VMEM],
        [slots_of([own]), *pinned([blocks]), own],
        scratch=[pltpu.VMEM(blocks.shape, BF16), pltpu.SemaphoreType.DMA],
    )
    relayed = call(
        functools.partial(relay_body, top, part),
        [held((size, tile), BF16)] * far,
        [VMEM, VMEM],
        [early[far, 0], sums],
    )
    late = {(far + t, s): move(relayed[t], t, s) for t, s in near}
    shifts, mine = list(early), list(early.values())
    late_slots = slots_of(list(late.values()))
    mat, fields, sums, late_slots = call(
        functools.partial(early_body, n_blk, n_col, shifts, nslots),
        [held(mat.shape, BF16), held(fields.shape, BF16), held((8, scn), F32)]
        + [pltpu.SMEM(late_slots.shape, jnp.int32)],
        [SMEM, SMEM] + [VMEM] * (3 + 2 * len(mine)),
        [slots_of(mine), late_slots, mat, fields, sums] + mine + other_core(mine),
        specs=[VMEM] * 3 + [SMEM],
        aliases={2: 0, 3: 1},
    )
    shifts, mine = list(late), list(late.values())
    *products, scales, _, _ = call(
        functools.partial(main_body, n_blk, n_col, shifts, nslots),
        [held((2 * ITERS * part, tile), BF16)] * n_blk
        + [like((8, scn), F32), held(mat.shape, BF16), held(fields.shape, BF16)],
        [SMEM] + [VMEM] * (4 + 2 * len(mine)),
        [late_slots, limits, mat, fields, sums] + mine + other_core(mine),
        scratch=[pltpu.VMEM((2 * ITERS, part, n * tile), BF16), pltpu.VMEM((tile, scn), F32)],
        flops=4 * ITERS * n * n * tile * tile * part,
        aliases={2: n_blk + 1, 3: n_blk + 2},
    )
    order = [0, *range(n_blk - 1, 0, -1)]
    parts = [products[t] if t == 0 else move(products[t], t, 0) for t in order]
    return call(
        functools.partial(final_body, order),
        [like((tile, scn), F32)] * 2,
        [VMEM] * (n_blk + FIELDS + 2),
        parts + [scales, cost, rhs, upper, x_init, y_init, limits],
        scratch=[pltpu.VMEM((2 * ITERS, scn, tile), BF16)],
    )


def project_box(value, upper, bounded):
    capped = jnp.where(bounded[None, :] > 0, jnp.minimum(value, upper), value)
    return jnp.maximum(capped, 0.0)


def collectives_plan(blocks, block_index, live, cost, rhs, upper, x_init, y_init, bounded):
    block_mats = blocks[0, 0]
    slots = block_index[0, 0]
    n_blk = lax.axis_size("blk")
    n_col = lax.axis_size("col")
    tile_size = block_mats.shape[1]
    scn_count = cost.shape[1]
    row_block = slots // n_blk
    col_block = slots % n_blk
    keep_mask = (jnp.arange(slots.shape[0]) < live[0, 0]).astype(jnp.float32)[:, None, None]
    totals = lax.psum((jnp.sum(cost * cost, axis=0), jnp.sum(rhs * rhs, axis=0)), ("blk", "col"))
    weight = jnp.sqrt(totals[0] + EPS) / jnp.sqrt(totals[1] + EPS)
    tau = (ETA / weight)[None, :]
    sigma = (ETA * weight)[None, :]
    primal = x_init
    dual = y_init
    for step in range(ITERS):
        gathered = lax.all_gather(dual.astype(jnp.bfloat16), "col", axis=0, tiled=True)
        pieces = gathered.reshape(n_col, tile_size, scn_count)[row_block]
        products = (
            jnp.einsum("bkt,bks->bts", block_mats, pieces, preferred_element_type=jnp.float32)
            * keep_mask
        )
        cols = jnp.zeros((n_blk, tile_size, scn_count), jnp.float32).at[col_block].add(products)
        kty = lax.psum_scatter(
            cols.reshape(n_blk * tile_size, scn_count).astype(jnp.bfloat16),
            "blk",
            scatter_dimension=0,
            tiled=True,
        ).astype(jnp.float32)
        x_new = project_box(primal - tau * (cost - kty), upper, bounded)
        xbar = (2.0 * x_new - primal).astype(jnp.bfloat16)
        whole = lax.all_gather(xbar, "blk", axis=0, tiled=True)
        primal = x_new
        row_pieces = whole.reshape(n_blk, tile_size, scn_count)[col_block]
        row_products = (
            jnp.einsum("bkt,bts->bks", block_mats, row_pieces, preferred_element_type=jnp.float32)
            * keep_mask
        )
        rows = jnp.zeros((n_col, tile_size, scn_count), jnp.float32).at[row_block].add(row_products)
        terms = rows.reshape(n_col * tile_size, scn_count)
        kx = lax.psum_scatter(
            terms.astype(jnp.bfloat16), "col", scatter_dimension=0, tiled=True
        ).astype(jnp.float32)
        dual = jnp.maximum(dual + sigma * (rhs - kx), 0.0)
    return (primal, dual)


def shards(*args):
    n_blk, n_col, n_rep = (lax.axis_size(axis) for axis in ("blk", "col", "rep"))
    blocks, cost = args[0], args[3]
    n, tile, nslots = n_blk * n_col, blocks.shape[-1], blocks.shape[2]
    fits = 2 * (n * tile) ** 2 <= MAX_MATRIX and cost.shape[1] % (16 * n_blk) == 0 and cost.shape[1] == tile
    even = n_blk & (n_blk - 1) == 0 and n_col & (n_col - 1) == 0 and n_blk > 1 and n_rep == 2 and nslots % 2 == 0
    x, y = (local_plan if fits and even else collectives_plan)(*args)
    return x, y


def solution(mesh):
    in_specs = (
        P("blk", "col", None, None, None),
        P("blk", "col", None),
        P("blk", "col"),
        P(("blk", "col"), ("groups", "rep")),
        P(("blk", "col"), ("groups", "rep")),
        P(("blk", "col"), ("groups", "rep")),
        P(("blk", "col"), ("groups", "rep")),
        P(("blk", "col"), ("groups", "rep")),
        P(("groups", "rep")),
    )
    out_specs = (P(("blk", "col"), ("groups", "rep")), P(("blk", "col"), ("groups", "rep")))
    return jax.shard_map(shards, mesh=mesh, in_specs=in_specs, out_specs=out_specs, check_vma=False)
```

```python
import functools
import math

import jax
import jax.numpy as jnp
from jax import lax
from jax.experimental import pallas as pl
from jax.experimental.pallas import tpu as pltpu
from jax.sharding import PartitionSpec as P

ITERS = 2


ETA = 0.4
EPS = 1e-06
MAX_MATRIX = 8 * 1024 * 1024
PARTS = 3
FIELDS = 5
SLOT_ROW = 2 * PARTS
INFO = 16

MIB = 1024 * 1024
VMEM = pl.BlockSpec(memory_space=pltpu.VMEM)
SMEM = pl.BlockSpec(memory_space=pltpu.SMEM)
ANY = pl.BlockSpec(memory_space=pl.ANY)
F32 = jnp.float32
BF16 = jnp.bfloat16


def held(shape, dtype):
    return pltpu.VMEM(shape, dtype)


def pinned(values):
    return [pltpu.with_memory_space_constraint(v, pltpu.HBM) for v in values]


def call(body, outs, in_specs, args, scratch=(), flops=0, limit=32, aliases=None, specs=None):
    nbytes = sum(math.prod(a.shape) * jnp.dtype(a.dtype).itemsize for a in list(args) + list(outs))
    return pl.pallas_call(
        body,
        out_shape=list(outs),
        in_specs=in_specs,
        out_specs=specs or [VMEM] * len(outs),
        scratch_shapes=list(scratch),
        input_output_aliases=aliases or {},
        compiler_params=pltpu.CompilerParams(vmem_limit_bytes=limit * MIB),
        cost_estimate=pl.CostEstimate(flops=flops, bytes_accessed=nbytes, transcendentals=0),
    )(*args)


def split_parts(values):
    high = values.astype(BF16).astype(F32)
    rest = values - high
    middle = rest.astype(BF16).astype(F32)
    low = (rest - middle).astype(BF16).astype(F32)
    return [high, middle, low]


def project(primal, grad, tau, upper, limited):
    value = primal - tau * grad
    capped = jnp.where(limited > 0, jnp.minimum(value, upper), value)
    return jnp.maximum(capped, 0.0)


def touch_body(part, after, out):
    del part, after, out


def prep_body(far, first_near, *refs):
    live, *sources = refs[: FIELDS + 3]
    far_out, *near_outs, own_out = refs[FIELDS + 3 : FIELDS + 5 + len(first_near)]
    *fields, share, index, turned, sems = refs[FIELDS + 5 + len(first_near) :]
    half, tile = share.shape[0], share.shape[1]
    first = lax.axis_index("rep") * half
    targets = (*fields, index)
    copies = [
        pltpu.make_async_copy(source, target, sems.at[k])
        for k, (source, target) in enumerate(zip(sources[:-1], targets))
    ]
    copies.append(pltpu.make_async_copy(sources[-1].at[0, 0, pl.ds(first, half)], share, sems.at[FIELDS + 1]))
    for copy in copies:
        copy.start()
    part = (own_out.shape[0] - INFO) // FIELDS
    nslots = index.shape[-1]
    rows = []
    for j, field in enumerate(fields):
        copies[j].wait()
        values = field[...]
        if j < 2:
            rows += split_parts(jnp.sum(values * values, axis=0, keepdims=True))
        turned[j] = values.T.astype(BF16)
    for copy in copies[FIELDS:]:
        copy.wait()
    lane = lax.broadcasted_iota(jnp.int32, (1, tile), 1)
    row = jnp.where(lane == nslots, live[0, 0].astype(F32), 0.0)
    for k in range(nslots):
        row = jnp.where(lane == k, index[0, 0, k].astype(F32), row)
    rows += [row, jnp.zeros((INFO - len(rows) - 1, tile), F32)]
    info = jnp.concatenate(rows, axis=0).astype(BF16)
    me_b = lax.axis_index("blk")

    def piece(out, at, t):
        rows = pl.ds(pl.multiple_of((me_b ^ t) * part, part), part)
        for j in range(FIELDS):
            out[at + j * part : at + (j + 1) * part, :] = turned[j, rows, :]

    top = half * tile
    for out in (far_out, *near_outs):
        for k in range(half):
            out[k * tile : (k + 1) * tile, :] = share[k]
    for t in range(far):
        piece(far_out, top + t * FIELDS * part, far + t)
    for out, (t, _) in zip(near_outs, first_near):
        piece(out, top, t)
    piece(own_out, 0, 0)
    for out in (far_out, *near_outs, own_out):
        out[out.shape[0] - INFO :, :] = info


def relay_body(top, part, came, after, *outs):
    del after
    for t, out in enumerate(outs):
        out[0:top, :] = came[0:top, :]
        at = top + t * FIELDS * part
        out[top : top + FIELDS * part, :] = came[at : at + FIELDS * part, :]
        out[top + FIELDS * part :, :] = came[came.shape[0] - INFO :, :]


def place(n_blk, n_col, mat, slots, source, shift, slot, block, nslots):
    tile = block.shape[-1]
    blk, col = lax.axis_index("blk") ^ shift[0], lax.axis_index("col") ^ shift[1]
    position = slots[source, slot]
    row = pl.multiple_of((blk * n_col + position // n_blk) * tile, tile)
    column = pl.multiple_of(((position % n_blk) * n_col + col) * tile, tile)

    @pl.when(slot < slots[source, nslots])
    def _():
        mat[pl.ds(row, tile), pl.ds(column, tile)] = block[...]


def place_shares(n_blk, n_col, mat, slots, source, shift, own_part, other_part, nslots):
    half = nslots // 2
    tile = own_part.shape[1]
    core = lax.axis_index("rep")
    for part, which in ((own_part, core), (other_part, 1 - core)):
        for k in range(half):
            block = part.at[k * tile : (k + 1) * tile, :]
            place(n_blk, n_col, mat, slots, source, shift, which * half + k, block, nslots)


def take(n_col, fields, shift, ref, at):
    part, tile = fields.shape[1], ref.shape[1]
    blk, col = lax.axis_index("blk") ^ shift[0], lax.axis_index("col") ^ shift[1]
    lanes = pl.ds(pl.multiple_of((blk * n_col + col) * tile, tile), tile)
    for j in range(FIELDS):
        fields[j, :, lanes] = ref[at + j * part : at + (j + 1) * part, :]
    info = ref[ref.shape[0] - INFO :, :].astype(F32)
    sums = []
    for j in range(2):
        first, second, third = (info[PARTS * j + k : PARTS * j + k + 1] for k in range(PARTS))
        sums.append((first + second) + third)
    return sums


def base_body(n_blk, n_col, slots, blocks_in, own, mat, fields, sums_out, blocks, sem):
    copy = pltpu.make_async_copy(blocks_in, blocks, sem)
    copy.start()
    nslots = blocks.shape[2]
    mat[...] = jnp.zeros(mat.shape, BF16)
    fields[...] = jnp.zeros(fields.shape, BF16)
    sums = take(n_col, fields, (0, 0), own, 0)
    sums_out[...] = jnp.concatenate(sums + [jnp.zeros((6, own.shape[1]), F32)], axis=0)
    copy.wait()
    for k in range(nslots):
        place(n_blk, n_col, mat, slots, 0, (0, 0), k, blocks.at[0, 0, k], nslots)


def early_body(n_blk, n_col, shifts, nslots, slots, late_slots, mat, fields, sums_in, *refs):
    count = len(shifts)
    mine, theirs = refs[:count], refs[count : 2 * count]
    _, _, sums_out, slots_out = refs[2 * count :]
    for source in range(slots_out.shape[0]):
        for k in range(slots_out.shape[1]):
            slots_out[source, k] = late_slots[source, k]
    sums = [sums_in[0:1, :], sums_in[1:2, :]]
    for m, (shift, own_part, other_part) in enumerate(zip(shifts, mine, theirs)):
        place_shares(n_blk, n_col, mat, slots, m, shift, own_part, other_part, nslots)
        more = take(n_col, fields, shift, own_part, nslots // 2 * own_part.shape[1])
        sums = [a + b for a, b in zip(sums, more)]
    sums_out[...] = jnp.concatenate(sums + [jnp.zeros((6, sums_in.shape[1]), F32)], axis=0)


def main_body(n_blk, n_col, shifts, nslots, slots, bounded, mat, fields, sums_in, *refs):
    count = len(shifts)
    mine, theirs = refs[:count], refs[count : 2 * count]
    *outs, scales, _, _, products, turned = refs[2 * count :]
    part, tile = fields.shape[1], mine[0].shape[1]
    me_b, me_c = lax.axis_index("blk"), lax.axis_index("col")
    sums = [sums_in[0:1, :], sums_in[1:2, :]]
    for m, (shift, own_part, other_part) in enumerate(zip(shifts, mine, theirs)):
        place_shares(n_blk, n_col, mat, slots, m, shift, own_part, other_part, nslots)
        more = take(n_col, fields, shift, own_part, nslots // 2 * tile)
        sums = [a + b for a, b in zip(sums, more)]
    cost, rhs, upper, primal, dual = (fields[j].astype(F32) for j in range(FIELDS))
    weight = jnp.sqrt(sums[0] + EPS) / jnp.sqrt(sums[1] + EPS)
    rows = jnp.concatenate([ETA / weight, ETA * weight, bounded[...].astype(F32), jnp.zeros((5, tile), F32)], axis=0)
    scales[...] = rows
    turned[...] = jnp.concatenate([rows, jnp.zeros((tile - 8, tile), F32)], axis=0).T
    own = turned[pl.ds(pl.multiple_of(me_b * part, part), part), :]
    tau, sigma, limited = own[:, 0:1], own[:, 1:2], own[:, 2:3]

    for step in range(ITERS):
        kty = jnp.dot(dual.astype(BF16), mat[...], preferred_element_type=F32)
        products[2 * step] = kty.astype(BF16)
        x_new = project(primal, cost - kty, tau, upper, limited)
        xbar = (2.0 * x_new - primal).astype(BF16)
        primal = x_new
        kx = lax.dot_general(xbar, mat[...], (((1,), (1,)), ((), ())), preferred_element_type=F32)
        products[2 * step + 1] = kx.astype(BF16)
        dual = jnp.maximum(dual + sigma * (rhs - kx), 0.0)
    for t, out in enumerate(outs):
        lanes = pl.ds(pl.multiple_of(((me_b ^ t) * n_col + me_c) * tile, tile), tile)
        for j in range(2 * ITERS):
            out[j * part : (j + 1) * part, :] = products[j, :, lanes]


def final_body(order, *refs):
    parts = refs[: len(order)]
    scales, cost, rhs, upper, x_in, y_in, bounded, x_out, y_out, products = refs[len(order) :]
    part = parts[0].shape[0] // (2 * ITERS)
    me_b = lax.axis_index("blk")
    for t, recv in zip(order, parts):
        rows = pl.ds(pl.multiple_of((me_b ^ t) * part, part), part)
        for j in range(2 * ITERS):
            products[j, rows, :] = recv[j * part : (j + 1) * part, :]

    def turned(j):
        return products[j].astype(F32).T

    tau, sigma = scales[0:1, :], scales[1:2, :]
    primal, dual = x_in[...], y_in[...]
    for step in range(ITERS):
        primal = project(primal, cost[...] - turned(2 * step), tau, upper[...], bounded[...])
        dual = jnp.maximum(dual + sigma * (rhs[...] - turned(2 * step + 1)), 0.0)
    x_out[...] = primal
    y_out[...] = dual


def local_plan(blocks, block_index, live, cost, rhs, upper, x_init, y_init, bounded):
    n_blk, n_col = lax.axis_size("blk"), lax.axis_size("col")
    n = n_blk * n_col
    tile, nslots = blocks.shape[-1], blocks.shape[2]
    scn = cost.shape[1]
    part = scn // n_blk
    like = jax.ShapeDtypeStruct
    limits = bounded[None, :]

    def move(value, t, s):
        pairs = [(b * n_col + c, (b ^ t) * n_col + (c ^ s)) for b in range(n_blk) for c in range(n_col)]
        return lax.ppermute(value, ("blk", "col"), pairs)

    far = n_blk // 2
    near = [(t, s) for t in range(far) for s in range(n_col) if (t, s) != (0, 0)]
    half = nslots // 2
    top = half * tile
    size = top + FIELDS * part + INFO
    first_near = [(0, s) for s in range(1, n_col)] + [(t, 0) for t in range(1, far)]
    far_out, *near_outs, own = call(
        functools.partial(prep_body, far, first_near),
        [held((top + FIELDS * far * part + INFO, tile), BF16)]
        + [held((size, tile), BF16)] * len(first_near)
        + [held((size - top, tile), BF16)],
        [SMEM] + [ANY] * (FIELDS + 2),
        [live] + pinned([cost, rhs, upper, x_init, y_init, block_index, blocks]),
        scratch=[pltpu.VMEM((tile, scn), F32)] * FIELDS
        + [pltpu.VMEM((half, tile, tile), BF16)]
        + [pltpu.SMEM(block_index.shape, jnp.int32)]
        + [pltpu.VMEM((FIELDS, scn, tile), BF16), pltpu.SemaphoreType.DMA((FIELDS + 2,))],
    )

    def other_core(values):
        return [lax.ppermute(v[:top], "rep", [(0, 1), (1, 0)]) for v in values]

    def slots_of(values):
        rows = [v[v.shape[0] - INFO + SLOT_ROW, : nslots + 1] for v in values]
        return jnp.stack(rows).astype(jnp.int32)

    early = {(far, 0): move(far_out, far, 0)}
    for (t, s), out in zip(first_near, near_outs):
        early[t, s] = move(out, t, s)
    for t in range(1, far):
        for s in range(1, n_col):
            early[t, s] = move(early[t, 0], 0, s)
    mat, fields, sums = call(
        functools.partial(base_body, n_blk, n_col),
        [held((n * tile, n * tile), BF16), held((FIELDS, part, n * tile), BF16), held((8, scn), F32)],
        [SMEM, ANY, VMEM],
        [slots_of([own]), *pinned([blocks]), own],
        scratch=[pltpu.VMEM(blocks.shape, BF16), pltpu.SemaphoreType.DMA],
    )
    relayed = call(
        functools.partial(relay_body, top, part),
        [held((size, tile), BF16)] * far,
        [VMEM, VMEM],
        [early[far, 0], sums],
    )
    late = {(far + t, s): move(relayed[t], t, s) for t, s in near}
    for s in range(1, n_col):
        (late[far, s],) = call(
            touch_body,
            [held((size, tile), BF16)],
            [ANY, ANY],
            [late[far, s], sums],
            specs=[ANY],
            aliases={0: 0},
            flops=2 * 10**9,
        )
    shifts, mine = list(early), list(early.values())
    late_slots = slots_of(list(late.values()))
    mat, fields, sums, late_slots = call(
        functools.partial(early_body, n_blk, n_col, shifts, nslots),
        [held(mat.shape, BF16), held(fields.shape, BF16), held((8, scn), F32)]
        + [pltpu.SMEM(late_slots.shape, jnp.int32)],
        [SMEM, SMEM] + [VMEM] * (3 + 2 * len(mine)),
        [slots_of(mine), late_slots, mat, fields, sums] + mine + other_core(mine),
        specs=[VMEM] * 3 + [SMEM],
        aliases={2: 0, 3: 1},
    )
    shifts, mine = list(late), list(late.values())
    *products, scales, _, _ = call(
        functools.partial(main_body, n_blk, n_col, shifts, nslots),
        [held((2 * ITERS * part, tile), BF16)] * n_blk
        + [like((8, scn), F32), held(mat.shape, BF16), held(fields.shape, BF16)],
        [SMEM] + [VMEM] * (4 + 2 * len(mine)),
        [late_slots, limits, mat, fields, sums] + mine + other_core(mine),
        scratch=[pltpu.VMEM((2 * ITERS, part, n * tile), BF16), pltpu.VMEM((tile, scn), F32)],
        flops=4 * ITERS * n * n * tile * tile * part,
        aliases={2: n_blk + 1, 3: n_blk + 2},
    )
    order = [0, *range(n_blk - 1, 0, -1)]
    parts = [products[t] if t == 0 else move(products[t], t, 0) for t in order]
    return call(
        functools.partial(final_body, order),
        [like((tile, scn), F32)] * 2,
        [VMEM] * (n_blk + FIELDS + 2),
        parts + [scales, cost, rhs, upper, x_init, y_init, limits],
        scratch=[pltpu.VMEM((2 * ITERS, scn, tile), BF16)],
    )


def project_box(value, upper, bounded):
    capped = jnp.where(bounded[None, :] > 0, jnp.minimum(value, upper), value)
    return jnp.maximum(capped, 0.0)


def collectives_plan(blocks, block_index, live, cost, rhs, upper, x_init, y_init, bounded):
    block_mats = blocks[0, 0]
    slots = block_index[0, 0]
    n_blk = lax.axis_size("blk")
    n_col = lax.axis_size("col")
    tile_size = block_mats.shape[1]
    scn_count = cost.shape[1]
    row_block = slots // n_blk
    col_block = slots % n_blk
    keep_mask = (jnp.arange(slots.shape[0]) < live[0, 0]).astype(jnp.float32)[:, None, None]
    totals = lax.psum((jnp.sum(cost * cost, axis=0), jnp.sum(rhs * rhs, axis=0)), ("blk", "col"))
    weight = jnp.sqrt(totals[0] + EPS) / jnp.sqrt(totals[1] + EPS)
    tau = (ETA / weight)[None, :]
    sigma = (ETA * weight)[None, :]
    primal = x_init
    dual = y_init
    for step in range(ITERS):
        gathered = lax.all_gather(dual.astype(jnp.bfloat16), "col", axis=0, tiled=True)
        pieces = gathered.reshape(n_col, tile_size, scn_count)[row_block]
        products = (
            jnp.einsum("bkt,bks->bts", block_mats, pieces, preferred_element_type=jnp.float32)
            * keep_mask
        )
        cols = jnp.zeros((n_blk, tile_size, scn_count), jnp.float32).at[col_block].add(products)
        kty = lax.psum_scatter(
            cols.reshape(n_blk * tile_size, scn_count).astype(jnp.bfloat16),
            "blk",
            scatter_dimension=0,
            tiled=True,
        ).astype(jnp.float32)
        x_new = project_box(primal - tau * (cost - kty), upper, bounded)
        xbar = (2.0 * x_new - primal).astype(jnp.bfloat16)
        whole = lax.all_gather(xbar, "blk", axis=0, tiled=True)
        primal = x_new
        row_pieces = whole.reshape(n_blk, tile_size, scn_count)[col_block]
        row_products = (
            jnp.einsum("bkt,bts->bks", block_mats, row_pieces, preferred_element_type=jnp.float32)
            * keep_mask
        )
        rows = jnp.zeros((n_col, tile_size, scn_count), jnp.float32).at[row_block].add(row_products)
        terms = rows.reshape(n_col * tile_size, scn_count)
        kx = lax.psum_scatter(
            terms.astype(jnp.bfloat16), "col", scatter_dimension=0, tiled=True
        ).astype(jnp.float32)
        dual = jnp.maximum(dual + sigma * (rhs - kx), 0.0)
    return (primal, dual)


def shards(*args):
    n_blk, n_col, n_rep = (lax.axis_size(axis) for axis in ("blk", "col", "rep"))
    blocks, cost = args[0], args[3]
    n, tile, nslots = n_blk * n_col, blocks.shape[-1], blocks.shape[2]
    fits = 2 * (n * tile) ** 2 <= MAX_MATRIX and cost.shape[1] % (16 * n_blk) == 0 and cost.shape[1] == tile
    even = n_blk & (n_blk - 1) == 0 and n_col & (n_col - 1) == 0 and n_blk > 1 and n_rep == 2 and nslots % 2 == 0
    x, y = (local_plan if fits and even else collectives_plan)(*args)
    return x, y


def solution(mesh):
    in_specs = (
        P("blk", "col", None, None, None),
        P("blk", "col", None),
        P("blk", "col"),
        P(("blk", "col"), ("groups", "rep")),
        P(("blk", "col"), ("groups", "rep")),
        P(("blk", "col"), ("groups", "rep")),
        P(("blk", "col"), ("groups", "rep")),
        P(("blk", "col"), ("groups", "rep")),
        P(("groups", "rep")),
    )
    out_specs = (P(("blk", "col"), ("groups", "rep")), P(("blk", "col"), ("groups", "rep")))
    return jax.shard_map(shards, mesh=mesh, in_specs=in_specs, out_specs=out_specs, check_vma=False)
```

```python
import functools
import math

import jax
import jax.numpy as jnp
from jax import lax
from jax.experimental import pallas as pl
from jax.experimental.pallas import tpu as pltpu
from jax.sharding import PartitionSpec as P

ITERS = 2


ETA = 0.4
EPS = 1e-06
MAX_MATRIX = 8 * 1024 * 1024
PARTS = 3
FIELDS = 5
SLOT_ROW = 2 * PARTS
INFO = 16

MIB = 1024 * 1024
VMEM = pl.BlockSpec(memory_space=pltpu.VMEM)
SMEM = pl.BlockSpec(memory_space=pltpu.SMEM)
ANY = pl.BlockSpec(memory_space=pl.ANY)
F32 = jnp.float32
BF16 = jnp.bfloat16


def held(shape, dtype):
    return pltpu.VMEM(shape, dtype)


def pinned(values):
    return [pltpu.with_memory_space_constraint(v, pltpu.HBM) for v in values]


def call(body, outs, in_specs, args, scratch=(), flops=0, limit=32, aliases=None, specs=None):
    nbytes = sum(math.prod(a.shape) * jnp.dtype(a.dtype).itemsize for a in list(args) + list(outs))
    return pl.pallas_call(
        body,
        out_shape=list(outs),
        in_specs=in_specs,
        out_specs=specs or [VMEM] * len(outs),
        scratch_shapes=list(scratch),
        input_output_aliases=aliases or {},
        compiler_params=pltpu.CompilerParams(vmem_limit_bytes=limit * MIB),
        cost_estimate=pl.CostEstimate(flops=flops, bytes_accessed=nbytes, transcendentals=0),
    )(*args)


def split_parts(values):
    high = values.astype(BF16).astype(F32)
    rest = values - high
    middle = rest.astype(BF16).astype(F32)
    low = (rest - middle).astype(BF16).astype(F32)
    return [high, middle, low]


def project(primal, grad, tau, upper, limited):
    value = primal - tau * grad
    capped = jnp.where(limited > 0, jnp.minimum(value, upper), value)
    return jnp.maximum(capped, 0.0)


def prep_body(far, first_near, *refs):
    live, *sources = refs[: FIELDS + 3]
    far_out, *near_outs, own_out = refs[FIELDS + 3 : FIELDS + 5 + len(first_near)]
    *fields, share, index, turned, sems = refs[FIELDS + 5 + len(first_near) :]
    half, tile = share.shape[0], share.shape[1]
    first = lax.axis_index("rep") * half
    targets = (*fields, index)
    copies = [
        pltpu.make_async_copy(source, target, sems.at[k])
        for k, (source, target) in enumerate(zip(sources[:-1], targets))
    ]
    copies.append(pltpu.make_async_copy(sources[-1].at[0, 0, pl.ds(first, half)], share, sems.at[FIELDS + 1]))
    for copy in copies:
        copy.start()
    part = (own_out.shape[0] - INFO) // FIELDS
    nslots = index.shape[-1]
    rows = []
    for j, field in enumerate(fields):
        copies[j].wait()
        values = field[...]
        if j < 2:
            rows += split_parts(jnp.sum(values * values, axis=0, keepdims=True))
        turned[j] = values.T.astype(BF16)
    for copy in copies[FIELDS:]:
        copy.wait()
    lane = lax.broadcasted_iota(jnp.int32, (1, tile), 1)
    row = jnp.where(lane == nslots, live[0, 0].astype(F32), 0.0)
    for k in range(nslots):
        row = jnp.where(lane == k, index[0, 0, k].astype(F32), row)
    rows += [row, jnp.zeros((INFO - len(rows) - 1, tile), F32)]
    info = jnp.concatenate(rows, axis=0).astype(BF16)
    me_b = lax.axis_index("blk")

    def piece(out, at, t):
        rows = pl.ds(pl.multiple_of((me_b ^ t) * part, part), part)
        for j in range(FIELDS):
            out[at + j * part : at + (j + 1) * part, :] = turned[j, rows, :]

    top = half * tile
    for out in (far_out, *near_outs):
        for k in range(half):
            out[k * tile : (k + 1) * tile, :] = share[k]
    for t in range(far):
        piece(far_out, top + t * FIELDS * part, far + t)
    for out, (t, _) in zip(near_outs, first_near):
        piece(out, top, t)
    piece(own_out, 0, 0)
    for out in (far_out, *near_outs, own_out):
        out[out.shape[0] - INFO :, :] = info


def relay_body(top, part, came, after, *outs):
    del after
    for t, out in enumerate(outs):
        out[0:top, :] = came[0:top, :]
        at = top + t * FIELDS * part
        out[top : top + FIELDS * part, :] = came[at : at + FIELDS * part, :]
        out[top + FIELDS * part :, :] = came[came.shape[0] - INFO :, :]


def place(n_blk, n_col, mat, slots, source, shift, slot, block, nslots):
    tile = block.shape[-1]
    blk, col = lax.axis_index("blk") ^ shift[0], lax.axis_index("col") ^ shift[1]
    position = slots[source, slot]
    row = pl.multiple_of((blk * n_col + position // n_blk) * tile, tile)
    column = pl.multiple_of(((position % n_blk) * n_col + col) * tile, tile)

    @pl.when(slot < slots[source, nslots])
    def _():
        mat[pl.ds(row, tile), pl.ds(column, tile)] = block[...]


def place_shares(n_blk, n_col, mat, slots, source, shift, own_part, other_part, nslots):
    half = nslots // 2
    tile = own_part.shape[1]
    core = lax.axis_index("rep")
    for part, which in ((own_part, core), (other_part, 1 - core)):
        for k in range(half):
            block = part.at[k * tile : (k + 1) * tile, :]
            place(n_blk, n_col, mat, slots, source, shift, which * half + k, block, nslots)


def take(n_col, fields, shift, ref, at):
    part, tile = fields.shape[1], ref.shape[1]
    blk, col = lax.axis_index("blk") ^ shift[0], lax.axis_index("col") ^ shift[1]
    lanes = pl.ds(pl.multiple_of((blk * n_col + col) * tile, tile), tile)
    for j in range(FIELDS):
        fields[j, :, lanes] = ref[at + j * part : at + (j + 1) * part, :]
    info = ref[ref.shape[0] - INFO :, :].astype(F32)
    sums = []
    for j in range(2):
        first, second, third = (info[PARTS * j + k : PARTS * j + k + 1] for k in range(PARTS))
        sums.append((first + second) + third)
    return sums


def base_body(n_blk, n_col, slots, blocks_in, own, mat, fields, sums_out, blocks, sem):
    copy = pltpu.make_async_copy(blocks_in, blocks, sem)
    copy.start()
    nslots = blocks.shape[2]
    mat[...] = jnp.zeros(mat.shape, BF16)
    fields[...] = jnp.zeros(fields.shape, BF16)
    sums = take(n_col, fields, (0, 0), own, 0)
    sums_out[...] = jnp.concatenate(sums + [jnp.zeros((6, own.shape[1]), F32)], axis=0)
    copy.wait()
    for k in range(nslots):
        place(n_blk, n_col, mat, slots, 0, (0, 0), k, blocks.at[0, 0, k], nslots)


def early_body(n_blk, n_col, shifts, nslots, slots, late_slots, mat, fields, sums_in, *refs):
    count = len(shifts)
    mine, theirs = refs[:count], refs[count : 2 * count]
    _, _, sums_out, slots_out = refs[2 * count :]
    for source in range(slots_out.shape[0]):
        for k in range(slots_out.shape[1]):
            slots_out[source, k] = late_slots[source, k]
    sums = [sums_in[0:1, :], sums_in[1:2, :]]
    for m, (shift, own_part, other_part) in enumerate(zip(shifts, mine, theirs)):
        place_shares(n_blk, n_col, mat, slots, m, shift, own_part, other_part, nslots)
        more = take(n_col, fields, shift, own_part, nslots // 2 * own_part.shape[1])
        sums = [a + b for a, b in zip(sums, more)]
    sums_out[...] = jnp.concatenate(sums + [jnp.zeros((6, sums_in.shape[1]), F32)], axis=0)


def main_body(n_blk, n_col, shifts, nslots, slots, bounded, mat, fields, sums_in, *refs):
    count = len(shifts)
    mine, theirs = refs[:count], refs[count : 2 * count]
    *outs, scales, _, _, products, turned = refs[2 * count :]
    part, tile = fields.shape[1], mine[0].shape[1]
    me_b, me_c = lax.axis_index("blk"), lax.axis_index("col")
    sums = [sums_in[0:1, :], sums_in[1:2, :]]
    for m, (shift, own_part, other_part) in enumerate(zip(shifts, mine, theirs)):
        place_shares(n_blk, n_col, mat, slots, m, shift, own_part, other_part, nslots)
        more = take(n_col, fields, shift, own_part, nslots // 2 * tile)
        sums = [a + b for a, b in zip(sums, more)]
    cost, rhs, upper, primal, dual = (fields[j].astype(F32) for j in range(FIELDS))
    weight = jnp.sqrt(sums[0] + EPS) / jnp.sqrt(sums[1] + EPS)
    rows = jnp.concatenate([ETA / weight, ETA * weight, bounded[...].astype(F32), jnp.zeros((5, tile), F32)], axis=0)
    scales[...] = rows
    turned[...] = jnp.concatenate([rows, jnp.zeros((tile - 8, tile), F32)], axis=0).T
    own = turned[pl.ds(pl.multiple_of(me_b * part, part), part), :]
    tau, sigma, limited = own[:, 0:1], own[:, 1:2], own[:, 2:3]

    for step in range(ITERS):
        kty = jnp.dot(dual.astype(BF16), mat[...], preferred_element_type=F32)
        products[2 * step] = kty.astype(BF16)
        x_new = project(primal, cost - kty, tau, upper, limited)
        xbar = (2.0 * x_new - primal).astype(BF16)
        primal = x_new
        kx = lax.dot_general(xbar, mat[...], (((1,), (1,)), ((), ())), preferred_element_type=F32)
        products[2 * step + 1] = kx.astype(BF16)
        dual = jnp.maximum(dual + sigma * (rhs - kx), 0.0)
    for t, out in enumerate(outs):
        lanes = pl.ds(pl.multiple_of(((me_b ^ t) * n_col + me_c) * tile, tile), tile)
        for j in range(2 * ITERS):
            out[j * part : (j + 1) * part, :] = products[j, :, lanes]


def final_body(order, *refs):
    parts = refs[: len(order)]
    scales, cost, rhs, upper, x_in, y_in, bounded, x_out, y_out, products = refs[len(order) :]
    part = parts[0].shape[0] // (2 * ITERS)
    me_b = lax.axis_index("blk")
    for t, recv in zip(order, parts):
        rows = pl.ds(pl.multiple_of((me_b ^ t) * part, part), part)
        for j in range(2 * ITERS):
            products[j, rows, :] = recv[j * part : (j + 1) * part, :]

    def turned(j):
        return products[j].astype(F32).T

    tau, sigma = scales[0:1, :], scales[1:2, :]
    primal, dual = x_in[...], y_in[...]
    for step in range(ITERS):
        primal = project(primal, cost[...] - turned(2 * step), tau, upper[...], bounded[...])
        dual = jnp.maximum(dual + sigma * (rhs[...] - turned(2 * step + 1)), 0.0)
    x_out[...] = primal
    y_out[...] = dual


def local_plan(blocks, block_index, live, cost, rhs, upper, x_init, y_init, bounded):
    n_blk, n_col = lax.axis_size("blk"), lax.axis_size("col")
    n = n_blk * n_col
    tile, nslots = blocks.shape[-1], blocks.shape[2]
    scn = cost.shape[1]
    part = scn // n_blk
    like = jax.ShapeDtypeStruct
    limits = bounded[None, :]

    def move(value, t, s):
        pairs = [(b * n_col + c, (b ^ t) * n_col + (c ^ s)) for b in range(n_blk) for c in range(n_col)]
        return lax.ppermute(value, ("blk", "col"), pairs)

    far = n_blk // 2
    near = [(t, s) for t in range(far) for s in range(n_col) if (t, s) != (0, 0)]
    half = nslots // 2
    top = half * tile
    size = top + FIELDS * part + INFO
    first_near = [(0, s) for s in range(1, n_col)] + [(t, 0) for t in range(1, far)]
    far_out, *near_outs, own = call(
        functools.partial(prep_body, far, first_near),
        [held((top + FIELDS * far * part + INFO, tile), BF16)]
        + [held((size, tile), BF16)] * len(first_near)
        + [held((size - top, tile), BF16)],
        [SMEM] + [ANY] * (FIELDS + 2),
        [live] + pinned([cost, rhs, upper, x_init, y_init, block_index, blocks]),
        scratch=[pltpu.VMEM((tile, scn), F32)] * FIELDS
        + [pltpu.VMEM((half, tile, tile), BF16)]
        + [pltpu.SMEM(block_index.shape, jnp.int32)]
        + [pltpu.VMEM((FIELDS, scn, tile), BF16), pltpu.SemaphoreType.DMA((FIELDS + 2,))],
    )

    def other_core(values):
        return [lax.ppermute(v[:top], "rep", [(0, 1), (1, 0)]) for v in values]

    def slots_of(values):
        rows = [v[v.shape[0] - INFO + SLOT_ROW, : nslots + 1] for v in values]
        return jnp.stack(rows).astype(jnp.int32)

    early = {(far, 0): move(far_out, far, 0)}
    for (t, s), out in zip(first_near, near_outs):
        early[t, s] = move(out, t, s)
    for t in range(1, far):
        for s in range(1, n_col):
            early[t, s] = move(early[t, 0], 0, s)
    mat, fields, sums = call(
        functools.partial(base_body, n_blk, n_col),
        [held((n * tile, n * tile), BF16), held((FIELDS, part, n * tile), BF16), held((8, scn), F32)],
        [SMEM, ANY, VMEM],
        [slots_of([own]), *pinned([blocks]), own],
        scratch=[pltpu.VMEM(blocks.shape, BF16), pltpu.SemaphoreType.DMA],
    )
    relayed = call(
        functools.partial(relay_body, top, part),
        [held((size, tile), BF16)] * far,
        [VMEM, VMEM],
        [early[far, 0], sums],
    )
    late = {(far + t, s): move(relayed[t], t, s) for t, s in sorted(near, key=sum, reverse=True)}
    shifts, mine = list(early), list(early.values())
    late_slots = slots_of(list(late.values()))
    mat, fields, sums, late_slots = call(
        functools.partial(early_body, n_blk, n_col, shifts, nslots),
        [held(mat.shape, BF16), held(fields.shape, BF16), held((8, scn), F32)]
        + [pltpu.SMEM(late_slots.shape, jnp.int32)],
        [SMEM, SMEM] + [VMEM] * (3 + 2 * len(mine)),
        [slots_of(mine), late_slots, mat, fields, sums] + mine + other_core(mine),
        specs=[VMEM] * 3 + [SMEM],
        aliases={2: 0, 3: 1},
    )
    shifts, mine = list(late), list(late.values())
    *products, scales, _, _ = call(
        functools.partial(main_body, n_blk, n_col, shifts, nslots),
        [held((2 * ITERS * part, tile), BF16)] * n_blk
        + [like((8, scn), F32), held(mat.shape, BF16), held(fields.shape, BF16)],
        [SMEM] + [VMEM] * (4 + 2 * len(mine)),
        [late_slots, limits, mat, fields, sums] + mine + other_core(mine),
        scratch=[pltpu.VMEM((2 * ITERS, part, n * tile), BF16), pltpu.VMEM((tile, scn), F32)],
        flops=4 * ITERS * n * n * tile * tile * part,
        aliases={2: n_blk + 1, 3: n_blk + 2},
    )
    order = [0, *range(n_blk - 1, 0, -1)]
    parts = [products[t] if t == 0 else move(products[t], t, 0) for t in order]
    return call(
        functools.partial(final_body, order),
        [like((tile, scn), F32)] * 2,
        [VMEM] * (n_blk + FIELDS + 2),
        parts + [scales, cost, rhs, upper, x_init, y_init, limits],
        scratch=[pltpu.VMEM((2 * ITERS, scn, tile), BF16)],
    )


def project_box(value, upper, bounded):
    capped = jnp.where(bounded[None, :] > 0, jnp.minimum(value, upper), value)
    return jnp.maximum(capped, 0.0)


def collectives_plan(blocks, block_index, live, cost, rhs, upper, x_init, y_init, bounded):
    block_mats = blocks[0, 0]
    slots = block_index[0, 0]
    n_blk = lax.axis_size("blk")
    n_col = lax.axis_size("col")
    tile_size = block_mats.shape[1]
    scn_count = cost.shape[1]
    row_block = slots // n_blk
    col_block = slots % n_blk
    keep_mask = (jnp.arange(slots.shape[0]) < live[0, 0]).astype(jnp.float32)[:, None, None]
    totals = lax.psum((jnp.sum(cost * cost, axis=0), jnp.sum(rhs * rhs, axis=0)), ("blk", "col"))
    weight = jnp.sqrt(totals[0] + EPS) / jnp.sqrt(totals[1] + EPS)
    tau = (ETA / weight)[None, :]
    sigma = (ETA * weight)[None, :]
    primal = x_init
    dual = y_init
    for step in range(ITERS):
        gathered = lax.all_gather(dual.astype(jnp.bfloat16), "col", axis=0, tiled=True)
        pieces = gathered.reshape(n_col, tile_size, scn_count)[row_block]
        products = (
            jnp.einsum("bkt,bks->bts", block_mats, pieces, preferred_element_type=jnp.float32)
            * keep_mask
        )
        cols = jnp.zeros((n_blk, tile_size, scn_count), jnp.float32).at[col_block].add(products)
        kty = lax.psum_scatter(
            cols.reshape(n_blk * tile_size, scn_count).astype(jnp.bfloat16),
            "blk",
            scatter_dimension=0,
            tiled=True,
        ).astype(jnp.float32)
        x_new = project_box(primal - tau * (cost - kty), upper, bounded)
        xbar = (2.0 * x_new - primal).astype(jnp.bfloat16)
        whole = lax.all_gather(xbar, "blk", axis=0, tiled=True)
        primal = x_new
        row_pieces = whole.reshape(n_blk, tile_size, scn_count)[col_block]
        row_products = (
            jnp.einsum("bkt,bts->bks", block_mats, row_pieces, preferred_element_type=jnp.float32)
            * keep_mask
        )
        rows = jnp.zeros((n_col, tile_size, scn_count), jnp.float32).at[row_block].add(row_products)
        terms = rows.reshape(n_col * tile_size, scn_count)
        kx = lax.psum_scatter(
            terms.astype(jnp.bfloat16), "col", scatter_dimension=0, tiled=True
        ).astype(jnp.float32)
        dual = jnp.maximum(dual + sigma * (rhs - kx), 0.0)
    return (primal, dual)


def shards(*args):
    n_blk, n_col, n_rep = (lax.axis_size(axis) for axis in ("blk", "col", "rep"))
    blocks, cost = args[0], args[3]
    n, tile, nslots = n_blk * n_col, blocks.shape[-1], blocks.shape[2]
    fits = 2 * (n * tile) ** 2 <= MAX_MATRIX and cost.shape[1] % (16 * n_blk) == 0 and cost.shape[1] == tile
    even = n_blk & (n_blk - 1) == 0 and n_col & (n_col - 1) == 0 and n_blk > 1 and n_rep == 2 and nslots % 2 == 0
    x, y = (local_plan if fits and even else collectives_plan)(*args)
    return x, y


def solution(mesh):
    in_specs = (
        P("blk", "col", None, None, None),
        P("blk", "col", None),
        P("blk", "col"),
        P(("blk", "col"), ("groups", "rep")),
        P(("blk", "col"), ("groups", "rep")),
        P(("blk", "col"), ("groups", "rep")),
        P(("blk", "col"), ("groups", "rep")),
        P(("blk", "col"), ("groups", "rep")),
        P(("groups", "rep")),
    )
    out_specs = (P(("blk", "col"), ("groups", "rep")), P(("blk", "col"), ("groups", "rep")))
    return jax.shard_map(shards, mesh=mesh, in_specs=in_specs, out_specs=out_specs, check_vma=False)
```

```python
import functools
import math

import jax
import jax.numpy as jnp
from jax import lax
from jax.experimental import pallas as pl
from jax.experimental.pallas import tpu as pltpu
from jax.sharding import PartitionSpec as P

ITERS = 2


ETA = 0.4
EPS = 1e-06
MAX_MATRIX = 8 * 1024 * 1024
PARTS = 3
FIELDS = 5
SLOT_ROW = 2 * PARTS
INFO = 16

MIB = 1024 * 1024
VMEM = pl.BlockSpec(memory_space=pltpu.VMEM)
SMEM = pl.BlockSpec(memory_space=pltpu.SMEM)
ANY = pl.BlockSpec(memory_space=pl.ANY)
F32 = jnp.float32
BF16 = jnp.bfloat16


def held(shape, dtype):
    return pltpu.VMEM(shape, dtype)


def pinned(values):
    return [pltpu.with_memory_space_constraint(v, pltpu.HBM) for v in values]


def call(body, outs, in_specs, args, scratch=(), flops=0, limit=32, aliases=None, specs=None):
    nbytes = sum(math.prod(a.shape) * jnp.dtype(a.dtype).itemsize for a in list(args) + list(outs))
    return pl.pallas_call(
        body,
        out_shape=list(outs),
        in_specs=in_specs,
        out_specs=specs or [VMEM] * len(outs),
        scratch_shapes=list(scratch),
        input_output_aliases=aliases or {},
        compiler_params=pltpu.CompilerParams(vmem_limit_bytes=limit * MIB),
        cost_estimate=pl.CostEstimate(flops=flops, bytes_accessed=nbytes, transcendentals=0),
    )(*args)


def split_parts(values):
    high = values.astype(BF16).astype(F32)
    rest = values - high
    middle = rest.astype(BF16).astype(F32)
    low = (rest - middle).astype(BF16).astype(F32)
    return [high, middle, low]


def project(primal, grad, tau, upper, limited):
    value = primal - tau * grad
    capped = jnp.where(limited > 0, jnp.minimum(value, upper), value)
    return jnp.maximum(capped, 0.0)


def prep_body(far, first_near, *refs):
    live, *sources = refs[: FIELDS + 3]
    far_out, *near_outs, own_out = refs[FIELDS + 3 : FIELDS + 5 + len(first_near)]
    *fields, share, index, turned, sems = refs[FIELDS + 5 + len(first_near) :]
    half, tile = share.shape[0], share.shape[1]
    first = lax.axis_index("rep") * half
    targets = (*fields, index)
    copies = [
        pltpu.make_async_copy(source, target, sems.at[k])
        for k, (source, target) in enumerate(zip(sources[:-1], targets))
    ]
    copies.append(pltpu.make_async_copy(sources[-1].at[0, 0, pl.ds(first, half)], share, sems.at[FIELDS + 1]))
    for copy in copies:
        copy.start()
    part = (own_out.shape[0] - INFO) // FIELDS
    nslots = index.shape[-1]
    rows = []
    for j, field in enumerate(fields):
        copies[j].wait()
        values = field[...]
        if j < 2:
            rows += split_parts(jnp.sum(values * values, axis=0, keepdims=True))
        turned[j] = values.astype(BF16).T
    for copy in copies[FIELDS:]:
        copy.wait()
    lane = lax.broadcasted_iota(jnp.int32, (1, tile), 1)
    row = jnp.where(lane == nslots, live[0, 0].astype(F32), 0.0)
    for k in range(nslots):
        row = jnp.where(lane == k, index[0, 0, k].astype(F32), row)
    rows += [row, jnp.zeros((INFO - len(rows) - 1, tile), F32)]
    info = jnp.concatenate(rows, axis=0).astype(BF16)
    me_b = lax.axis_index("blk")

    def piece(out, at, t):
        rows = pl.ds(pl.multiple_of((me_b ^ t) * part, part), part)
        for j in range(FIELDS):
            out[at + j * part : at + (j + 1) * part, :] = turned[j, rows, :]

    top = half * tile
    for out in (far_out, *near_outs):
        for k in range(half):
            out[k * tile : (k + 1) * tile, :] = share[k]
    for t in range(far):
        piece(far_out, top + t * FIELDS * part, far + t)
    for out, (t, _) in zip(near_outs, first_near):
        piece(out, top, t)
    piece(own_out, 0, 0)
    for out in (far_out, *near_outs, own_out):
        out[out.shape[0] - INFO :, :] = info


def relay_body(top, part, came, after, *outs):
    del after
    for t, out in enumerate(outs):
        out[0:top, :] = came[0:top, :]
        at = top + t * FIELDS * part
        out[top : top + FIELDS * part, :] = came[at : at + FIELDS * part, :]
        out[top + FIELDS * part :, :] = came[came.shape[0] - INFO :, :]


def place(n_blk, n_col, mat, slots, source, shift, slot, block, nslots):
    tile = block.shape[-1]
    blk, col = lax.axis_index("blk") ^ shift[0], lax.axis_index("col") ^ shift[1]
    position = slots[source, slot]
    row = pl.multiple_of((blk * n_col + position // n_blk) * tile, tile)
    column = pl.multiple_of(((position % n_blk) * n_col + col) * tile, tile)

    @pl.when(slot < slots[source, nslots])
    def _():
        mat[pl.ds(row, tile), pl.ds(column, tile)] = block[...]


def place_shares(n_blk, n_col, mat, slots, source, shift, own_part, other_part, nslots):
    half = nslots // 2
    tile = own_part.shape[1]
    core = lax.axis_index("rep")
    for part, which in ((own_part, core), (other_part, 1 - core)):
        for k in range(half):
            block = part.at[k * tile : (k + 1) * tile, :]
            place(n_blk, n_col, mat, slots, source, shift, which * half + k, block, nslots)


def take(n_col, fields, shift, ref, at):
    part, tile = fields.shape[1], ref.shape[1]
    blk, col = lax.axis_index("blk") ^ shift[0], lax.axis_index("col") ^ shift[1]
    lanes = pl.ds(pl.multiple_of((blk * n_col + col) * tile, tile), tile)
    for j in range(FIELDS):
        fields[j, :, lanes] = ref[at + j * part : at + (j + 1) * part, :]
    info = ref[ref.shape[0] - INFO :, :].astype(F32)
    sums = []
    for j in range(2):
        first, second, third = (info[PARTS * j + k : PARTS * j + k + 1] for k in range(PARTS))
        sums.append((first + second) + third)
    return sums


def base_body(n_blk, n_col, slots, blocks_in, own, mat, fields, sums_out, blocks, sem):
    copy = pltpu.make_async_copy(blocks_in, blocks, sem)
    copy.start()
    nslots = blocks.shape[2]
    mat[...] = jnp.zeros(mat.shape, BF16)
    fields[...] = jnp.zeros(fields.shape, BF16)
    sums = take(n_col, fields, (0, 0), own, 0)
    sums_out[...] = jnp.concatenate(sums + [jnp.zeros((6, own.shape[1]), F32)], axis=0)
    copy.wait()
    for k in range(nslots):
        place(n_blk, n_col, mat, slots, 0, (0, 0), k, blocks.at[0, 0, k], nslots)


def early_body(n_blk, n_col, shifts, nslots, slots, late_slots, mat, fields, sums_in, *refs):
    count = len(shifts)
    mine, theirs = refs[:count], refs[count : 2 * count]
    _, _, sums_out, slots_out = refs[2 * count :]
    for source in range(slots_out.shape[0]):
        for k in range(slots_out.shape[1]):
            slots_out[source, k] = late_slots[source, k]
    sums = [sums_in[0:1, :], sums_in[1:2, :]]
    for m, (shift, own_part, other_part) in enumerate(zip(shifts, mine, theirs)):
        place_shares(n_blk, n_col, mat, slots, m, shift, own_part, other_part, nslots)
        more = take(n_col, fields, shift, own_part, nslots // 2 * own_part.shape[1])
        sums = [a + b for a, b in zip(sums, more)]
    sums_out[...] = jnp.concatenate(sums + [jnp.zeros((6, sums_in.shape[1]), F32)], axis=0)


def main_body(n_blk, n_col, shifts, nslots, slots, bounded, mat, fields, sums_in, *refs):
    count = len(shifts)
    mine, theirs = refs[:count], refs[count : 2 * count]
    *outs, scales, _, _, products, turned = refs[2 * count :]
    part, tile = fields.shape[1], mine[0].shape[1]
    me_b, me_c = lax.axis_index("blk"), lax.axis_index("col")
    sums = [sums_in[0:1, :], sums_in[1:2, :]]
    for m, (shift, own_part, other_part) in enumerate(zip(shifts, mine, theirs)):
        place_shares(n_blk, n_col, mat, slots, m, shift, own_part, other_part, nslots)
        more = take(n_col, fields, shift, own_part, nslots // 2 * tile)
        sums = [a + b for a, b in zip(sums, more)]
    cost, rhs, upper, primal, dual = (fields[j].astype(F32) for j in range(FIELDS))
    weight = jnp.sqrt(sums[0] + EPS) / jnp.sqrt(sums[1] + EPS)
    rows = jnp.concatenate([ETA / weight, ETA * weight, bounded[...].astype(F32), jnp.zeros((5, tile), F32)], axis=0)
    scales[...] = rows
    turned[...] = jnp.concatenate([rows, jnp.zeros((tile - 8, tile), F32)], axis=0).T
    own = turned[pl.ds(pl.multiple_of(me_b * part, part), part), :]
    tau, sigma, limited = own[:, 0:1], own[:, 1:2], own[:, 2:3]

    for step in range(ITERS):
        kty = jnp.dot(dual.astype(BF16), mat[...], preferred_element_type=F32)
        products[2 * step] = kty.astype(BF16)
        x_new = project(primal, cost - kty, tau, upper, limited)
        xbar = (2.0 * x_new - primal).astype(BF16)
        primal = x_new
        kx = lax.dot_general(xbar, mat[...], (((1,), (1,)), ((), ())), preferred_element_type=F32)
        products[2 * step + 1] = kx.astype(BF16)
        dual = jnp.maximum(dual + sigma * (rhs - kx), 0.0)
    for t, out in enumerate(outs):
        lanes = pl.ds(pl.multiple_of(((me_b ^ t) * n_col + me_c) * tile, tile), tile)
        for j in range(2 * ITERS):
            out[j * part : (j + 1) * part, :] = products[j, :, lanes]


def final_body(order, *refs):
    parts = refs[: len(order)]
    scales, cost, rhs, upper, x_in, y_in, bounded, x_out, y_out, products = refs[len(order) :]
    part = parts[0].shape[0] // (2 * ITERS)
    me_b = lax.axis_index("blk")
    for t, recv in zip(order, parts):
        rows = pl.ds(pl.multiple_of((me_b ^ t) * part, part), part)
        for j in range(2 * ITERS):
            products[j, rows, :] = recv[j * part : (j + 1) * part, :]

    def turned(j):
        return products[j].T.astype(F32)

    tau, sigma = scales[0:1, :], scales[1:2, :]
    primal, dual = x_in[...], y_in[...]
    for step in range(ITERS):
        primal = project(primal, cost[...] - turned(2 * step), tau, upper[...], bounded[...])
        dual = jnp.maximum(dual + sigma * (rhs[...] - turned(2 * step + 1)), 0.0)
    x_out[...] = primal
    y_out[...] = dual


def local_plan(blocks, block_index, live, cost, rhs, upper, x_init, y_init, bounded):
    n_blk, n_col = lax.axis_size("blk"), lax.axis_size("col")
    n = n_blk * n_col
    tile, nslots = blocks.shape[-1], blocks.shape[2]
    scn = cost.shape[1]
    part = scn // n_blk
    like = jax.ShapeDtypeStruct
    limits = bounded[None, :]

    def move(value, t, s):
        pairs = [(b * n_col + c, (b ^ t) * n_col + (c ^ s)) for b in range(n_blk) for c in range(n_col)]
        return lax.ppermute(value, ("blk", "col"), pairs)

    far = n_blk // 2
    near = [(t, s) for t in range(far) for s in range(n_col) if (t, s) != (0, 0)]
    half = nslots // 2
    top = half * tile
    size = top + FIELDS * part + INFO
    first_near = [(0, s) for s in range(1, n_col)] + [(t, 0) for t in range(1, far)]
    far_out, *near_outs, own = call(
        functools.partial(prep_body, far, first_near),
        [held((top + FIELDS * far * part + INFO, tile), BF16)]
        + [held((size, tile), BF16)] * len(first_near)
        + [held((size - top, tile), BF16)],
        [SMEM] + [ANY] * (FIELDS + 2),
        [live] + pinned([cost, rhs, upper, x_init, y_init, block_index, blocks]),
        scratch=[pltpu.VMEM((tile, scn), F32)] * FIELDS
        + [pltpu.VMEM((half, tile, tile), BF16)]
        + [pltpu.SMEM(block_index.shape, jnp.int32)]
        + [pltpu.VMEM((FIELDS, scn, tile), BF16), pltpu.SemaphoreType.DMA((FIELDS + 2,))],
    )

    def other_core(values):
        return [lax.ppermute(v[:top], "rep", [(0, 1), (1, 0)]) for v in values]

    def slots_of(values):
        rows = [v[v.shape[0] - INFO + SLOT_ROW, : nslots + 1] for v in values]
        return jnp.stack(rows).astype(jnp.int32)

    early = {(far, 0): move(far_out, far, 0)}
    for (t, s), out in zip(first_near, near_outs):
        early[t, s] = move(out, t, s)
    for t in range(1, far):
        for s in range(1, n_col):
            early[t, s] = move(early[t, 0], 0, s)
    mat, fields, sums = call(
        functools.partial(base_body, n_blk, n_col),
        [held((n * tile, n * tile), BF16), held((FIELDS, part, n * tile), BF16), held((8, scn), F32)],
        [SMEM, ANY, VMEM],
        [slots_of([own]), *pinned([blocks]), own],
        scratch=[pltpu.VMEM(blocks.shape, BF16), pltpu.SemaphoreType.DMA],
    )
    relayed = call(
        functools.partial(relay_body, top, part),
        [held((size, tile), BF16)] * far,
        [VMEM, VMEM],
        [early[far, 0], sums],
    )
    late = {(far + t, s): move(relayed[t], t, s) for t, s in sorted(near, key=sum, reverse=True)}
    shifts, mine = list(early), list(early.values())
    late_slots = slots_of(list(late.values()))
    mat, fields, sums, late_slots = call(
        functools.partial(early_body, n_blk, n_col, shifts, nslots),
        [held(mat.shape, BF16), held(fields.shape, BF16), held((8, scn), F32)]
        + [pltpu.SMEM(late_slots.shape, jnp.int32)],
        [SMEM, SMEM] + [VMEM] * (3 + 2 * len(mine)),
        [slots_of(mine), late_slots, mat, fields, sums] + mine + other_core(mine),
        specs=[VMEM] * 3 + [SMEM],
        aliases={2: 0, 3: 1},
    )
    shifts, mine = list(late), list(late.values())
    *products, scales, _, _ = call(
        functools.partial(main_body, n_blk, n_col, shifts, nslots),
        [held((2 * ITERS * part, tile), BF16)] * n_blk
        + [like((8, scn), F32), held(mat.shape, BF16), held(fields.shape, BF16)],
        [SMEM] + [VMEM] * (4 + 2 * len(mine)),
        [late_slots, limits, mat, fields, sums] + mine + other_core(mine),
        scratch=[pltpu.VMEM((2 * ITERS, part, n * tile), BF16), pltpu.VMEM((tile, scn), F32)],
        flops=4 * ITERS * n * n * tile * tile * part,
        aliases={2: n_blk + 1, 3: n_blk + 2},
    )
    order = [0, *range(n_blk - 1, 0, -1)]
    parts = [products[t] if t == 0 else move(products[t], t, 0) for t in order]
    return call(
        functools.partial(final_body, order),
        [like((tile, scn), F32)] * 2,
        [VMEM] * (n_blk + FIELDS + 2),
        parts + [scales, cost, rhs, upper, x_init, y_init, limits],
        scratch=[pltpu.VMEM((2 * ITERS, scn, tile), BF16)],
    )


def project_box(value, upper, bounded):
    capped = jnp.where(bounded[None, :] > 0, jnp.minimum(value, upper), value)
    return jnp.maximum(capped, 0.0)


def collectives_plan(blocks, block_index, live, cost, rhs, upper, x_init, y_init, bounded):
    block_mats = blocks[0, 0]
    slots = block_index[0, 0]
    n_blk = lax.axis_size("blk")
    n_col = lax.axis_size("col")
    tile_size = block_mats.shape[1]
    scn_count = cost.shape[1]
    row_block = slots // n_blk
    col_block = slots % n_blk
    keep_mask = (jnp.arange(slots.shape[0]) < live[0, 0]).astype(jnp.float32)[:, None, None]
    totals = lax.psum((jnp.sum(cost * cost, axis=0), jnp.sum(rhs * rhs, axis=0)), ("blk", "col"))
    weight = jnp.sqrt(totals[0] + EPS) / jnp.sqrt(totals[1] + EPS)
    tau = (ETA / weight)[None, :]
    sigma = (ETA * weight)[None, :]
    primal = x_init
    dual = y_init
    for step in range(ITERS):
        gathered = lax.all_gather(dual.astype(jnp.bfloat16), "col", axis=0, tiled=True)
        pieces = gathered.reshape(n_col, tile_size, scn_count)[row_block]
        products = (
            jnp.einsum("bkt,bks->bts", block_mats, pieces, preferred_element_type=jnp.float32)
            * keep_mask
        )
        cols = jnp.zeros((n_blk, tile_size, scn_count), jnp.float32).at[col_block].add(products)
        kty = lax.psum_scatter(
            cols.reshape(n_blk * tile_size, scn_count).astype(jnp.bfloat16),
            "blk",
            scatter_dimension=0,
            tiled=True,
        ).astype(jnp.float32)
        x_new = project_box(primal - tau * (cost - kty), upper, bounded)
        xbar = (2.0 * x_new - primal).astype(jnp.bfloat16)
        whole = lax.all_gather(xbar, "blk", axis=0, tiled=True)
        primal = x_new
        row_pieces = whole.reshape(n_blk, tile_size, scn_count)[col_block]
        row_products = (
            jnp.einsum("bkt,bts->bks", block_mats, row_pieces, preferred_element_type=jnp.float32)
            * keep_mask
        )
        rows = jnp.zeros((n_col, tile_size, scn_count), jnp.float32).at[row_block].add(row_products)
        terms = rows.reshape(n_col * tile_size, scn_count)
        kx = lax.psum_scatter(
            terms.astype(jnp.bfloat16), "col", scatter_dimension=0, tiled=True
        ).astype(jnp.float32)
        dual = jnp.maximum(dual + sigma * (rhs - kx), 0.0)
    return (primal, dual)


def shards(*args):
    n_blk, n_col, n_rep = (lax.axis_size(axis) for axis in ("blk", "col", "rep"))
    blocks, cost = args[0], args[3]
    n, tile, nslots = n_blk * n_col, blocks.shape[-1], blocks.shape[2]
    fits = 2 * (n * tile) ** 2 <= MAX_MATRIX and cost.shape[1] % (16 * n_blk) == 0 and cost.shape[1] == tile
    even = n_blk & (n_blk - 1) == 0 and n_col & (n_col - 1) == 0 and n_blk > 1 and n_rep == 2 and nslots % 2 == 0
    x, y = (local_plan if fits and even else collectives_plan)(*args)
    return x, y


def solution(mesh):
    in_specs = (
        P("blk", "col", None, None, None),
        P("blk", "col", None),
        P("blk", "col"),
        P(("blk", "col"), ("groups", "rep")),
        P(("blk", "col"), ("groups", "rep")),
        P(("blk", "col"), ("groups", "rep")),
        P(("blk", "col"), ("groups", "rep")),
        P(("blk", "col"), ("groups", "rep")),
        P(("groups", "rep")),
    )
    out_specs = (P(("blk", "col"), ("groups", "rep")), P(("blk", "col"), ("groups", "rep")))
    return jax.shard_map(shards, mesh=mesh, in_specs=in_specs, out_specs=out_specs, check_vma=False)
```
